32 devices in a mesh: groups: 2 (over x), gx: 16 (over z, y, core).
Axes of the slice: x: 2, y: 2, z: 4, core: 2. Of those that a mesh axis runs over, the one named last changes fastest.
Arguments:
- adjoint_state: float32 [8, 96, 128, 128], P(None, 'groups', 'gx'), parts along dimension 1, may hold values from -6 to 6
- forward_fields: bfloat16 [2, 3, 96, 128, 128], P(None, None, 'groups', 'gx'), parts along dimension 2, may hold values from -6 to 6
- vel_coeffs: float32 [8, 128], P('groups'), parts along dimension 0, may hold values from 0.2 to 0.8
- stress_coeffs: float32 [8, 128], P('groups'), parts along dimension 0, may hold values from 0.15 to 0.6
- drm_cells: int32 [4096], P('gx'), may hold values from 120 to 16383, as said below
- drm_force: float32 [32, 2, 2, 4096], P('groups', None, None, 'gx'), parts along dimension 0, may hold values from -6 to 6
- source_id: int32 [96], P('groups'), parts along dimension 0, may hold values from 0 to 15
Outputs:
- adjoint_out: float32 [8, 96, 128, 128], P(None, 'groups', 'gx'), parts along dimension 1
- gradients: float32 [4, 128], P('groups'), parts along dimension 0
The draws below stay inside these ranges and needn't reach their ends.
There are 2 independent parts, one for each index of `groups`. The reference program is written for one: setup_inputs(seed, part) draws one part's arguments, and reference() takes and returns one part's arrays. A program takes and returns all parts, laid end to end along the dimension named above; an argument that names none is the same for every part. Nothing has to cross between parts.
Inputs may be any that keep to these rules, and one draw needn't show every extreme that they name: `drm_cells`: in each aligned block b of 256 entries, every entry names a cell x * 128 + z with b * 8 <= x < (b + 1) * 8 and 120 <= z < 128; cells may repeat.
All inputs are finite; a program needn't handle non-finite values.
Results may differ from the reference program's by a relative error of at most 0.0003.
Values sent between devices are 32-bit elements; how exact they have to be, the bound alone decides.
No kernel may reach another device: no remote copies, remote signals or barrier semaphores. Data moves between devices by JAX's collectives and lax.ppermute only.
A program may use at most 64 MiB of HBM per device.

```python
import math
import jax
import jax.numpy as jnp

CX = 8
NZ = 128
EVENTS = 48
NSRC = 16
STEPS = 2
LAYER = 8
DRM_DEV = 256
NX = 128
NDRM = 4096


def draw_drm_cells(key, part):
    block_count = NDRM // DRM_DEV
    key_lateral, key_depth = jax.random.split(key)
    lateral = jax.random.randint(key_lateral, (block_count, DRM_DEV), 0, CX)
    depth_index = jax.random.randint(key_depth, (block_count, DRM_DEV), NZ - LAYER, NZ)
    lateral = lateral.at[:, 0].set(0).at[:, DRM_DEV - 1].set(CX - 1)
    depth_index = depth_index.at[:, 0].set(NZ - LAYER).at[:, DRM_DEV - 1].set(NZ - 1)
    offsets = (jnp.arange(block_count, dtype=jnp.int32) * CX)[:, None]
    return ((lateral + offsets) * NZ + depth_index).reshape(-1).astype(jnp.int32)


def plant(entries, rng, least, high):
    longest = entries.shape.index(max(entries.shape))
    spots = []
    for shift in (0, 1):
        where = [jax.random.randint(jax.random.fold_in(rng, axis), (), 0, length) for axis, length in enumerate(entries.shape)]
        where[longest] = (where[longest] + shift) % entries.shape[longest]
        spots.append(tuple(where))
    return entries.at[spots[0]].set(least).at[spots[1]].set(high)


def block_scale(stream_key, extent, shards, least, high):
    gain, own = 1.0, jax.random.fold_in(stream_key, 6)
    for axis_at, shards_of in shards:
        steps = jnp.exp(jax.random.uniform(jax.random.fold_in(own, axis_at), (shards_of,), jnp.float32, least / len(shards), high / len(shards)))
        gain = gain * jnp.repeat(steps, extent[axis_at] // shards_of).reshape([-1 if axis == axis_at else 1 for axis in range(len(extent))])
    return gain


def noise(own_key, shape, width, bound, pieces=(), held_as=jnp.bfloat16):
    factor_of = block_scale(own_key, shape, pieces, -0.22, 0.18) if pieces else 1.0
    result = jax.random.normal(own_key, shape, jnp.float32) * width * factor_of
    return jnp.minimum(jnp.maximum(result, -bound), bound).astype(held_as)


def setup_inputs(seed: int = 0, part: int = 0) -> dict:
    streams_of = jax.random.split(jax.random.key(seed), 8)
    part_splits = jax.random.split(jax.random.fold_in(streams_of[7], part), 8)
    return {
        "adjoint_state": noise(part_splits[0], (8, EVENTS, NX, NZ), 1.0, 6.0, ((2, 16),), jnp.float32),
        "forward_fields": noise(part_splits[1], (STEPS, 3, EVENTS, NX, NZ), 1.0, 6.0, ((3, 16),)),
        "vel_coeffs": jnp.clip(jnp.exp(jax.random.uniform(part_splits[2], (4, NZ), jnp.float32, math.log(0.2), math.log(0.8))), 0.2, 0.8),
        "stress_coeffs": jnp.clip(jnp.exp(jax.random.uniform(part_splits[3], (4, NZ), jnp.float32, math.log(0.15), math.log(0.6))), 0.15, 0.6),
        "drm_cells": draw_drm_cells(jax.random.fold_in(streams_of[7], 71), part),
        "drm_force": noise(part_splits[5], (NSRC, STEPS, 2, NDRM), 1.0, 6.0, ((3, 16),), jnp.float32),
        "source_id": plant(jax.random.randint(part_splits[6], (EVENTS,), 0, NSRC), jax.random.fold_in(part_splits[6], 1), 0, NSRC - 1).astype(jnp.int32),
    }


def lower_diff(values, before):
    return values - jnp.concatenate([before, values[:, :-1]], axis=1)


def upper_diff(values, beyond):
    return jnp.concatenate([values[:, 1:], beyond], axis=1) - values


def depth_lower(values):
    return values - jnp.concatenate([jnp.zeros_like(values[:, :, :1]), values[:, :, :-1]], axis=2)


def depth_upper(values):
    return jnp.concatenate([values[:, :, 1:], jnp.zeros_like(values[:, :, :1])], axis=2) - values


def velocity_update(fields, before, forcing, vel_coeffs):
    vel_x, vel_z, flow_x, flow_z, stress_xx, stress_zz, stress_xz, pressure = fields
    mass_solid, mass_couple, mass_fluid, drag_rate = vel_coeffs[0], vel_coeffs[1], vel_coeffs[2], vel_coeffs[3]
    force_x = lower_diff(stress_xx, before[0]) + depth_lower(stress_xz)
    force_z = lower_diff(stress_xz, before[1]) + depth_lower(stress_zz)
    push_x = lower_diff(pressure, before[2]) + drag_rate * flow_x
    push_z = depth_lower(pressure) + drag_rate * flow_z
    vel_x = vel_x + mass_solid * force_x + mass_couple * push_x + forcing[0]
    vel_z = vel_z + mass_solid * force_z + mass_couple * push_z + forcing[1]
    flow_x = flow_x - mass_couple * force_x - mass_fluid * push_x
    flow_z = flow_z - mass_couple * force_z - mass_fluid * push_z
    return [vel_x, vel_z, flow_x, flow_z, stress_xx, stress_zz, stress_xz, pressure]


def stress_update(fields, beyond, stress_coeffs):
    vel_x, vel_z, flow_x, flow_z, stress_xx, stress_zz, stress_xz, pressure = fields
    lame_total, shear_modulus, coupling, fluid_modulus = stress_coeffs[0], stress_coeffs[1], stress_coeffs[2], stress_coeffs[3]
    strain_x = upper_diff(vel_x, beyond[0])
    strain_z = depth_upper(vel_z)
    dilation = strain_x + strain_z
    inflow = upper_diff(flow_x, beyond[2]) + depth_upper(flow_z)
    stress_xx = stress_xx + lame_total * dilation + 2.0 * shear_modulus * strain_x - coupling * inflow
    stress_zz = stress_zz + lame_total * dilation + 2.0 * shear_modulus * strain_z - coupling * inflow
    stress_xz = stress_xz + shear_modulus * (depth_upper(vel_x) + upper_diff(vel_z, beyond[1]))
    pressure = pressure - coupling * dilation - fluid_modulus * inflow
    return [vel_x, vel_z, flow_x, flow_z, stress_xx, stress_zz, stress_xz, pressure]


def reference(adjoint_state, forward_fields, vel_coeffs, stress_coeffs, drm_cells, drm_force, source_id):
    fields = [adjoint_state[field_index] for field_index in range(8)]
    zero_rim = jnp.zeros((EVENTS, 1, NZ), jnp.float32)
    rims = [zero_rim, zero_rim, zero_rim]
    selected = drm_force[source_id]
    perm_total = jnp.zeros((NZ,), jnp.float32)
    poro_total = jnp.zeros((NZ,), jnp.float32)
    for step_index in range(STEPS):
        drm_term = jnp.transpose(selected[:, step_index], (1, 0, 2))
        forcing_plane = jnp.zeros((2, EVENTS, NX * NZ), jnp.float32).at[:, :, drm_cells].add(drm_term)
        forcing_plane = forcing_plane.reshape(2, EVENTS, NX, NZ)
        fields = velocity_update(fields, rims, forcing_plane, vel_coeffs)
        flow_prod = fields[2] * forward_fields[step_index, 0].astype(jnp.float32) + fields[3] * forward_fields[step_index, 1].astype(jnp.float32)
        perm_total = perm_total + jnp.sum(flow_prod, axis=(0, 1))
        fields = stress_update(fields, rims, stress_coeffs)
        poro_total = poro_total + jnp.sum(fields[7] * forward_fields[step_index, 2].astype(jnp.float32), axis=(0, 1))
    normalizer = (EVENTS * NX) ** -0.5
    gradients = jnp.stack([vel_coeffs[2] * vel_coeffs[3] * perm_total, stress_coeffs[3] * poro_total]) * normalizer
    return jnp.stack(fields), gradients
```

```python
import functools

import jax
import jax.numpy as jnp
from jax import lax
from jax.experimental import pallas as pl
from jax.experimental.pallas import tpu as pltpu
from jax.sharding import PartitionSpec as P

LAYER = 8
FIELDS = 8
VX, VZ, QX, QZ, SXX, SZZ, SXZ, PR = range(FIELDS)
HALO = 6
EXACT = lax.Precision.HIGHEST


def depth_lower(values):
    lane = lax.broadcasted_iota(jnp.int32, values.shape, 1)
    return values - jnp.where(lane == 0, 0.0, pltpu.roll(values, 1, 1))


def depth_upper(values):
    depth = values.shape[1]
    lane = lax.broadcasted_iota(jnp.int32, values.shape, 1)
    return jnp.where(lane == depth - 1, 0.0, pltpu.roll(values, depth - 1, 1)) - values


def row_lower(values):
    row = lax.broadcasted_iota(jnp.int32, values.shape, 0)
    return values - jnp.where(row == 0, 0.0, pltpu.roll(values, 1, 0))


def row_upper(values):
    rows = values.shape[0]
    row = lax.broadcasted_iota(jnp.int32, values.shape, 0)
    return jnp.where(row == rows - 1, 0.0, pltpu.roll(values, rows - 1, 0)) - values


def velocity_gain(coeffs, force_x, force_z, push_x, push_z):
    solid, couple, fluid, _ = coeffs
    return (
        solid * force_x + couple * push_x,
        solid * force_z + couple * push_z,
        -couple * force_x - fluid * push_x,
        -couple * force_z - fluid * push_z,
    )


def stress_gain(coeffs, strain_x, strain_z, inflow, shear):
    lame, modulus, coupling, fluid = coeffs
    dilation = strain_x + strain_z
    common = lame * dilation - coupling * inflow
    return (
        common + 2.0 * modulus * strain_x,
        common + 2.0 * modulus * strain_z,
        modulus * shear,
        -coupling * dilation - fluid * inflow,
    )


def beyond_gain(coeffs, vel_x, vel_z, flow_x):
    lame, modulus, coupling, fluid = coeffs
    return (
        (lame + 2.0 * modulus) * vel_x - coupling * flow_x,
        lame * vel_x - coupling * flow_x,
        modulus * vel_z,
        -coupling * vel_x - fluid * flow_x,
    )


def plus(left, right):
    return tuple(a + b for a, b in zip(left, right))


def minus(left, right):
    return tuple(a - b for a, b in zip(left, right))


def load_coeffs(ref):
    return tuple(ref[pl.ds(i, 1), :] for i in range(4))


def edge_kernel(
    sizes,
    state_hbm,
    forward_hbm,
    vel_hbm,
    stress_hbm,
    cells_hbm,
    force_hbm,
    source_hbm,
    state,
    forward,
    forcing,
    message_core,
    message_chip,
    vel_ref,
    stress_ref,
    cells,
    force,
    by_source,
    source,
    sems,
):
    events, rows, depth, steps, sources = sizes
    copies = [
        pltpu.make_async_copy(src, dst, sems.at[i])
        for i, (src, dst) in enumerate(
            [
                (cells_hbm, cells),
                (force_hbm, force),
                (source_hbm, source),
                (vel_hbm, vel_ref),
                (stress_hbm, stress_ref),
                (state_hbm, state),
                (forward_hbm, forward),
            ]
        )
    ]
    for copy in copies:
        copy.start()
    copies[0].wait()
    copies[1].wait()
    lanes = cells.shape[1]
    local = cells[...] & (rows * depth - 1)
    slot = (local // depth) * LAYER + (local & (depth - 1)) - (depth - LAYER)
    layers = None
    for block in range(cells.shape[0]):
        spots = lax.broadcasted_iota(jnp.int32, (depth, lanes), 0)
        hit = (spots == slot[block : block + 1, :]).astype(jnp.float32)
        part = lax.dot_general(
            force[...],
            hit,
            (((1,), (1,)), ((), ())),
            precision=EXACT,
            preferred_element_type=jnp.float32,
        )
        if block:
            part = pltpu.roll(part, part.shape[0] - 2 * block, 0)
        layers = part if layers is None else layers + part
    lane = lax.broadcasted_iota(jnp.int32, layers.shape, 1)
    for row in range(rows):
        moved = pltpu.roll(layers, (depth - LAYER - LAYER * row) % depth, 1)
        by_source[pl.ds(row, layers.shape[0], stride=rows), :] = jnp.where(
            lane >= depth - LAYER, moved, 0.0
        )
    copies[2].wait()
    blocks = cells.shape[0]
    for event in range(events):
        record = source[event]
        for step in range(steps):
            for part in range(2):
                at = (record * steps + step) * 2 * blocks + part
                forcing[pl.ds(((step * 2 + part) * events + event) * rows, rows), :] = by_source[
                    pl.ds(pl.multiple_of(at * rows, rows), rows), :
                ]
    for copy in copies[3:6]:
        copy.wait()
    vel = load_coeffs(vel_ref)
    stress = load_coeffs(stress_ref)
    odd = lax.rem(lax.axis_index("gx"), 2) == 1
    last = rows - 1

    def rim(chunk, field, row):
        return state[pl.ds((field * events + chunk) * rows + row, 8, stride=rows), :]

    def pushed(chunk, step, part, row):
        return forcing[
            pl.ds(((step * 2 + part) * events + chunk) * rows + row, 8, stride=rows), :
        ]

    for chunk in range(0, events, 8):
        first = [rim(chunk, f, 0) for f in range(FIELDS)]
        second = [rim(chunk, f, 1) for f in range(FIELDS)]
        final = [rim(chunk, f, last) for f in range(FIELDS)]
        inner = {f: rim(chunk, f, last - 1) for f in (SXX, SXZ, PR)}

        def kicked(fields, gains, step, row):
            vel_x, vel_z, flow_x, flow_z = plus(fields, gains)
            return (
                vel_x + pushed(chunk, step, 0, row),
                vel_z + pushed(chunk, step, 1, row),
                flow_x,
                flow_z,
            )

        def forces(fields, before):
            return (
                fields[SXX] - before[SXX] + depth_lower(fields[SXZ]),
                fields[SXZ] - before[SXZ] + depth_lower(fields[SZZ]),
                fields[PR] - before[PR] + vel[3] * fields[QX],
                depth_lower(fields[PR]) + vel[3] * fields[QZ],
            )

        nothing = {SXX: 0.0, SXZ: 0.0, PR: 0.0}
        vel_first = kicked(first[:4], velocity_gain(vel, *forces(first, nothing)), 0, 0)
        vel_second = kicked(second[:4], velocity_gain(vel, *forces(second, first)), 0, 1)
        vel_final = kicked(final[:4], velocity_gain(vel, *forces(final, inner)), 0, last)
        stress_first = plus(
            first[4:],
            stress_gain(
                stress,
                vel_second[0] - vel_first[0],
                depth_upper(vel_first[1]),
                vel_second[2] - vel_first[2] + depth_upper(vel_first[3]),
                depth_upper(vel_first[0]) + vel_second[1] - vel_first[1],
            ),
        )
        stress_final = plus(
            final[4:],
            stress_gain(
                stress,
                -vel_final[0],
                depth_upper(vel_final[1]),
                -vel_final[2] + depth_upper(vel_final[3]),
                depth_upper(vel_final[0]) - vel_final[1],
            ),
        )
        again = kicked(
            vel_first,
            velocity_gain(vel, *forces(list(vel_first) + list(stress_first), nothing)),
            1,
            0,
        )
        right = [final[SXX], final[SXZ], final[PR], stress_final[0], stress_final[2], stress_final[3]]
        left = [vel_first[0], vel_first[1], vel_first[2], again[0], again[1], again[2]]
        for i in range(HALO):
            at = pl.ds(i * events + chunk, 8)
            message_core[at, :] = jnp.where(odd, left[i], right[i])
            message_chip[at, :] = jnp.where(odd, right[i], left[i])
    copies[6].wait()


def bulk_kernel(
    sizes, state_in, forward, forcing, vel_ref, stress_ref, state, weights, sums
):
    events, rows, depth, steps, _ = sizes
    vel = tuple(jnp.broadcast_to(c, (rows, depth)) for c in load_coeffs(vel_ref))
    stress = tuple(jnp.broadcast_to(c, (rows, depth)) for c in load_coeffs(stress_ref))
    pair = 2

    def body(i, carry):
        perm, poro = carry
        for sub in range(pair):
            event = i * pair + sub

            def tile(kind):
                return pl.ds(pl.multiple_of((kind * events + event) * rows, rows), rows)

            fields = [state_in[tile(f), :] for f in range(FIELDS)]
            for step in range(steps):
                factors = []
                for kind in range(3):
                    at = (step * 3 + kind) * events * rows
                    both = forward[pl.ds(pl.multiple_of(at + i * pair * rows, pair * rows), pair * rows), :]
                    value = both.astype(jnp.float32)[sub * rows : (sub + 1) * rows, :]
                    weights[tile(step * 3 + kind), :] = value
                    factors.append(value)
                gains = velocity_gain(
                    vel,
                    row_lower(fields[SXX]) + depth_lower(fields[SXZ]),
                    row_lower(fields[SXZ]) + depth_lower(fields[SZZ]),
                    row_lower(fields[PR]) + vel[3] * fields[QX],
                    depth_lower(fields[PR]) + vel[3] * fields[QZ],
                )
                fields[:4] = plus(fields[:4], gains)
                fields[VX] = fields[VX] + forcing[tile(step * 2), :]
                fields[VZ] = fields[VZ] + forcing[tile(step * 2 + 1), :]
                perm = perm + fields[QX] * factors[0] + fields[QZ] * factors[1]
                fields[4:] = plus(
                    fields[4:],
                    stress_gain(
                        stress,
                        row_upper(fields[VX]),
                        depth_upper(fields[VZ]),
                        row_upper(fields[QX]) + depth_upper(fields[QZ]),
                        depth_upper(fields[VX]) + row_upper(fields[VZ]),
                    ),
                )
                poro = poro + fields[PR] * factors[2]
            for f in range(FIELDS):
                state[tile(f), :] = fields[f]
        return perm, poro

    zero = jnp.zeros((rows, depth), jnp.float32)
    perm, poro = lax.fori_loop(0, events // pair, body, (zero, zero))
    sums[pl.ds(0, rows), :] = perm
    sums[pl.ds(rows, rows), :] = poro


def join_kernel(
    sizes,
    normalizer,
    state_in,
    weights,
    sums,
    sent_core,
    sent_chip,
    got_core,
    got_chip,
    vel_ref,
    stress_ref,
    state,
    totals,
):
    events, rows, depth, _, _ = sizes
    vel = load_coeffs(vel_ref)
    stress = load_coeffs(stress_ref)
    place = lax.axis_index("gx")
    odd = lax.rem(place, 2) == 1
    has_left = place > 0
    has_right = place < lax.axis_size("gx") - 1
    last = rows - 1
    perm = sums[pl.ds(0, rows), :]
    poro = sums[pl.ds(rows, rows), :]

    def forces(stresses, flows):
        return (
            stresses[0] + depth_lower(stresses[2]),
            stresses[2] + depth_lower(stresses[1]),
            stresses[3] + vel[3] * flows[0],
            depth_lower(stresses[3]) + vel[3] * flows[1],
        )

    def from_before(stress_x, stress_xz, pressure):
        return velocity_gain(vel, -stress_x, -stress_xz, -pressure, 0.0)

    def strains(vels, after):
        return stress_gain(
            stress,
            after[0] - vels[0],
            depth_upper(vels[1]),
            after[2] - vels[2] + depth_upper(vels[3]),
            depth_upper(vels[0]) + after[1] - vels[1],
        )

    for chunk in range(0, events, 8):

        def row_of(ref, i):
            return ref[pl.ds(i * events + chunk, 8), :]

        own_core = [row_of(sent_core, i) for i in range(HALO)]
        own_chip = [row_of(sent_chip, i) for i in range(HALO)]
        new_core = [row_of(got_core, i) for i in range(HALO)]
        new_chip = [row_of(got_chip, i) for i in range(HALO)]
        left_own = [jnp.where(odd, a, b) for a, b in zip(own_core, own_chip)]
        right_own = [jnp.where(odd, b, a) for a, b in zip(own_core, own_chip)]
        left = [jnp.where(has_left, jnp.where(odd, a, b), 0.0) for a, b in zip(new_core, new_chip)]
        right = [jnp.where(has_right, jnp.where(odd, b, a), 0.0) for a, b in zip(new_core, new_chip)]

        gain_first = from_before(*left[:3])
        true_first = plus(left_own[:3], gain_first[:3])
        before = beyond_gain(stress, *true_first)
        before = [
            jnp.where(has_left, a + b, 0.0)
            for a, b in zip(left[3:], (before[0], before[2], before[3]))
        ]
        nothing = (0.0, 0.0, 0.0)
        stress_first = strains(gain_first, nothing)
        gain_after = from_before(*right_own[:3])
        after = plus(right[:3], gain_after[:3])
        after = [jnp.where(has_right, a, 0.0) for a in after]
        stress_last = beyond_gain(stress, *after)
        true_last = plus(right_own[3:], (stress_last[0], stress_last[2], stress_last[3]))

        vel_first = plus(
            plus(gain_first, velocity_gain(vel, *forces(stress_first, gain_first[2:]))),
            from_before(*before),
        )
        vel_second = from_before(stress_first[0], stress_first[2], stress_first[3])
        vel_last = velocity_gain(
            vel,
            stress_last[0] + depth_lower(stress_last[2]),
            stress_last[2] + depth_lower(stress_last[1]),
            stress_last[3],
            depth_lower(stress_last[3]),
        )
        stress_after = strains(gain_after, nothing)
        again = plus(
            plus(gain_after, velocity_gain(vel, *forces(stress_after, gain_after[2:]))),
            from_before(*true_last),
        )
        again = [jnp.where(has_right, a + b, 0.0) for a, b in zip(right[3:], again)]
        end_first = plus(stress_first, strains(vel_first, vel_second))
        end_second = strains(vel_second, nothing)
        end_inner = beyond_gain(stress, *vel_last[:3])
        end_last = plus(stress_last, strains(vel_last, again))

        def factor(step, kind, row):
            return weights[pl.ds(((step * 3 + kind) * events + chunk) * rows + row, 8, stride=rows), :]

        perm = perm + gain_first[2] * factor(0, 0, 0) + gain_first[3] * factor(0, 1, 0)
        for row, vels in ((0, vel_first), (1, vel_second), (last, vel_last)):
            perm = perm + vels[2] * factor(1, 0, row) + vels[3] * factor(1, 1, row)
        poro = poro + stress_first[3] * factor(0, 2, 0) + stress_last[3] * factor(0, 2, last)
        ends = ((0, end_first), (1, end_second), (last - 1, end_inner), (last, end_last))
        for row, stresses in ends:
            poro = poro + stresses[3] * factor(1, 2, row)

        changes = [(0, 0, vel_first), (1, 0, vel_second), (last, 0, vel_last)]
        changes += [(row, 4, stresses) for row, stresses in ends]
        for row, start, values in changes:
            for i, value in enumerate(values):
                at = pl.ds(((start + i) * events + chunk) * rows + row, 8, stride=rows)
                state[at, :] = state_in[at, :] + value

    perm = jnp.sum(perm, axis=0, keepdims=True) * (vel[2] * vel[3] * normalizer)
    poro = jnp.sum(poro, axis=0, keepdims=True) * (stress[3] * normalizer)
    totals[pl.ds(0, 1), :] = perm
    totals[pl.ds(1, 1), :] = poro


def swap_with(value, size, mask):
    return lax.ppermute(value, "gx", [(i, i ^ mask) for i in range(size)])


def swap_over_chips(value, groups, size):
    route = []
    for group in range(groups):
        base = group * size
        other = (group ^ 1) * size
        for i in range(1, size - 1, 2):
            route += [(base + i, base + i + 1), (base + i + 1, base + i)]
        route += [(base, other), (base + size - 1, other + size - 1)]
    return lax.ppermute(value, ("groups", "gx"), route)


def shards(
    adjoint_state, forward_fields, vel_coeffs, stress_coeffs, drm_cells, drm_force, source_id
):
    fields, events, rows, depth = adjoint_state.shape
    steps = forward_fields.shape[0]
    sources = drm_force.shape[0]
    entries = drm_cells.shape[0]
    size = lax.axis_size("gx")
    groups = lax.axis_size("groups")
    sizes = (events, rows, depth, steps, sources)
    blocks = entries // 128
    tiles = events * rows
    f32 = jnp.float32
    any_space = pl.BlockSpec(memory_space=pl.ANY)
    vmem = pl.BlockSpec(memory_space=pltpu.VMEM)
    state = adjoint_state.reshape(fields * tiles, depth)
    forward = forward_fields.reshape(steps * 3 * tiles, depth)
    cells = drm_cells.reshape(blocks, 128)
    force = drm_force.reshape(sources * steps, 2, blocks, 128).transpose(0, 2, 1, 3)
    force = force.reshape(sources * steps * 2 * blocks, 128)
    message = jax.ShapeDtypeStruct((HALO * events, depth), f32)

    state, forward, forcing, message_core, message_chip = pl.pallas_call(
        functools.partial(edge_kernel, sizes),
        out_shape=(
            pltpu.VMEM(state.shape, f32),
            pltpu.VMEM(forward.shape, forward.dtype),
            pltpu.VMEM((steps * 2 * tiles, depth), f32),
            message,
            message,
        ),
        in_specs=[any_space] * 7,
        out_specs=(vmem,) * 5,
        scratch_shapes=[
            pltpu.VMEM(vel_coeffs.shape, f32),
            pltpu.VMEM(stress_coeffs.shape, f32),
            pltpu.VMEM(cells.shape, jnp.int32),
            pltpu.VMEM(force.shape, f32),
            pltpu.VMEM((force.shape[0] * rows, depth), f32),
            pltpu.SMEM(source_id.shape, jnp.int32),
            pltpu.SemaphoreType.DMA((7,)),
        ],
        name="edges",
    )(state, forward, vel_coeffs, stress_coeffs, cells, force, source_id)

    got_chip = swap_over_chips(message_chip, groups, size)
    got_core = swap_with(message_core, size, 1)

    state, weights, sums = pl.pallas_call(
        functools.partial(bulk_kernel, sizes),
        out_shape=(
            pltpu.VMEM(state.shape, f32),
            pltpu.VMEM((steps * 3 * tiles, depth), f32),
            pltpu.VMEM((2 * rows, depth), f32),
        ),
        in_specs=[vmem] * 5,
        out_specs=(vmem,) * 3,
        input_output_aliases={0: 0},
        cost_estimate=pl.CostEstimate(
            flops=steps * 80 * tiles * depth, bytes_accessed=8 * state.size, transcendentals=0
        ),
        name="bulk",
    )(state, forward, forcing, vel_coeffs, stress_coeffs)

    normalizer = (events * rows * size) ** (-0.5)
    state, totals = pl.pallas_call(
        functools.partial(join_kernel, sizes, normalizer),
        out_shape=(
            pltpu.VMEM(state.shape, f32),
            jax.ShapeDtypeStruct((2, depth), f32),
        ),
        in_specs=[vmem] * 9,
        out_specs=(vmem,) * 2,
        input_output_aliases={0: 0},
        name="join",
    )(
        state,
        weights,
        sums,
        message_core,
        message_chip,
        got_core,
        got_chip,
        vel_coeffs,
        stress_coeffs,
    )
    mask = 1
    while mask < size:
        totals = totals + swap_with(totals, size, mask | 1)
        mask *= 2
    return state.reshape(adjoint_state.shape), totals


def solution(mesh):
    in_specs = (
        P(None, "groups", "gx", None),
        P(None, None, "groups", "gx", None),
        P("groups", None),
        P("groups", None),
        P("gx"),
        P("groups", None, None, "gx"),
        P("groups"),
    )
    out_specs = (P(None, "groups", "gx", None), P("groups", None))
    return jax.shard_map(shards, mesh=mesh, in_specs=in_specs, out_specs=out_specs, check_vma=False)
```

```python
import functools

import jax
import jax.numpy as jnp
from jax import lax
from jax.experimental import pallas as pl
from jax.experimental.pallas import tpu as pltpu
from jax.sharding import PartitionSpec as P

LAYER = 8
FIELDS = 8
VX, VZ, QX, QZ, SXX, SZZ, SXZ, PR = range(FIELDS)
HALO = 6
GROUPS = (16, 8, 4, 2)
ROOM = 16 << 20
EXACT = lax.Precision.HIGHEST


def depth_lower(values):
    lane = lax.broadcasted_iota(jnp.int32, values.shape, 1)
    return values - jnp.where(lane == 0, 0.0, pltpu.roll(values, 1, 1))


def depth_upper(values):
    depth = values.shape[1]
    lane = lax.broadcasted_iota(jnp.int32, values.shape, 1)
    return jnp.where(lane == depth - 1, 0.0, pltpu.roll(values, depth - 1, 1)) - values


def row_lower(values):
    row = lax.broadcasted_iota(jnp.int32, values.shape, 0)
    return values - jnp.where(row == 0, 0.0, pltpu.roll(values, 1, 0))


def row_upper(values):
    rows = values.shape[0]
    row = lax.broadcasted_iota(jnp.int32, values.shape, 0)
    return jnp.where(row == rows - 1, 0.0, pltpu.roll(values, rows - 1, 0)) - values


def velocity_gain(coeffs, force_x, force_z, push_x, push_z):
    solid, couple, fluid, _ = coeffs
    return (
        solid * force_x + couple * push_x,
        solid * force_z + couple * push_z,
        -couple * force_x - fluid * push_x,
        -couple * force_z - fluid * push_z,
    )


def stress_gain(coeffs, strain_x, strain_z, inflow, shear):
    lame, modulus, coupling, fluid = coeffs
    dilation = strain_x + strain_z
    common = lame * dilation - coupling * inflow
    return (
        common + 2.0 * modulus * strain_x,
        common + 2.0 * modulus * strain_z,
        modulus * shear,
        -coupling * dilation - fluid * inflow,
    )


def beyond_gain(coeffs, vel_x, vel_z, flow_x):
    lame, modulus, coupling, fluid = coeffs
    return (
        (lame + 2.0 * modulus) * vel_x - coupling * flow_x,
        lame * vel_x - coupling * flow_x,
        modulus * vel_z,
        -coupling * vel_x - fluid * flow_x,
    )


def plus(left, right):
    return tuple(a + b for a, b in zip(left, right))


def minus(left, right):
    return tuple(a - b for a, b in zip(left, right))


def load_coeffs(ref):
    return tuple(ref[pl.ds(i, 1), :] for i in range(4))


def edge_kernel(
    sizes,
    state_hbm,
    forward_hbm,
    vel_hbm,
    stress_hbm,
    cells_hbm,
    force_hbm,
    source_hbm,
    state,
    forward,
    forcing,
    message_core,
    message_chip,
    vel_ref,
    stress_ref,
    cells,
    force,
    by_source,
    source,
    sems,
):
    events, rows, depth, steps, sources = sizes
    copies = [
        pltpu.make_async_copy(src, dst, sems.at[i])
        for i, (src, dst) in enumerate(
            [
                (cells_hbm, cells),
                (force_hbm, force),
                (source_hbm, source),
                (vel_hbm, vel_ref),
                (stress_hbm, stress_ref),
                (state_hbm, state),
                (forward_hbm, forward),
            ]
        )
    ]
    for copy in copies:
        copy.start()
    copies[0].wait()
    copies[1].wait()
    lanes = cells.shape[1]
    local = cells[...] & (rows * depth - 1)
    slot = (local // depth) * LAYER + (local & (depth - 1)) - (depth - LAYER)
    layers = None
    for block in range(cells.shape[0]):
        spots = lax.broadcasted_iota(jnp.int32, (depth, lanes), 0)
        hit = (spots == slot[block : block + 1, :]).astype(jnp.float32)
        part = lax.dot_general(
            force[...],
            hit,
            (((1,), (1,)), ((), ())),
            precision=EXACT,
            preferred_element_type=jnp.float32,
        )
        if block:
            part = pltpu.roll(part, part.shape[0] - 2 * block, 0)
        layers = part if layers is None else layers + part
    lane = lax.broadcasted_iota(jnp.int32, layers.shape, 1)
    for row in range(rows):
        moved = pltpu.roll(layers, (depth - LAYER - LAYER * row) % depth, 1)
        by_source[pl.ds(row, layers.shape[0], stride=rows), :] = jnp.where(
            lane >= depth - LAYER, moved, 0.0
        )
    copies[2].wait()
    blocks = cells.shape[0]
    for event in range(events):
        record = source[event]
        for step in range(steps):
            for part in range(2):
                at = (record * steps + step) * 2 * blocks + part
                forcing[pl.ds(((step * 2 + part) * events + event) * rows, rows), :] = by_source[
                    pl.ds(pl.multiple_of(at * rows, rows), rows), :
                ]
    for copy in copies[3:6]:
        copy.wait()
    vel = load_coeffs(vel_ref)
    stress = load_coeffs(stress_ref)
    odd = lax.rem(lax.axis_index("gx"), 2) == 1
    last = rows - 1

    def rim(chunk, field, row):
        return state[pl.ds((field * events + chunk) * rows + row, 8, stride=rows), :]

    def pushed(chunk, step, part, row):
        return forcing[
            pl.ds(((step * 2 + part) * events + chunk) * rows + row, 8, stride=rows), :
        ]

    for chunk in range(0, events, 8):
        first = [rim(chunk, f, 0) for f in range(FIELDS)]
        second = [rim(chunk, f, 1) for f in range(FIELDS)]
        final = [rim(chunk, f, last) for f in range(FIELDS)]
        inner = {f: rim(chunk, f, last - 1) for f in (SXX, SXZ, PR)}

        def kicked(fields, gains, step, row):
            vel_x, vel_z, flow_x, flow_z = plus(fields, gains)
            return (
                vel_x + pushed(chunk, step, 0, row),
                vel_z + pushed(chunk, step, 1, row),
                flow_x,
                flow_z,
            )

        def forces(fields, before):
            return (
                fields[SXX] - before[SXX] + depth_lower(fields[SXZ]),
                fields[SXZ] - before[SXZ] + depth_lower(fields[SZZ]),
                fields[PR] - before[PR] + vel[3] * fields[QX],
                depth_lower(fields[PR]) + vel[3] * fields[QZ],
            )

        nothing = {SXX: 0.0, SXZ: 0.0, PR: 0.0}
        vel_first = kicked(first[:4], velocity_gain(vel, *forces(first, nothing)), 0, 0)
        vel_second = kicked(second[:4], velocity_gain(vel, *forces(second, first)), 0, 1)
        vel_final = kicked(final[:4], velocity_gain(vel, *forces(final, inner)), 0, last)
        stress_first = plus(
            first[4:],
            stress_gain(
                stress,
                vel_second[0] - vel_first[0],
                depth_upper(vel_first[1]),
                vel_second[2] - vel_first[2] + depth_upper(vel_first[3]),
                depth_upper(vel_first[0]) + vel_second[1] - vel_first[1],
            ),
        )
        stress_final = plus(
            final[4:],
            stress_gain(
                stress,
                -vel_final[0],
                depth_upper(vel_final[1]),
                -vel_final[2] + depth_upper(vel_final[3]),
                depth_upper(vel_final[0]) - vel_final[1],
            ),
        )
        again = kicked(
            vel_first,
            velocity_gain(vel, *forces(list(vel_first) + list(stress_first), nothing)),
            1,
            0,
        )
        right = [final[SXX], final[SXZ], final[PR], stress_final[0], stress_final[2], stress_final[3]]
        left = [vel_first[0], vel_first[1], vel_first[2], again[0], again[1], again[2]]
        for i in range(HALO):
            at = pl.ds(i * events + chunk, 8)
            message_core[at, :] = jnp.where(odd, left[i], right[i])
            message_chip[at, :] = jnp.where(odd, right[i], left[i])
    copies[6].wait()


def bulk_kernel(
    sizes, state_in, forward, forcing, vel_ref, stress_ref, state, weights, sums
):
    events, rows, depth, steps, _ = sizes
    vel = tuple(jnp.broadcast_to(c, (rows, depth)) for c in load_coeffs(vel_ref))
    stress = tuple(jnp.broadcast_to(c, (rows, depth)) for c in load_coeffs(stress_ref))
    group = next(g for g in GROUPS if events % g == 0)

    def body(i, carry):
        perm, poro = carry

        def tile(kind, sub):
            return pl.ds(pl.multiple_of((kind * events + i * group + sub) * rows, rows), rows)

        fields = [[state_in[tile(f, sub), :] for f in range(FIELDS)] for sub in range(group)]
        for step in range(steps):
            factors = [[] for _ in range(group)]
            for kind in range(3):
                for sub in range(0, group, 2):
                    at = ((step * 3 + kind) * events + i * group + sub) * rows
                    both = forward[pl.ds(pl.multiple_of(at, 2 * rows), 2 * rows), :].astype(jnp.float32)
                    for half in range(2):
                        value = both[half * rows : (half + 1) * rows]
                        weights[tile(step * 3 + kind, sub + half), :] = value
                        factors[sub + half].append(value)
            for sub, own in enumerate(fields):
                gains = velocity_gain(
                    vel,
                    row_lower(own[SXX]) + depth_lower(own[SXZ]),
                    row_lower(own[SXZ]) + depth_lower(own[SZZ]),
                    row_lower(own[PR]) + vel[3] * own[QX],
                    depth_lower(own[PR]) + vel[3] * own[QZ],
                )
                own[:4] = plus(own[:4], gains)
                own[VX] = own[VX] + forcing[tile(step * 2, sub), :]
                own[VZ] = own[VZ] + forcing[tile(step * 2 + 1, sub), :]
                perm = perm + own[QX] * factors[sub][0] + own[QZ] * factors[sub][1]
            for sub, own in enumerate(fields):
                own[4:] = plus(
                    own[4:],
                    stress_gain(
                        stress,
                        row_upper(own[VX]),
                        depth_upper(own[VZ]),
                        row_upper(own[QX]) + depth_upper(own[QZ]),
                        depth_upper(own[VX]) + row_upper(own[VZ]),
                    ),
                )
                poro = poro + own[PR] * factors[sub][2]
        for sub, own in enumerate(fields):
            for f in range(FIELDS):
                state[tile(f, sub), :] = own[f]
        return perm, poro

    zero = jnp.zeros((rows, depth), jnp.float32)
    perm, poro = lax.fori_loop(0, events // group, body, (zero, zero))
    sums[pl.ds(0, rows), :] = perm
    sums[pl.ds(rows, rows), :] = poro


def join_kernel(
    sizes,
    normalizer,
    state_in,
    weights,
    sums,
    sent_core,
    sent_chip,
    got_core,
    got_chip,
    vel_ref,
    stress_ref,
    state,
    totals,
):
    events, rows, depth, _, _ = sizes
    vel = load_coeffs(vel_ref)
    stress = load_coeffs(stress_ref)
    place = lax.axis_index("gx")
    odd = lax.rem(place, 2) == 1
    has_left = place > 0
    has_right = place < lax.axis_size("gx") - 1
    last = rows - 1
    perm = sums[pl.ds(0, rows), :]
    poro = sums[pl.ds(rows, rows), :]

    def forces(stresses, flows):
        return (
            stresses[0] + depth_lower(stresses[2]),
            stresses[2] + depth_lower(stresses[1]),
            stresses[3] + vel[3] * flows[0],
            depth_lower(stresses[3]) + vel[3] * flows[1],
        )

    def from_before(stress_x, stress_xz, pressure):
        return velocity_gain(vel, -stress_x, -stress_xz, -pressure, 0.0)

    def strains(vels, after):
        return stress_gain(
            stress,
            after[0] - vels[0],
            depth_upper(vels[1]),
            after[2] - vels[2] + depth_upper(vels[3]),
            depth_upper(vels[0]) + after[1] - vels[1],
        )

    for chunk in range(0, events, 8):

        def row_of(ref, i):
            return ref[pl.ds(i * events + chunk, 8), :]

        own_core = [row_of(sent_core, i) for i in range(HALO)]
        own_chip = [row_of(sent_chip, i) for i in range(HALO)]
        new_core = [row_of(got_core, i) for i in range(HALO)]
        new_chip = [row_of(got_chip, i) for i in range(HALO)]
        left_own = [jnp.where(odd, a, b) for a, b in zip(own_core, own_chip)]
        right_own = [jnp.where(odd, b, a) for a, b in zip(own_core, own_chip)]
        left = [jnp.where(has_left, jnp.where(odd, a, b), 0.0) for a, b in zip(new_core, new_chip)]
        right = [jnp.where(has_right, jnp.where(odd, b, a), 0.0) for a, b in zip(new_core, new_chip)]

        gain_first = from_before(*left[:3])
        true_first = plus(left_own[:3], gain_first[:3])
        before = beyond_gain(stress, *true_first)
        before = [
            jnp.where(has_left, a + b, 0.0)
            for a, b in zip(left[3:], (before[0], before[2], before[3]))
        ]
        nothing = (0.0, 0.0, 0.0)
        stress_first = strains(gain_first, nothing)
        gain_after = from_before(*right_own[:3])
        after = plus(right[:3], gain_after[:3])
        after = [jnp.where(has_right, a, 0.0) for a in after]
        stress_last = beyond_gain(stress, *after)
        true_last = plus(right_own[3:], (stress_last[0], stress_last[2], stress_last[3]))

        vel_first = plus(
            plus(gain_first, velocity_gain(vel, *forces(stress_first, gain_first[2:]))),
            from_before(*before),
        )
        vel_second = from_before(stress_first[0], stress_first[2], stress_first[3])
        vel_last = velocity_gain(
            vel,
            stress_last[0] + depth_lower(stress_last[2]),
            stress_last[2] + depth_lower(stress_last[1]),
            stress_last[3],
            depth_lower(stress_last[3]),
        )
        stress_after = strains(gain_after, nothing)
        again = plus(
            plus(gain_after, velocity_gain(vel, *forces(stress_after, gain_after[2:]))),
            from_before(*true_last),
        )
        again = [jnp.where(has_right, a + b, 0.0) for a, b in zip(right[3:], again)]
        end_first = plus(stress_first, strains(vel_first, vel_second))
        end_second = strains(vel_second, nothing)
        end_inner = beyond_gain(stress, *vel_last[:3])
        end_last = plus(stress_last, strains(vel_last, again))

        def factor(step, kind, row):
            return weights[pl.ds(((step * 3 + kind) * events + chunk) * rows + row, 8, stride=rows), :]

        perm = perm + gain_first[2] * factor(0, 0, 0) + gain_first[3] * factor(0, 1, 0)
        for row, vels in ((0, vel_first), (1, vel_second), (last, vel_last)):
            perm = perm + vels[2] * factor(1, 0, row) + vels[3] * factor(1, 1, row)
        poro = poro + stress_first[3] * factor(0, 2, 0) + stress_last[3] * factor(0, 2, last)
        ends = ((0, end_first), (1, end_second), (last - 1, end_inner), (last, end_last))
        for row, stresses in ends:
            poro = poro + stresses[3] * factor(1, 2, row)

        changes = [(0, 0, vel_first), (1, 0, vel_second), (last, 0, vel_last)]
        changes += [(row, 4, stresses) for row, stresses in ends]
        for row, start, values in changes:
            for i, value in enumerate(values):
                at = pl.ds(((start + i) * events + chunk) * rows + row, 8, stride=rows)
                state[at, :] = state_in[at, :] + value

    perm = jnp.sum(perm, axis=0, keepdims=True) * (vel[2] * vel[3] * normalizer)
    poro = jnp.sum(poro, axis=0, keepdims=True) * (stress[3] * normalizer)
    totals[pl.ds(0, 1), :] = perm
    totals[pl.ds(1, 1), :] = poro


def swap_with(value, size, mask):
    return lax.ppermute(value, "gx", [(i, i ^ mask) for i in range(size)])


def swap_over_chips(value, groups, size):
    route = []
    for group in range(groups):
        base = group * size
        other = (group ^ 1) * size
        for i in range(1, size - 1, 2):
            route += [(base + i, base + i + 1), (base + i + 1, base + i)]
        route += [(base, other), (base + size - 1, other + size - 1)]
    return lax.ppermute(value, ("groups", "gx"), route)


def shards(
    adjoint_state, forward_fields, vel_coeffs, stress_coeffs, drm_cells, drm_force, source_id
):
    fields, events, rows, depth = adjoint_state.shape
    steps = forward_fields.shape[0]
    sources = drm_force.shape[0]
    entries = drm_cells.shape[0]
    size = lax.axis_size("gx")
    groups = lax.axis_size("groups")
    sizes = (events, rows, depth, steps, sources)
    blocks = entries // 128
    tiles = events * rows
    f32 = jnp.float32
    any_space = pl.BlockSpec(memory_space=pl.ANY)
    vmem = pl.BlockSpec(memory_space=pltpu.VMEM)
    state = adjoint_state.reshape(fields * tiles, depth)
    forward = forward_fields.reshape(steps * 3 * tiles, depth)
    cells = drm_cells.reshape(blocks, 128)
    force = drm_force.reshape(sources * steps, 2, blocks, 128).transpose(0, 2, 1, 3)
    force = force.reshape(sources * steps * 2 * blocks, 128)
    message = pltpu.VMEM((HALO * events, depth), f32)
    limits = pltpu.CompilerParams(vmem_limit_bytes=ROOM)

    def kept(space, *values):
        return tuple(pltpu.with_memory_space_constraint(v, space) for v in values)

    state, forward, forcing, message_core, message_chip, vel, stress = pl.pallas_call(
        functools.partial(edge_kernel, sizes),
        out_shape=(
            pltpu.VMEM(state.shape, f32),
            pltpu.VMEM(forward.shape, forward.dtype),
            pltpu.VMEM((steps * 2 * tiles, depth), f32),
            message,
            message,
            pltpu.VMEM(vel_coeffs.shape, f32),
            pltpu.VMEM(stress_coeffs.shape, f32),
        ),
        in_specs=[any_space] * 7,
        out_specs=(vmem,) * 7,
        scratch_shapes=[
            pltpu.VMEM(cells.shape, jnp.int32),
            pltpu.VMEM(force.shape, f32),
            pltpu.VMEM((force.shape[0] * rows, depth), f32),
            pltpu.SMEM(source_id.shape, jnp.int32),
            pltpu.SemaphoreType.DMA((7,)),
        ],
        compiler_params=limits,
        name="edges",
    )(*kept(pltpu.HBM, state, forward, vel_coeffs, stress_coeffs, cells, force, source_id))

    got_chip = swap_over_chips(message_chip, groups, size)
    got_core = swap_with(message_core, size, 1)

    state, weights, sums = pl.pallas_call(
        functools.partial(bulk_kernel, sizes),
        out_shape=(
            pltpu.VMEM(state.shape, f32),
            pltpu.VMEM((steps * 3 * tiles, depth), f32),
            pltpu.VMEM((2 * rows, depth), f32),
        ),
        in_specs=[vmem] * 5,
        out_specs=(vmem,) * 3,
        input_output_aliases={0: 0},
        compiler_params=limits,
        cost_estimate=pl.CostEstimate(
            flops=steps * 80 * tiles * depth, bytes_accessed=8 * state.size, transcendentals=0
        ),
        name="bulk",
    )(*kept(pltpu.VMEM, state, forward, forcing, vel, stress))

    normalizer = (events * rows * size) ** (-0.5)
    state, totals = pl.pallas_call(
        functools.partial(join_kernel, sizes, normalizer),
        out_shape=(
            pltpu.VMEM(state.shape, f32),
            pltpu.VMEM((2, depth), f32),
        ),
        in_specs=[vmem] * 9,
        out_specs=(vmem,) * 2,
        input_output_aliases={0: 0},
        compiler_params=limits,
        name="join",
    )(*kept(pltpu.VMEM, state, weights, sums, message_core, message_chip, got_core, got_chip, vel, stress))
    mask = 1
    while mask < size:
        totals = totals + swap_with(totals, size, mask | 1)
        mask *= 2
    return state.reshape(adjoint_state.shape), totals


def solution(mesh):
    in_specs = (
        P(None, "groups", "gx", None),
        P(None, None, "groups", "gx", None),
        P("groups", None),
        P("groups", None),
        P("gx"),
        P("groups", None, None, "gx"),
        P("groups"),
    )
    out_specs = (P(None, "groups", "gx", None), P("groups", None))
    return jax.shard_map(shards, mesh=mesh, in_specs=in_specs, out_specs=out_specs, check_vma=False)
```

```python
import functools

import jax
import jax.numpy as jnp
from jax import lax
from jax.experimental import pallas as pl
from jax.experimental.pallas import tpu as pltpu
from jax.sharding import PartitionSpec as P

LAYER = 8
FIELDS = 8
VX, VZ, QX, QZ, SXX, SZZ, SXZ, PR = range(FIELDS)
HALO = 6
PUSHED = ((0, 0), (0, 1), (1, 0), (0, -1))
GROUPS = (16, 8, 4, 2)
ROOM = 16 << 20


def depth_lower(values):
    lane = lax.broadcasted_iota(jnp.int32, values.shape, 1)
    return values - jnp.where(lane == 0, 0.0, pltpu.roll(values, 1, 1))


def depth_upper(values):
    depth = values.shape[1]
    lane = lax.broadcasted_iota(jnp.int32, values.shape, 1)
    return jnp.where(lane == depth - 1, 0.0, pltpu.roll(values, depth - 1, 1)) - values


def row_lower(values):
    row = lax.broadcasted_iota(jnp.int32, values.shape, 0)
    return values - jnp.where(row == 0, 0.0, pltpu.roll(values, 1, 0))


def row_upper(values):
    rows = values.shape[0]
    row = lax.broadcasted_iota(jnp.int32, values.shape, 0)
    return jnp.where(row == rows - 1, 0.0, pltpu.roll(values, rows - 1, 0)) - values


def velocity_gain(coeffs, force_x, force_z, push_x, push_z):
    solid, couple, fluid, _ = coeffs
    return (
        solid * force_x + couple * push_x,
        solid * force_z + couple * push_z,
        -couple * force_x - fluid * push_x,
        -couple * force_z - fluid * push_z,
    )


def stress_gain(coeffs, strain_x, strain_z, inflow, shear):
    lame, modulus, coupling, fluid = coeffs
    dilation = strain_x + strain_z
    common = lame * dilation - coupling * inflow
    return (
        common + 2.0 * modulus * strain_x,
        common + 2.0 * modulus * strain_z,
        modulus * shear,
        -coupling * dilation - fluid * inflow,
    )


def beyond_gain(coeffs, vel_x, vel_z, flow_x):
    lame, modulus, coupling, fluid = coeffs
    return (
        (lame + 2.0 * modulus) * vel_x - coupling * flow_x,
        lame * vel_x - coupling * flow_x,
        modulus * vel_z,
        -coupling * vel_x - fluid * flow_x,
    )


def plus(left, right):
    return tuple(a + b for a, b in zip(left, right))


def minus(left, right):
    return tuple(a - b for a, b in zip(left, right))


def load_coeffs(ref):
    return tuple(ref[pl.ds(i, 1), :] for i in range(4))


def at_row(layers, row, depth):
    lane = lax.broadcasted_iota(jnp.int32, layers.shape, 1)
    moved = pltpu.roll(layers, (depth - LAYER - LAYER * row) % depth, 1)
    return jnp.where(lane >= depth - LAYER, moved, 0.0)


def edge_kernel(
    sizes,
    state_hbm,
    vel_hbm,
    stress_hbm,
    cells_hbm,
    force_hbm,
    source_hbm,
    table_ref,
    message_core,
    message_chip,
    vel_ref,
    stress_ref,
    near,
    cells,
    force,
    near_force,
    pushes,
    source,
    sems,
):
    events, rows, depth, steps, sources = sizes
    copies = [
        pltpu.make_async_copy(src, dst, sems.at[i])
        for i, (src, dst) in enumerate(
            [
                (cells_hbm, cells),
                (force_hbm, force),
                (source_hbm, source),
                (vel_hbm, vel_ref),
                (stress_hbm, stress_ref),
                (state_hbm.at[:, pl.ds(0, 2)], near.at[:, pl.ds(0, 2)]),
                (state_hbm.at[:, pl.ds(rows - 2, 2)], near.at[:, pl.ds(rows - 2, 2)]),
            ]
        )
    ]
    for copy in copies:
        copy.start()
    copies[0].wait()
    copies[1].wait()
    lanes = cells.shape[1]
    local = cells[...] & (rows * depth - 1)
    slot = (local // depth) * LAYER + (local & (depth - 1)) - (depth - LAYER)
    layers = None
    rest = force[...]
    pieces = []
    for _ in range(3):
        pieces.append(rest.astype(jnp.bfloat16))
        rest = rest - pieces[-1].astype(jnp.float32)
    for block in range(cells.shape[0]):
        spots = lax.broadcasted_iota(jnp.int32, (depth, lanes), 0)
        hit = (spots == slot[block : block + 1, :]).astype(jnp.float32).astype(jnp.bfloat16)
        part = None
        for piece in pieces:
            term = lax.dot_general(
                piece, hit, (((1,), (1,)), ((), ())), preferred_element_type=jnp.float32
            )
            part = term if part is None else part + term
        if block:
            part = pltpu.roll(part, part.shape[0] - 2 * block, 0)
        layers = part if layers is None else layers + part
    table_ref[...] = layers
    def moved(row):
        return at_row(layers, row, depth)

    own = lax.broadcasted_iota(jnp.int32, layers.shape, 0) & (rows - 1)
    picked = jnp.where(own < 6, pltpu.roll(moved(1), 2, 0), pltpu.roll(moved(rows - 1), 6, 0))
    near_force[...] = jnp.where((own & 2) == 0, moved(0), picked)
    copies[2].wait()
    for event in range(events):
        record = pl.multiple_of(source[event] * rows, rows)
        pushes[pl.ds(event * rows, rows), :] = near_force[pl.ds(record, rows), :]
    for copy in copies[3:]:
        copy.wait()
    vel = load_coeffs(vel_ref)
    stress = load_coeffs(stress_ref)
    odd = lax.rem(lax.axis_index("gx"), 2) == 1
    last = rows - 1
    state = near.reshape(near.shape[0] * rows, depth)

    def rim(chunk, field, row):
        return state[pl.ds((field * events + chunk) * rows + row, 8, stride=rows), :]

    def pushed(chunk, step, part, row):
        at = PUSHED.index((step, row if row < last else -1)) * 2 + part
        return pushes[pl.ds(chunk * rows + at, 8, stride=rows), :]

    for chunk in range(0, events, 8):
        first = [rim(chunk, f, 0) for f in range(FIELDS)]
        second = [rim(chunk, f, 1) for f in range(FIELDS)]
        final = [rim(chunk, f, last) for f in range(FIELDS)]
        inner = {f: rim(chunk, f, last - 1) for f in (SXX, SXZ, PR)}

        def kicked(fields, gains, step, row):
            vel_x, vel_z, flow_x, flow_z = plus(fields, gains)
            return (
                vel_x + pushed(chunk, step, 0, row),
                vel_z + pushed(chunk, step, 1, row),
                flow_x,
                flow_z,
            )

        def forces(fields, before):
            return (
                fields[SXX] - before[SXX] + depth_lower(fields[SXZ]),
                fields[SXZ] - before[SXZ] + depth_lower(fields[SZZ]),
                fields[PR] - before[PR] + vel[3] * fields[QX],
                depth_lower(fields[PR]) + vel[3] * fields[QZ],
            )

        nothing = {SXX: 0.0, SXZ: 0.0, PR: 0.0}
        vel_first = kicked(first[:4], velocity_gain(vel, *forces(first, nothing)), 0, 0)
        vel_second = kicked(second[:4], velocity_gain(vel, *forces(second, first)), 0, 1)
        vel_final = kicked(final[:4], velocity_gain(vel, *forces(final, inner)), 0, last)
        stress_first = plus(
            first[4:],
            stress_gain(
                stress,
                vel_second[0] - vel_first[0],
                depth_upper(vel_first[1]),
                vel_second[2] - vel_first[2] + depth_upper(vel_first[3]),
                depth_upper(vel_first[0]) + vel_second[1] - vel_first[1],
            ),
        )
        stress_final = plus(
            final[4:],
            stress_gain(
                stress,
                -vel_final[0],
                depth_upper(vel_final[1]),
                -vel_final[2] + depth_upper(vel_final[3]),
                depth_upper(vel_final[0]) - vel_final[1],
            ),
        )
        again = kicked(
            vel_first,
            velocity_gain(vel, *forces(list(vel_first) + list(stress_first), nothing)),
            1,
            0,
        )
        right = [final[SXX], final[SXZ], final[PR], stress_final[0], stress_final[2], stress_final[3]]
        left = [vel_first[0], vel_first[1], vel_first[2], again[0], again[1], again[2]]
        for i in range(HALO):
            at = pl.ds(i * events + chunk, 8)
            message_core[at, :] = jnp.where(odd, left[i], right[i])
            message_chip[at, :] = jnp.where(odd, right[i], left[i])

def bulk_kernel(
    sizes,
    state_hbm,
    forward_hbm,
    source_hbm,
    table_ref,
    vel_ref,
    stress_ref,
    state,
    weights,
    sums,
    forward,
    by_source,
    source,
    sems,
):
    events, rows, depth, steps, _ = sizes
    group = next(g for g in GROUPS if events % g == 0)

    def copies(i):
        at = i * group * rows
        own = pl.ds(at if isinstance(at, int) else pl.multiple_of(at, group * rows), group * rows)
        return (
            pltpu.make_async_copy(state_hbm.at[:, own], state.at[:, own], sems.at[0, i]),
            pltpu.make_async_copy(forward_hbm.at[:, own], forward.at[:, own], sems.at[1, i]),
        )

    source_copy = pltpu.make_async_copy(source_hbm, source, sems.at[2, 0])
    source_copy.start()
    for i in range(events // group):
        for copy in copies(i):
            copy.start()
    layers = table_ref[...]
    for row in range(rows):
        by_source[pl.ds(row, layers.shape[0], stride=rows), :] = at_row(layers, row, depth)
    vel = tuple(jnp.broadcast_to(c, (rows, depth)) for c in load_coeffs(vel_ref))
    stress = tuple(jnp.broadcast_to(c, (rows, depth)) for c in load_coeffs(stress_ref))

    def body(i, carry):
        perm, poro = carry

        def tile(sub, count=1):
            at = (i * group + sub) * rows
            return pl.ds(pl.multiple_of(at, count * rows), count * rows)

        def pushed(step, part, sub):
            at = source[i * group + sub] * rows + step * 4 + part
            return by_source[pl.ds(pl.multiple_of(at * rows, rows), rows), :]

        for copy in copies(i):
            copy.wait()
        fields = [[state[f, tile(sub), :] for f in range(FIELDS)] for sub in range(group)]
        for step in range(steps):
            factors = [[] for _ in range(group)]
            for kind in range(3):
                for sub in range(0, group, 2):
                    both = forward[step * 3 + kind, tile(sub, 2), :].astype(jnp.float32)
                    for half in range(2):
                        value = both[half * rows : (half + 1) * rows]
                        weights[step * 3 + kind, tile(sub + half), :] = value
                        factors[sub + half].append(value)
            for sub, own in enumerate(fields):
                gains = velocity_gain(
                    vel,
                    row_lower(own[SXX]) + depth_lower(own[SXZ]),
                    row_lower(own[SXZ]) + depth_lower(own[SZZ]),
                    row_lower(own[PR]) + vel[3] * own[QX],
                    depth_lower(own[PR]) + vel[3] * own[QZ],
                )
                own[:4] = plus(own[:4], gains)
                own[VX] = own[VX] + pushed(step, 0, sub)
                own[VZ] = own[VZ] + pushed(step, 1, sub)
                perm = perm + own[QX] * factors[sub][0] + own[QZ] * factors[sub][1]
            for sub, own in enumerate(fields):
                own[4:] = plus(
                    own[4:],
                    stress_gain(
                        stress,
                        row_upper(own[VX]),
                        depth_upper(own[VZ]),
                        row_upper(own[QX]) + depth_upper(own[QZ]),
                        depth_upper(own[VX]) + row_upper(own[VZ]),
                    ),
                )
                poro = poro + own[PR] * factors[sub][2]
        for sub, own in enumerate(fields):
            for f in range(FIELDS):
                state[f, tile(sub), :] = own[f]
        return perm, poro

    zero = jnp.zeros((rows, depth), jnp.float32)
    source_copy.wait()
    perm, poro = lax.fori_loop(0, events // group, body, (zero, zero))
    sums[pl.ds(0, rows), :] = perm
    sums[pl.ds(rows, rows), :] = poro


def join_kernel(
    sizes,
    normalizer,
    weights,
    sums,
    sent_chip,
    sent_core,
    got_chip,
    got_core,
    vel_ref,
    stress_ref,
    changes,
    totals,
):
    events, rows, depth, _, _ = sizes
    vel = load_coeffs(vel_ref)
    stress = load_coeffs(stress_ref)
    place = lax.axis_index("gx")
    odd = lax.rem(place, 2) == 1
    has_left = place > 0
    has_right = place < lax.axis_size("gx") - 1
    last = rows - 1
    perm = sums[pl.ds(0, rows), :]
    poro = sums[pl.ds(rows, rows), :]

    def forces(stresses, flows):
        return (
            stresses[0] + depth_lower(stresses[2]),
            stresses[2] + depth_lower(stresses[1]),
            stresses[3] + vel[3] * flows[0],
            depth_lower(stresses[3]) + vel[3] * flows[1],
        )

    def from_before(stress_x, stress_xz, pressure):
        return velocity_gain(vel, -stress_x, -stress_xz, -pressure, 0.0)

    def strains(vels, after):
        return stress_gain(
            stress,
            after[0] - vels[0],
            depth_upper(vels[1]),
            after[2] - vels[2] + depth_upper(vels[3]),
            depth_upper(vels[0]) + after[1] - vels[1],
        )

    for chunk in range(0, events, 8):

        def row_of(ref, i):
            return ref[pl.ds(i * events + chunk, 8), :]

        own_core = [row_of(sent_core, i) for i in range(HALO)]
        own_chip = [row_of(sent_chip, i) for i in range(HALO)]
        new_core = [row_of(got_core, i) for i in range(HALO)]
        new_chip = [row_of(got_chip, i) for i in range(HALO)]
        left_own = [jnp.where(odd, a, b) for a, b in zip(own_core, own_chip)]
        right_own = [jnp.where(odd, b, a) for a, b in zip(own_core, own_chip)]
        left = [jnp.where(has_left, jnp.where(odd, a, b), 0.0) for a, b in zip(new_core, new_chip)]
        right = [jnp.where(has_right, jnp.where(odd, b, a), 0.0) for a, b in zip(new_core, new_chip)]

        gain_first = from_before(*left[:3])
        true_first = plus(left_own[:3], gain_first[:3])
        before = beyond_gain(stress, *true_first)
        before = [
            jnp.where(has_left, a + b, 0.0)
            for a, b in zip(left[3:], (before[0], before[2], before[3]))
        ]
        nothing = (0.0, 0.0, 0.0)
        stress_first = strains(gain_first, nothing)
        gain_after = from_before(*right_own[:3])
        after = plus(right[:3], gain_after[:3])
        after = [jnp.where(has_right, a, 0.0) for a in after]
        stress_last = beyond_gain(stress, *after)
        true_last = plus(right_own[3:], (stress_last[0], stress_last[2], stress_last[3]))

        vel_first = plus(
            plus(gain_first, velocity_gain(vel, *forces(stress_first, gain_first[2:]))),
            from_before(*before),
        )
        vel_second = from_before(stress_first[0], stress_first[2], stress_first[3])
        vel_last = velocity_gain(
            vel,
            stress_last[0] + depth_lower(stress_last[2]),
            stress_last[2] + depth_lower(stress_last[1]),
            stress_last[3],
            depth_lower(stress_last[3]),
        )
        stress_after = strains(gain_after, nothing)
        again = plus(
            plus(gain_after, velocity_gain(vel, *forces(stress_after, gain_after[2:]))),
            from_before(*true_last),
        )
        again = [jnp.where(has_right, a + b, 0.0) for a, b in zip(right[3:], again)]
        end_first = plus(stress_first, strains(vel_first, vel_second))
        end_second = strains(vel_second, nothing)
        end_inner = beyond_gain(stress, *vel_last[:3])
        end_last = plus(stress_last, strains(vel_last, again))

        def factor(step, kind, row):
            return weights[step * 3 + kind, pl.ds(chunk * rows + row, 8, stride=rows), :]

        perm = perm + gain_first[2] * factor(0, 0, 0) + gain_first[3] * factor(0, 1, 0)
        for row, vels in ((0, vel_first), (1, vel_second), (last, vel_last)):
            perm = perm + vels[2] * factor(1, 0, row) + vels[3] * factor(1, 1, row)
        poro = poro + stress_first[3] * factor(0, 2, 0) + stress_last[3] * factor(0, 2, last)
        ends = ((0, end_first), (1, end_second), (last - 1, end_inner), (last, end_last))
        for row, stresses in ends:
            poro = poro + stresses[3] * factor(1, 2, row)

        values = vel_first + vel_second + vel_last + end_first + end_second + end_inner + end_last
        for i, value in enumerate(values):
            changes[i, pl.ds(chunk, 8), :] = value

    perm = jnp.sum(perm, axis=0, keepdims=True) * (vel[2] * vel[3] * normalizer)
    poro = jnp.sum(poro, axis=0, keepdims=True) * (stress[3] * normalizer)
    totals[pl.ds(0, 1), :] = perm
    totals[pl.ds(1, 1), :] = poro


def finish_kernel(sizes, state_in, changes, state, out_hbm, sems):
    events, rows, _, _, _ = sizes
    last = rows - 1
    places = [(start, row, f) for start, ends in ((0, (0, 1, last)), (4, (0, 1, last - 1, last))) for row in ends for f in range(4)]
    copies = []
    for field in range(FIELDS):
        for i, (start, row, f) in enumerate(places):
            if start + f == field:
                at = pl.ds(row, events, stride=rows)
                state[field, at, :] = state_in[field, at, :] + changes[i]
        copies.append(pltpu.make_async_copy(state.at[field], out_hbm.at[field], sems.at[field]))
        copies[-1].start()
    for copy in copies:
        copy.wait()


def swap_with(value, size, mask):
    return lax.ppermute(value, "gx", [(i, i ^ mask) for i in range(size)])


def swap_over_chips(value, groups, size):
    route = []
    for group in range(groups):
        base = group * size
        other = (group ^ 1) * size
        for i in range(1, size - 1, 2):
            route += [(base + i, base + i + 1), (base + i + 1, base + i)]
        route += [(base, other), (base + size - 1, other + size - 1)]
    return lax.ppermute(value, ("groups", "gx"), route)


def shards(
    adjoint_state, forward_fields, vel_coeffs, stress_coeffs, drm_cells, drm_force, source_id
):
    fields, events, rows, depth = adjoint_state.shape
    steps = forward_fields.shape[0]
    sources = drm_force.shape[0]
    entries = drm_cells.shape[0]
    size = lax.axis_size("gx")
    groups = lax.axis_size("groups")
    sizes = (events, rows, depth, steps, sources)
    blocks = entries // 128
    tiles = events * rows
    f32 = jnp.float32
    any_space = pl.BlockSpec(memory_space=pl.ANY)
    vmem = pl.BlockSpec(memory_space=pltpu.VMEM)
    state = adjoint_state.reshape(fields, tiles, depth)
    forward = forward_fields.reshape(steps * 3, tiles, depth)
    cells = drm_cells.reshape(blocks, 128)
    force = drm_force.reshape(sources * steps, 2, blocks, 128).transpose(0, 2, 1, 3)
    force = force.reshape(sources * steps * 2 * blocks, 128)
    message = pltpu.VMEM((HALO * events, depth), f32)
    limits = pltpu.CompilerParams(vmem_limit_bytes=ROOM)

    def kept(space, *values):
        return tuple(pltpu.with_memory_space_constraint(v, space) for v in values)

    table, message_core, message_chip, vel, stress = pl.pallas_call(
        functools.partial(edge_kernel, sizes),
        out_shape=(
            pltpu.VMEM(force.shape, f32),
            message,
            message,
            pltpu.VMEM(vel_coeffs.shape, f32),
            pltpu.VMEM(stress_coeffs.shape, f32),
        ),
        in_specs=[any_space] * 6,
        out_specs=(vmem,) * 5,
        scratch_shapes=[
            pltpu.VMEM((fields * events, rows, depth), f32),
            pltpu.VMEM(cells.shape, jnp.int32),
            pltpu.VMEM(force.shape, f32),
            pltpu.VMEM(force.shape, f32),
            pltpu.VMEM((tiles, depth), f32),
            pltpu.SMEM(source_id.shape, jnp.int32),
            pltpu.SemaphoreType.DMA((7,)),
        ],
        compiler_params=limits,
        name="edges",
    )(
        *kept(
            pltpu.HBM,
            state.reshape(fields * events, rows, depth),
            vel_coeffs,
            stress_coeffs,
            cells,
            force,
            source_id,
        )
    )

    got_core = swap_with(message_core, size, 1)
    got_chip = swap_over_chips(message_chip, groups, size)

    state, weights, sums = pl.pallas_call(
        functools.partial(bulk_kernel, sizes),
        out_shape=(
            pltpu.VMEM(state.shape, f32),
            pltpu.VMEM(forward.shape, f32),
            pltpu.VMEM((2 * rows, depth), f32),
        ),
        in_specs=[any_space] * 3 + [vmem] * 3,
        out_specs=(vmem,) * 3,
        scratch_shapes=[
            pltpu.VMEM(forward.shape, forward.dtype),
            pltpu.VMEM((force.shape[0] * rows, depth), f32),
            pltpu.SMEM(source_id.shape, jnp.int32),
            pltpu.SemaphoreType.DMA((3, events)),
        ],
        compiler_params=limits,
        cost_estimate=pl.CostEstimate(
            flops=steps * 80 * tiles * depth, bytes_accessed=8 * state.size, transcendentals=0
        ),
        name="bulk",
    )(*kept(pltpu.HBM, state, forward, source_id), *kept(pltpu.VMEM, table, vel, stress))

    normalizer = (events * rows * size) ** (-0.5)
    rows_changed = 28
    changes, totals = pl.pallas_call(
        functools.partial(join_kernel, sizes, normalizer),
        out_shape=(
            pltpu.VMEM((rows_changed, events, depth), f32),
            pltpu.VMEM((2, depth), f32),
        ),
        in_specs=[vmem] * 8,
        out_specs=(vmem,) * 2,
        compiler_params=limits,
        name="join",
    )(*kept(pltpu.VMEM, weights, sums, message_chip, message_core, got_chip, got_core, vel, stress))

    _, out = pl.pallas_call(
        functools.partial(finish_kernel, sizes),
        out_shape=(pltpu.VMEM(state.shape, f32), jax.ShapeDtypeStruct(state.shape, f32)),
        in_specs=[vmem] * 2,
        out_specs=(vmem, any_space),
        input_output_aliases={0: 0},
        scratch_shapes=[pltpu.SemaphoreType.DMA((fields,))],
        compiler_params=limits,
        cost_estimate=pl.CostEstimate(flops=0, bytes_accessed=2 * 4 * state.size, transcendentals=0),
        name="finish",
    )(*kept(pltpu.VMEM, state, changes))
    mask = 1
    while mask < size:
        totals = totals + swap_with(totals, size, mask | 1)
        mask *= 2
    return out.reshape(adjoint_state.shape), totals


def solution(mesh):
    in_specs = (
        P(None, "groups", "gx", None),
        P(None, None, "groups", "gx", None),
        P("groups", None),
        P("groups", None),
        P("gx"),
        P("groups", None, None, "gx"),
        P("groups"),
    )
    out_specs = (P(None, "groups", "gx", None), P("groups", None))
    return jax.shard_map(shards, mesh=mesh, in_specs=in_specs, out_specs=out_specs, check_vma=False)
```

```python
import functools

import jax
import jax.numpy as jnp
from jax import lax
from jax.experimental import pallas as pl
from jax.experimental.pallas import tpu as pltpu
from jax.sharding import PartitionSpec as P

LAYER = 8
FIELDS = 8
VX, VZ, QX, QZ, SXX, SZZ, SXZ, PR = range(FIELDS)
HALO = 6
PUSHED = ((0, 0), (0, 1), (1, 0), (0, -1))
GROUPS = (16, 8, 4, 2)
ROOM = 16 << 20


def depth_lower(values):
    lane = lax.broadcasted_iota(jnp.int32, values.shape, 1)
    return values - jnp.where(lane == 0, 0.0, pltpu.roll(values, 1, 1))


def depth_upper(values):
    depth = values.shape[1]
    lane = lax.broadcasted_iota(jnp.int32, values.shape, 1)
    return jnp.where(lane == depth - 1, 0.0, pltpu.roll(values, depth - 1, 1)) - values


def row_lower(values):
    row = lax.broadcasted_iota(jnp.int32, values.shape, 0)
    return values - jnp.where(row == 0, 0.0, pltpu.roll(values, 1, 0))


def row_upper(values):
    rows = values.shape[0]
    row = lax.broadcasted_iota(jnp.int32, values.shape, 0)
    return jnp.where(row == rows - 1, 0.0, pltpu.roll(values, rows - 1, 0)) - values


def velocity_gain(coeffs, force_x, force_z, push_x, push_z):
    solid, couple, fluid, _ = coeffs
    return (
        solid * force_x + couple * push_x,
        solid * force_z + couple * push_z,
        -couple * force_x - fluid * push_x,
        -couple * force_z - fluid * push_z,
    )


def stress_gain(coeffs, strain_x, strain_z, inflow, shear):
    lame, modulus, coupling, fluid = coeffs
    dilation = strain_x + strain_z
    common = lame * dilation - coupling * inflow
    return (
        common + 2.0 * modulus * strain_x,
        common + 2.0 * modulus * strain_z,
        modulus * shear,
        -coupling * dilation - fluid * inflow,
    )


def beyond_gain(coeffs, vel_x, vel_z, flow_x):
    lame, modulus, coupling, fluid = coeffs
    return (
        (lame + 2.0 * modulus) * vel_x - coupling * flow_x,
        lame * vel_x - coupling * flow_x,
        modulus * vel_z,
        -coupling * vel_x - fluid * flow_x,
    )


def plus(left, right):
    return tuple(a + b for a, b in zip(left, right))


def minus(left, right):
    return tuple(a - b for a, b in zip(left, right))


def load_coeffs(ref):
    return tuple(ref[pl.ds(i, 1), :] for i in range(4))


def at_row(layers, row, depth):
    lane = lax.broadcasted_iota(jnp.int32, layers.shape, 1)
    moved = pltpu.roll(layers, (depth - LAYER - LAYER * row) % depth, 1)
    return jnp.where(lane >= depth - LAYER, moved, 0.0)


def edge_kernel(
    sizes,
    state_hbm,
    vel_hbm,
    stress_hbm,
    cells_hbm,
    force_hbm,
    source_hbm,
    table_ref,
    message_first,
    message_second,
    message_chip,
    vel_ref,
    stress_ref,
    near,
    cells,
    force,
    near_force,
    pushes,
    source,
    sems,
):
    events, rows, depth, steps, sources = sizes
    copies = [
        pltpu.make_async_copy(src, dst, sems.at[i])
        for i, (src, dst) in enumerate(
            [
                (cells_hbm, cells),
                (force_hbm, force),
                (source_hbm, source),
                (vel_hbm, vel_ref),
                (stress_hbm, stress_ref),
                (state_hbm.at[:, pl.ds(0, 2)], near.at[:, pl.ds(0, 2)]),
                (state_hbm.at[:, pl.ds(rows - 2, 2)], near.at[:, pl.ds(rows - 2, 2)]),
            ]
        )
    ]
    for copy in copies:
        copy.start()
    copies[0].wait()
    copies[1].wait()
    lanes = cells.shape[1]
    local = cells[...] & (rows * depth - 1)
    slot = (local // depth) * LAYER + (local & (depth - 1)) - (depth - LAYER)
    blocks = cells.shape[0]
    spots = lax.broadcasted_iota(jnp.int32, (depth, lanes), 0)
    hits = [(spots == slot[i : i + 1, :]).astype(jnp.float32).astype(jnp.bfloat16) for i in range(blocks)]
    rest = force[...]
    pieces = []
    for _ in range(3):
        pieces.append(rest.astype(jnp.bfloat16))
        rest = rest - pieces[-1].astype(jnp.float32)
    terms = [
        lax.dot_general(
            jnp.concatenate(pieces, axis=0),
            hit,
            (((1,), (1,)), ((), ())),
            preferred_element_type=jnp.float32,
        )
        for hit in hits
    ]
    count = force.shape[0]
    terms = [t[:count] + t[count : 2 * count] + t[2 * count :] for t in terms]
    layers = terms[0]
    for block in range(1, blocks):
        layers = layers + pltpu.roll(terms[block], count - 2 * block, 0)
    table_ref[...] = layers
    def moved(row):
        return at_row(layers, row, depth)

    own = lax.broadcasted_iota(jnp.int32, layers.shape, 0) & (rows - 1)
    picked = jnp.where(own < 6, pltpu.roll(moved(1), 2, 0), pltpu.roll(moved(rows - 1), 6, 0))
    near_force[...] = jnp.where((own & 2) == 0, moved(0), picked)
    copies[2].wait()
    for event in range(events):
        record = pl.multiple_of(source[event] * rows, rows)
        pushes[pl.ds(event * rows, rows), :] = near_force[pl.ds(record, rows), :]
    for copy in copies[3:]:
        copy.wait()
    vel = load_coeffs(vel_ref)
    stress = load_coeffs(stress_ref)
    odd = lax.rem(lax.axis_index("gx"), 2) == 1
    message_core = (message_first, message_second)
    last = rows - 1
    state = near.reshape(near.shape[0] * rows, depth)

    def rim(chunk, field, row):
        return state[pl.ds((field * events + chunk) * rows + row, 8, stride=rows), :]

    def pushed(chunk, step, part, row):
        at = PUSHED.index((step, row if row < last else -1)) * 2 + part
        return pushes[pl.ds(chunk * rows + at, 8, stride=rows), :]

    for chunk in range(0, events, 8):
        first = [rim(chunk, f, 0) for f in range(FIELDS)]
        second = [rim(chunk, f, 1) for f in range(FIELDS)]
        final = [rim(chunk, f, last) for f in range(FIELDS)]
        inner = {f: rim(chunk, f, last - 1) for f in (SXX, SXZ, PR)}

        def kicked(fields, gains, step, row):
            vel_x, vel_z, flow_x, flow_z = plus(fields, gains)
            return (
                vel_x + pushed(chunk, step, 0, row),
                vel_z + pushed(chunk, step, 1, row),
                flow_x,
                flow_z,
            )

        def forces(fields, before):
            return (
                fields[SXX] - before[SXX] + depth_lower(fields[SXZ]),
                fields[SXZ] - before[SXZ] + depth_lower(fields[SZZ]),
                fields[PR] - before[PR] + vel[3] * fields[QX],
                depth_lower(fields[PR]) + vel[3] * fields[QZ],
            )

        nothing = {SXX: 0.0, SXZ: 0.0, PR: 0.0}
        vel_first = kicked(first[:4], velocity_gain(vel, *forces(first, nothing)), 0, 0)
        vel_second = kicked(second[:4], velocity_gain(vel, *forces(second, first)), 0, 1)
        vel_final = kicked(final[:4], velocity_gain(vel, *forces(final, inner)), 0, last)
        stress_first = plus(
            first[4:],
            stress_gain(
                stress,
                vel_second[0] - vel_first[0],
                depth_upper(vel_first[1]),
                vel_second[2] - vel_first[2] + depth_upper(vel_first[3]),
                depth_upper(vel_first[0]) + vel_second[1] - vel_first[1],
            ),
        )
        stress_final = plus(
            final[4:],
            stress_gain(
                stress,
                -vel_final[0],
                depth_upper(vel_final[1]),
                -vel_final[2] + depth_upper(vel_final[3]),
                depth_upper(vel_final[0]) - vel_final[1],
            ),
        )
        again = kicked(
            vel_first,
            velocity_gain(vel, *forces(list(vel_first) + list(stress_first), nothing)),
            1,
            0,
        )
        right = [final[SXX], final[SXZ], final[PR], stress_final[0], stress_final[2], stress_final[3]]
        left = [vel_first[0], vel_first[1], vel_first[2], again[0], again[1], again[2]]
        for i in range(HALO):
            at = pl.ds(i * events + chunk, 8)
            half = message_core[i // 3]
            half[pl.ds(i % 3 * events + chunk, 8), :] = jnp.where(odd, left[i], right[i])
            message_chip[at, :] = jnp.where(odd, right[i], left[i])

def group_of(events):
    return next(g for g in GROUPS if events % g == 0)


def bulk_kernel(
    sizes,
    state_hbm,
    forward_hbm,
    source_hbm,
    table_ref,
    vel_ref,
    stress_ref,
    state,
    weights,
    sums,
    forward,
    by_source,
    source,
    sems,
):
    events, rows, depth, steps, _ = sizes
    group = group_of(events)

    def copies(i):
        at = i * group * rows
        own = pl.ds(at if isinstance(at, int) else pl.multiple_of(at, group * rows), group * rows)
        return (
            pltpu.make_async_copy(state_hbm.at[:, own], state.at[:, own], sems.at[0, i]),
            pltpu.make_async_copy(forward_hbm.at[:, own], forward.at[:, own], sems.at[1, i]),
        )

    source_copy = pltpu.make_async_copy(source_hbm, source, sems.at[0, events // group])
    source_copy.start()
    for i in range(events // group):
        for copy in copies(i):
            copy.start()
    layers = table_ref[...]
    for row in range(rows):
        by_source[pl.ds(row, layers.shape[0], stride=rows), :] = at_row(layers, row, depth)
    vel = tuple(jnp.broadcast_to(c, (rows, depth)) for c in load_coeffs(vel_ref))
    stress = tuple(jnp.broadcast_to(c, (rows, depth)) for c in load_coeffs(stress_ref))

    def body(i, carry):
        perm, poro = carry

        def tile(sub, count=1):
            at = (i * group + sub) * rows
            return pl.ds(pl.multiple_of(at, count * rows), count * rows)

        def pushed(step, part, sub):
            at = source[i * group + sub] * rows + step * 4 + part
            return by_source[pl.ds(pl.multiple_of(at * rows, rows), rows), :]

        for copy in copies(i):
            copy.wait()
        fields = [[state[f, tile(sub), :] for f in range(FIELDS)] for sub in range(group)]
        for step in range(steps):
            factors = [[] for _ in range(group)]
            for kind in range(3):
                for sub in range(0, group, 2):
                    both = forward[step * 3 + kind, tile(sub, 2), :].astype(jnp.float32)
                    for half in range(2):
                        value = both[half * rows : (half + 1) * rows]
                        weights[step * 3 + kind, tile(sub + half), :] = value
                        factors[sub + half].append(value)
            for sub, own in enumerate(fields):
                gains = velocity_gain(
                    vel,
                    row_lower(own[SXX]) + depth_lower(own[SXZ]),
                    row_lower(own[SXZ]) + depth_lower(own[SZZ]),
                    row_lower(own[PR]) + vel[3] * own[QX],
                    depth_lower(own[PR]) + vel[3] * own[QZ],
                )
                own[:4] = plus(own[:4], gains)
                own[VX] = own[VX] + pushed(step, 0, sub)
                own[VZ] = own[VZ] + pushed(step, 1, sub)
                perm = perm + own[QX] * factors[sub][0] + own[QZ] * factors[sub][1]
            for sub, own in enumerate(fields):
                own[4:] = plus(
                    own[4:],
                    stress_gain(
                        stress,
                        row_upper(own[VX]),
                        depth_upper(own[VZ]),
                        row_upper(own[QX]) + depth_upper(own[QZ]),
                        depth_upper(own[VX]) + row_upper(own[VZ]),
                    ),
                )
                poro = poro + own[PR] * factors[sub][2]
        for sub, own in enumerate(fields):
            for f in range(FIELDS):
                state[f, tile(sub), :] = own[f]
        return perm, poro

    zero = jnp.zeros((rows, depth), jnp.float32)
    source_copy.wait()
    perm, poro = lax.fori_loop(0, events // group, body, (zero, zero))
    sums[pl.ds(0, rows), :] = perm
    sums[pl.ds(rows, rows), :] = poro


def from_before(vel, stress_x, stress_xz, pressure):
    return velocity_gain(vel, -stress_x, -stress_xz, -pressure, 0.0)


def forces(vel, stresses, flows):
    return (
        stresses[0] + depth_lower(stresses[2]),
        stresses[2] + depth_lower(stresses[1]),
        stresses[3] + vel[3] * flows[0],
        depth_lower(stresses[3]) + vel[3] * flows[1],
    )


def strains(stress, vels, after):
    return stress_gain(
        stress,
        after[0] - vels[0],
        depth_upper(vels[1]),
        after[2] - vels[2] + depth_upper(vels[3]),
        depth_upper(vels[0]) + after[1] - vels[1],
    )


NOTHING = (0.0, 0.0, 0.0)


def left_changes(vel, stress, sent, got, factor):
    gain_first = from_before(vel, *got[:3])
    before = beyond_gain(stress, *plus(sent[:3], gain_first[:3]))
    before = plus(got[3:], (before[0], before[2], before[3]))
    stress_first = strains(stress, gain_first, NOTHING)
    vel_first = plus(
        plus(gain_first, velocity_gain(vel, *forces(vel, stress_first, gain_first[2:]))),
        from_before(vel, *before),
    )
    vel_second = from_before(vel, stress_first[0], stress_first[2], stress_first[3])
    end_first = plus(stress_first, strains(stress, vel_first, vel_second))
    end_second = strains(stress, vel_second, NOTHING)
    perm = gain_first[2] * factor(0, 0, 0) + gain_first[3] * factor(0, 1, 0)
    for row, vels in ((0, vel_first), (1, vel_second)):
        perm = perm + vels[2] * factor(1, 0, row) + vels[3] * factor(1, 1, row)
    poro = stress_first[3] * factor(0, 2, 0)
    for row, stresses in ((0, end_first), (1, end_second)):
        poro = poro + stresses[3] * factor(1, 2, row)
    return vel_first + vel_second + end_first + end_second, perm, poro


def right_changes(vel, stress, sent, got, factor, last):
    gain_after = from_before(vel, *sent[:3])
    stress_last = beyond_gain(stress, *plus(got[:3], gain_after[:3]))
    true_last = plus(sent[3:], (stress_last[0], stress_last[2], stress_last[3]))
    vel_last = velocity_gain(
        vel,
        stress_last[0] + depth_lower(stress_last[2]),
        stress_last[2] + depth_lower(stress_last[1]),
        stress_last[3],
        depth_lower(stress_last[3]),
    )
    stress_after = strains(stress, gain_after, NOTHING)
    again = plus(
        plus(gain_after, velocity_gain(vel, *forces(vel, stress_after, gain_after[2:]))),
        from_before(vel, *true_last),
    )
    again = plus(got[3:], again[:3])
    end_inner = beyond_gain(stress, *vel_last[:3])
    end_last = plus(stress_last, strains(stress, vel_last, again))
    perm = vel_last[2] * factor(1, 0, last) + vel_last[3] * factor(1, 1, last)
    poro = stress_last[3] * factor(0, 2, last)
    for row, stresses in ((last - 1, end_inner), (last, end_last)):
        poro = poro + stresses[3] * factor(1, 2, row)
    return vel_last + end_inner + end_last, perm, poro


def side_sums(sizes, over_chips, weights, sent, got, vel_ref, stress_ref, changes):
    events, rows, depth, _, _ = sizes
    vel = load_coeffs(vel_ref)
    stress = load_coeffs(stress_ref)
    last = rows - 1
    left, right = sides(over_chips)

    def fill(changed, partial):
        for chunk in range(0, events, 8):

            def row_of(refs, i):
                each = HALO // len(refs)
                return refs[i // each][pl.ds(i % each * events + chunk, 8), :]

            def factor(step, kind, row):
                return weights[step * 3 + kind, pl.ds(chunk * rows + row, 8, stride=rows), :]

            own = tuple(row_of(sent, i) for i in range(HALO))
            new = tuple(row_of(got, i) for i in range(HALO))
            values, perm, poro = changed(vel, stress, own, new, factor)
            for i, value in enumerate(values):
                changes[i, pl.ds(chunk, 8), :] = value
            partial = (partial[0] + perm, partial[1] + poro)
        return partial

    zero = (jnp.zeros((8, depth), jnp.float32),) * 2
    return lax.cond(
        left,
        lambda: fill(left_changes, zero),
        lambda: lax.cond(
            right, lambda: fill(functools.partial(right_changes, last=last), zero), lambda: zero
        ),
    )


def sides(over_chips):
    place = lax.axis_index("gx")
    odd = lax.rem(place, 2) == 1
    if over_chips:
        return jnp.logical_and(jnp.logical_not(odd), place > 0), jnp.logical_and(
            odd, place < lax.axis_size("gx") - 1
        )
    return odd, jnp.logical_not(odd)


def core_kernel(
    sizes, sums_in, weights, sent_a, sent_b, got_a, got_b, vel_ref, stress_ref, changes, sums
):
    rows = sizes[1]
    sent, got = (sent_a, sent_b), (got_a, got_b)
    perm, poro = side_sums(sizes, False, weights, sent, got, vel_ref, stress_ref, changes)
    sums[pl.ds(0, rows), :] = sums_in[pl.ds(0, rows), :] + perm
    sums[pl.ds(rows, rows), :] = sums_in[pl.ds(rows, rows), :] + poro


def chip_kernel(
    sizes, normalizer, sums, weights, sent, got, vel_ref, stress_ref, changes, totals
):
    rows = sizes[1]
    vel = load_coeffs(vel_ref)
    stress = load_coeffs(stress_ref)
    perm, poro = side_sums(sizes, True, weights, (sent,), (got,), vel_ref, stress_ref, changes)
    perm = jnp.sum(sums[pl.ds(0, rows), :] + perm, axis=0, keepdims=True)
    poro = jnp.sum(sums[pl.ds(rows, rows), :] + poro, axis=0, keepdims=True)
    totals[pl.ds(0, 1), :] = perm * (vel[2] * vel[3] * normalizer)
    totals[pl.ds(1, 1), :] = poro * (stress[3] * normalizer)


def finish_kernel(sizes, state_in, changes_core, changes_chip, state, out_hbm, done, sems):
    events, rows, _, _, _ = sizes
    last = rows - 1
    left_places = [(s + f, row) for s in (0, 4) for row in (0, 1) for f in range(4)]
    right_places = [(f, last) for f in range(4)] + [(4 + f, row) for row in (last - 1, last) for f in range(4)]

    def patch(changes, places, fields):
        for i, (field, row) in enumerate(places):
            if field in fields:
                at = pl.ds(row, events, stride=rows)
                state[field, at, :] = state_in[field, at, :] + changes[i]

    half = FIELDS // 2
    copies = []
    for i in range(2):
        fields = range(i * half, (i + 1) * half)
        for over_chips, changes in ((False, changes_core), (True, changes_chip)):
            left, right = sides(over_chips)
            pl.when(left)(functools.partial(patch, changes, left_places, fields))
            pl.when(right)(functools.partial(patch, changes, right_places, fields))
        own = pl.ds(i * half, half)
        copies.append(pltpu.make_async_copy(state.at[own], out_hbm.at[own], sems.at[i]))
        copies[i].start()
    done[...] = jnp.zeros_like(done)
    for copy in copies:
        copy.wait()


def swap_with(value, size, mask):
    return lax.ppermute(value, "gx", [(i, i ^ mask) for i in range(size)])


def swap_over_chips(value, groups, size):
    route = []
    for group in range(groups):
        base = group * size
        other = (group ^ 1) * size
        for i in range(1, size - 1, 2):
            route += [(base + i, base + i + 1), (base + i + 1, base + i)]
        route += [(base, other), (base + size - 1, other + size - 1)]
    return lax.ppermute(value, ("groups", "gx"), route)


def shards(
    adjoint_state, forward_fields, vel_coeffs, stress_coeffs, drm_cells, drm_force, source_id
):
    fields, events, rows, depth = adjoint_state.shape
    steps = forward_fields.shape[0]
    sources = drm_force.shape[0]
    entries = drm_cells.shape[0]
    size = lax.axis_size("gx")
    groups = lax.axis_size("groups")
    sizes = (events, rows, depth, steps, sources)
    blocks = entries // 128
    tiles = events * rows
    group = group_of(events)
    f32 = jnp.float32
    any_space = pl.BlockSpec(memory_space=pl.ANY)
    vmem = pl.BlockSpec(memory_space=pltpu.VMEM)
    state = adjoint_state.reshape(fields, tiles, depth)
    forward = forward_fields.reshape(steps * 3, tiles, depth)
    cells = drm_cells.reshape(blocks, 128)
    force = drm_force.reshape(sources * steps, 2, blocks, 128).transpose(0, 2, 1, 3)
    force = force.reshape(sources * steps * 2 * blocks, 128)
    message = pltpu.VMEM((HALO * events, depth), f32)
    half = pltpu.VMEM((HALO // 2 * events, depth), f32)
    limits = pltpu.CompilerParams(vmem_limit_bytes=ROOM)

    def kept(space, *values):
        return tuple(pltpu.with_memory_space_constraint(v, space) for v in values)

    table, message_first, message_second, message_chip, vel, stress = pl.pallas_call(
        functools.partial(edge_kernel, sizes),
        out_shape=(
            pltpu.VMEM(force.shape, f32),
            half,
            half,
            message,
            pltpu.VMEM(vel_coeffs.shape, f32),
            pltpu.VMEM(stress_coeffs.shape, f32),
        ),
        in_specs=[any_space] * 6,
        out_specs=(vmem,) * 6,
        scratch_shapes=[
            pltpu.VMEM((fields * events, rows, depth), f32),
            pltpu.VMEM(cells.shape, jnp.int32),
            pltpu.VMEM(force.shape, f32),
            pltpu.VMEM(force.shape, f32),
            pltpu.VMEM((tiles, depth), f32),
            pltpu.SMEM(source_id.shape, jnp.int32),
            pltpu.SemaphoreType.DMA((7,)),
        ],
        compiler_params=limits,
        name="edges",
    )(
        *kept(
            pltpu.HBM,
            state.reshape(fields * events, rows, depth),
            vel_coeffs,
            stress_coeffs,
            cells,
            force,
            source_id,
        )
    )

    got_first = swap_with(message_first, size, 1)
    got_second = swap_with(message_second, size, 1)
    got_chip = swap_over_chips(message_chip, groups, size)

    state, weights, sums = pl.pallas_call(
        functools.partial(bulk_kernel, sizes),
        out_shape=(
            pltpu.VMEM(state.shape, f32),
            pltpu.VMEM(forward.shape, f32),
            pltpu.VMEM((2 * rows, depth), f32),
        ),
        in_specs=[any_space] * 3 + [vmem] * 3,
        out_specs=(vmem,) * 3,
        scratch_shapes=[
            pltpu.VMEM(forward.shape, forward.dtype),
            pltpu.VMEM((force.shape[0] * rows, depth), f32),
            pltpu.SMEM(source_id.shape, jnp.int32),
            pltpu.SemaphoreType.DMA((2, events // group + 1)),
        ],
        compiler_params=limits,
        cost_estimate=pl.CostEstimate(
            flops=steps * 80 * tiles * depth, bytes_accessed=8 * state.size, transcendentals=0
        ),
        name="bulk",
    )(*kept(pltpu.HBM, state, forward, source_id), *kept(pltpu.VMEM, table, vel, stress))

    normalizer = (events * rows * size) ** (-0.5)
    changed = pltpu.VMEM((16, events, depth), f32)
    changes_core, sums = pl.pallas_call(
        functools.partial(core_kernel, sizes),
        out_shape=(changed, pltpu.VMEM(sums.shape, f32)),
        in_specs=[vmem] * 8,
        out_specs=(vmem,) * 2,
        compiler_params=limits,
        name="join_core",
    )(
        *kept(
            pltpu.VMEM,
            sums,
            weights,
            message_first,
            message_second,
            got_first,
            got_second,
            vel,
            stress,
        )
    )

    changes_chip, totals = pl.pallas_call(
        functools.partial(chip_kernel, sizes, normalizer),
        out_shape=(changed, pltpu.VMEM((2, depth), f32)),
        in_specs=[vmem] * 6,
        out_specs=(vmem,) * 2,
        compiler_params=limits,
        name="join_chip",
    )(*kept(pltpu.VMEM, sums, weights, message_chip, got_chip, vel, stress))

    _, out, done = pl.pallas_call(
        functools.partial(finish_kernel, sizes),
        out_shape=(
            pltpu.VMEM(state.shape, f32),
            jax.ShapeDtypeStruct(state.shape, f32),
            pltpu.VMEM((2, depth), f32),
        ),
        in_specs=[vmem] * 3,
        out_specs=(vmem, any_space, vmem),
        input_output_aliases={0: 0},
        scratch_shapes=[pltpu.SemaphoreType.DMA((2,))],
        compiler_params=limits,
        cost_estimate=pl.CostEstimate(flops=0, bytes_accessed=2 * 4 * state.size, transcendentals=0),
        name="finish",
    )(*kept(pltpu.VMEM, state, changes_core, changes_chip))

    mask = 1
    while mask < size:
        totals = totals + swap_with(totals, size, mask | 1)
        if mask * 4 == size:
            totals = totals + done
        mask *= 2
    return out.reshape(adjoint_state.shape), totals


def solution(mesh):
    in_specs = (
        P(None, "groups", "gx", None),
        P(None, None, "groups", "gx", None),
        P("groups", None),
        P("groups", None),
        P("gx"),
        P("groups", None, None, "gx"),
        P("groups"),
    )
    out_specs = (P(None, "groups", "gx", None), P("groups", None))
    return jax.shard_map(shards, mesh=mesh, in_specs=in_specs, out_specs=out_specs, check_vma=False)
```

```python
import functools

import jax
import jax.numpy as jnp
from jax import lax
from jax.experimental import pallas as pl
from jax.experimental.pallas import tpu as pltpu
from jax.sharding import PartitionSpec as P

LAYER = 8
FIELDS = 8
VX, VZ, QX, QZ, SXX, SZZ, SXZ, PR = range(FIELDS)
HALO = 6
SOON = 5
LATE = 3
PUSHED = ((0, 0), (0, 1), (1, 0), (0, -1))
GROUPS = (16, 8, 4, 2)
ROOM = 16 << 20


def depth_lower(values):
    lane = lax.broadcasted_iota(jnp.int32, values.shape, 1)
    return values - jnp.where(lane == 0, 0.0, pltpu.roll(values, 1, 1))


def depth_upper(values):
    depth = values.shape[1]
    lane = lax.broadcasted_iota(jnp.int32, values.shape, 1)
    return jnp.where(lane == depth - 1, 0.0, pltpu.roll(values, depth - 1, 1)) - values


def row_lower(values):
    row = lax.broadcasted_iota(jnp.int32, values.shape, 0)
    return values - jnp.where(row == 0, 0.0, pltpu.roll(values, 1, 0))


def row_upper(values):
    rows = values.shape[0]
    row = lax.broadcasted_iota(jnp.int32, values.shape, 0)
    return jnp.where(row == rows - 1, 0.0, pltpu.roll(values, rows - 1, 0)) - values


def velocity_gain(coeffs, force_x, force_z, push_x, push_z):
    solid, couple, fluid, _ = coeffs
    return (
        solid * force_x + couple * push_x,
        solid * force_z + couple * push_z,
        -couple * force_x - fluid * push_x,
        -couple * force_z - fluid * push_z,
    )


def stress_gain(coeffs, strain_x, strain_z, inflow, shear):
    lame, modulus, coupling, fluid = coeffs
    dilation = strain_x + strain_z
    common = lame * dilation - coupling * inflow
    return (
        common + 2.0 * modulus * strain_x,
        common + 2.0 * modulus * strain_z,
        modulus * shear,
        -coupling * dilation - fluid * inflow,
    )


def beyond_gain(coeffs, vel_x, vel_z, flow_x):
    lame, modulus, coupling, fluid = coeffs
    return (
        (lame + 2.0 * modulus) * vel_x - coupling * flow_x,
        lame * vel_x - coupling * flow_x,
        modulus * vel_z,
        -coupling * vel_x - fluid * flow_x,
    )


def plus(left, right):
    return tuple(a + b for a, b in zip(left, right))


def minus(left, right):
    return tuple(a - b for a, b in zip(left, right))


def load_coeffs(ref):
    return tuple(ref[pl.ds(i, 1), :] for i in range(4))


def at_row(layers, row, depth):
    lane = lax.broadcasted_iota(jnp.int32, layers.shape, 1)
    moved = pltpu.roll(layers, (depth - LAYER - LAYER * row) % depth, 1)
    return jnp.where(lane >= depth - LAYER, moved, 0.0)


def exact_pieces(values):
    pieces = []
    for _ in range(3):
        pieces.append(values.astype(jnp.bfloat16))
        values = values - pieces[-1].astype(jnp.float32)
    return pieces


def edge_kernel(
    sizes,
    state_hbm,
    forward_hbm,
    vel_hbm,
    stress_hbm,
    cells_hbm,
    force_hbm,
    source_hbm,
    row_hbm,
    forward,
    source_row,
    table_ref,
    message_first,
    message_second,
    message_chip,
    message_late,
    vel_ref,
    stress_ref,
    near,
    weights,
    cells,
    force,
    near_force,
    pushes,
    source,
    sems,
):
    events, rows, depth, steps, sources = sizes
    final_kind = steps * 3 - 1
    copies = [
        pltpu.make_async_copy(src, dst, sems.at[i])
        for i, (src, dst) in enumerate(
            [
                (cells_hbm, cells),
                (force_hbm, force),
                (source_hbm, source),
                (vel_hbm, vel_ref),
                (stress_hbm, stress_ref),
                (state_hbm.at[:, pl.ds(0, 2)], near.at[:, pl.ds(0, 2)]),
                (state_hbm.at[:, pl.ds(rows - 2, 2)], near.at[:, pl.ds(rows - 2, 2)]),
                (forward_hbm.at[pl.ds(final_kind, 1)], forward.at[pl.ds(final_kind, 1)]),
                (row_hbm, source_row),
                (forward_hbm.at[pl.ds(0, final_kind)], forward.at[pl.ds(0, final_kind)]),
            ]
        )
    ]
    for copy in copies:
        copy.start()
    copies[0].wait()
    copies[1].wait()
    lanes = cells.shape[1]
    local = cells[...] & (rows * depth - 1)
    slot = (local // depth) * LAYER + (local & (depth - 1)) - (depth - LAYER)
    blocks = cells.shape[0]
    spots = lax.broadcasted_iota(jnp.int32, (depth, lanes), 0)
    hits = [(spots == slot[i : i + 1, :]).astype(jnp.float32).astype(jnp.bfloat16) for i in range(blocks)]
    pieces = exact_pieces(force[...])
    terms = [
        lax.dot_general(
            jnp.concatenate(pieces, axis=0),
            hit,
            (((1,), (1,)), ((), ())),
            preferred_element_type=jnp.float32,
        )
        for hit in hits
    ]
    count = force.shape[0]
    terms = [t[:count] + t[count : 2 * count] + t[2 * count :] for t in terms]
    layers = terms[0]
    for block in range(1, blocks):
        layers = layers + pltpu.roll(terms[block], count - 2 * block, 0)
    table_ref[...] = layers
    def moved(row):
        return at_row(layers, row, depth)

    own = lax.broadcasted_iota(jnp.int32, layers.shape, 0) & (rows - 1)
    picked = jnp.where(own < 6, pltpu.roll(moved(1), 2, 0), pltpu.roll(moved(rows - 1), 6, 0))
    near_force[...] = jnp.where((own & 2) == 0, moved(0), picked)
    copies[2].wait()
    for event in range(events):
        record = pl.multiple_of(source[event] * rows, rows)
        pushes[pl.ds(event * rows, rows), :] = near_force[pl.ds(record, rows), :]
    for copy in copies[3:-1]:
        copy.wait()
    weights[...] = forward[final_kind].astype(jnp.float32)
    vel = load_coeffs(vel_ref)
    stress = load_coeffs(stress_ref)
    odd = lax.rem(lax.axis_index("gx"), 2) == 1
    message_core = (message_first, message_second)
    last = rows - 1
    state = near.reshape(near.shape[0] * rows, depth)

    def rim(chunk, field, row):
        return state[pl.ds((field * events + chunk) * rows + row, 8, stride=rows), :]

    def pushed(chunk, step, part, row):
        at = PUSHED.index((step, row if row < last else -1)) * 2 + part
        return pushes[pl.ds(chunk * rows + at, 8, stride=rows), :]

    for chunk in range(0, events, 8):
        first = [rim(chunk, f, 0) for f in range(FIELDS)]
        second = [rim(chunk, f, 1) for f in range(FIELDS)]
        final = [rim(chunk, f, last) for f in range(FIELDS)]
        inner = {f: rim(chunk, f, last - 1) for f in (SXX, SXZ, PR)}

        def kicked(fields, gains, step, row):
            vel_x, vel_z, flow_x, flow_z = plus(fields, gains)
            return (
                vel_x + pushed(chunk, step, 0, row),
                vel_z + pushed(chunk, step, 1, row),
                flow_x,
                flow_z,
            )

        def forces(fields, before):
            return (
                fields[SXX] - before[SXX] + depth_lower(fields[SXZ]),
                fields[SXZ] - before[SXZ] + depth_lower(fields[SZZ]),
                fields[PR] - before[PR] + vel[3] * fields[QX],
                depth_lower(fields[PR]) + vel[3] * fields[QZ],
            )

        nothing = {SXX: 0.0, SXZ: 0.0, PR: 0.0}
        vel_first = kicked(first[:4], velocity_gain(vel, *forces(first, nothing)), 0, 0)
        vel_second = kicked(second[:4], velocity_gain(vel, *forces(second, first)), 0, 1)
        vel_final = kicked(final[:4], velocity_gain(vel, *forces(final, inner)), 0, last)
        stress_first = plus(
            first[4:],
            stress_gain(
                stress,
                vel_second[0] - vel_first[0],
                depth_upper(vel_first[1]),
                vel_second[2] - vel_first[2] + depth_upper(vel_first[3]),
                depth_upper(vel_first[0]) + vel_second[1] - vel_first[1],
            ),
        )
        stress_final = plus(
            final[4:],
            stress_gain(
                stress,
                -vel_final[0],
                depth_upper(vel_final[1]),
                -vel_final[2] + depth_upper(vel_final[3]),
                depth_upper(vel_final[0]) - vel_final[1],
            ),
        )
        again = kicked(
            vel_first,
            velocity_gain(vel, *forces(list(vel_first) + list(stress_first), nothing)),
            1,
            0,
        )
        right = [final[SXX], final[SXZ], final[PR], stress_final[0], stress_final[2], stress_final[3]]
        left = [vel_first[0], vel_first[1], vel_first[2], again[0], again[1], again[2]]
        for i in range(HALO):
            half = message_core[i // 3]
            half[pl.ds(i % 3 * events + chunk, 8), :] = jnp.where(odd, left[i], right[i])
        flow = vel[1] * stress_final[0] + vel[2] * stress_final[3]
        drain = stress[2] * again[0] + stress[3] * again[2]
        weight = weights[pl.ds(chunk * rows, 8, stride=rows), :]
        right_soon = right[:3] + [flow, stress_final[2]]
        left_soon = left[:3] + [drain, weight]
        right_late = [stress_final[0], stress_final[3], stress_final[3]]
        for i in range(SOON):
            message_chip[pl.ds(i * events + chunk, 8), :] = jnp.where(odd, right_soon[i], left_soon[i])
        for i in range(LATE):
            message_late[pl.ds(i * events + chunk, 8), :] = jnp.where(odd, right_late[i], left[3 + i])
    copies[-1].wait()


def group_of(events):
    return next(g for g in GROUPS if events % g == 0)


def bulk_kernel(
    sizes,
    state_in,
    forward,
    source_row,
    table_ref,
    vel_ref,
    stress_ref,
    late_in,
    state,
    weights,
    sums,
    late,
    forcing,
):
    events, rows, depth, steps, sources = sizes
    group = group_of(events)
    each = table_ref.shape[0] // sources
    kinds = [(step, part) for step in range(steps) for part in range(2)]
    table = jnp.concatenate(
        [
            table_ref[pl.ds(step * (each // steps) + part, sources, stride=each), :]
            for step, part in kinds
        ],
        axis=1,
    )
    pieces = exact_pieces(table)
    records = lax.broadcasted_iota(jnp.int32, (sources, events), 0)
    hit = (records == source_row[...]).astype(jnp.float32)
    by_event = lax.dot_general(
        jnp.concatenate([hit] * len(pieces), axis=0).astype(jnp.bfloat16),
        jnp.concatenate(pieces, axis=0),
        (((0,), (0,)), ((), ())),
        preferred_element_type=jnp.float32,
    )
    for kind in range(len(kinds)):
        layers = by_event[:, kind * depth : (kind + 1) * depth]
        for row in range(rows):
            at = pl.ds(kind * events * rows + row, events, stride=rows)
            forcing[at, :] = at_row(layers, row, depth)
    vel = tuple(jnp.broadcast_to(c, (rows, depth)) for c in load_coeffs(vel_ref))
    stress = tuple(jnp.broadcast_to(c, (rows, depth)) for c in load_coeffs(stress_ref))

    def body(i, carry):
        perm, poro = carry

        def tile(sub, count=1):
            at = (i * group + sub) * rows
            return pl.ds(pl.multiple_of(at, count * rows), count * rows)

        def pushed(step, part, sub):
            at = ((step * 2 + part) * events + i * group + sub) * rows
            return forcing[pl.ds(pl.multiple_of(at, rows), rows), :]

        fields = [[state_in[f, tile(sub), :] for f in range(FIELDS)] for sub in range(group)]
        for step in range(steps):
            factors = [[] for _ in range(group)]
            for kind in range(3):
                for sub in range(0, group, 2):
                    both = forward[step * 3 + kind, tile(sub, 2), :].astype(jnp.float32)
                    for half in range(2):
                        value = both[half * rows : (half + 1) * rows]
                        weights[step * 3 + kind, tile(sub + half), :] = value
                        factors[sub + half].append(value)
            for sub, own in enumerate(fields):
                gains = velocity_gain(
                    vel,
                    row_lower(own[SXX]) + depth_lower(own[SXZ]),
                    row_lower(own[SXZ]) + depth_lower(own[SZZ]),
                    row_lower(own[PR]) + vel[3] * own[QX],
                    depth_lower(own[PR]) + vel[3] * own[QZ],
                )
                own[:4] = plus(own[:4], gains)
                own[VX] = own[VX] + pushed(step, 0, sub)
                own[VZ] = own[VZ] + pushed(step, 1, sub)
                perm = perm + own[QX] * factors[sub][0] + own[QZ] * factors[sub][1]
            for sub, own in enumerate(fields):
                own[4:] = plus(
                    own[4:],
                    stress_gain(
                        stress,
                        row_upper(own[VX]),
                        depth_upper(own[VZ]),
                        row_upper(own[QX]) + depth_upper(own[QZ]),
                        depth_upper(own[VX]) + row_upper(own[VZ]),
                    ),
                )
                poro = poro + own[PR] * factors[sub][2]
        for sub, own in enumerate(fields):
            for f in range(FIELDS):
                state[f, tile(sub), :] = own[f]
        return perm, poro

    zero = jnp.zeros((rows, depth), jnp.float32)
    perm, poro = lax.fori_loop(0, events // group, body, (zero, zero))
    sums[pl.ds(0, rows), :] = perm
    sums[pl.ds(rows, rows), :] = poro


def from_before(vel, stress_x, stress_xz, pressure):
    return velocity_gain(vel, -stress_x, -stress_xz, -pressure, 0.0)


def forces(vel, stresses, flows):
    return (
        stresses[0] + depth_lower(stresses[2]),
        stresses[2] + depth_lower(stresses[1]),
        stresses[3] + vel[3] * flows[0],
        depth_lower(stresses[3]) + vel[3] * flows[1],
    )


def strains(stress, vels, after):
    return stress_gain(
        stress,
        after[0] - vels[0],
        depth_upper(vels[1]),
        after[2] - vels[2] + depth_upper(vels[3]),
        depth_upper(vels[0]) + after[1] - vels[1],
    )


NOTHING = (0.0, 0.0, 0.0)


def left_changes(vel, stress, sent, got, factor):
    gain_first = from_before(vel, *got[:3])
    before = beyond_gain(stress, *plus(sent[:3], gain_first[:3]))
    before = plus(got[3:], (before[0], before[2], before[3]))
    stress_first = strains(stress, gain_first, NOTHING)
    vel_first = plus(
        plus(gain_first, velocity_gain(vel, *forces(vel, stress_first, gain_first[2:]))),
        from_before(vel, *before),
    )
    vel_second = from_before(vel, stress_first[0], stress_first[2], stress_first[3])
    end_first = plus(stress_first, strains(stress, vel_first, vel_second))
    end_second = strains(stress, vel_second, NOTHING)
    perm = gain_first[2] * factor(0, 0, 0) + gain_first[3] * factor(0, 1, 0)
    for row, vels in ((0, vel_first), (1, vel_second)):
        perm = perm + vels[2] * factor(1, 0, row) + vels[3] * factor(1, 1, row)
    poro = stress_first[3] * factor(0, 2, 0)
    for row, stresses in ((0, end_first), (1, end_second)):
        poro = poro + stresses[3] * factor(1, 2, row)
    return vel_first + vel_second + end_first + end_second, perm, poro


def right_changes(vel, stress, sent, got, factor, last):
    gain_after = from_before(vel, *sent[:3])
    stress_last = beyond_gain(stress, *plus(got[:3], gain_after[:3]))
    true_last = plus(sent[3:], (stress_last[0], stress_last[2], stress_last[3]))
    vel_last = velocity_gain(
        vel,
        stress_last[0] + depth_lower(stress_last[2]),
        stress_last[2] + depth_lower(stress_last[1]),
        stress_last[3],
        depth_lower(stress_last[3]),
    )
    stress_after = strains(stress, gain_after, NOTHING)
    again = plus(
        plus(gain_after, velocity_gain(vel, *forces(vel, stress_after, gain_after[2:]))),
        from_before(vel, *true_last),
    )
    again = plus(got[3:], again[:3])
    end_inner = beyond_gain(stress, *vel_last[:3])
    end_last = plus(stress_last, strains(stress, vel_last, again))
    perm = vel_last[2] * factor(1, 0, last) + vel_last[3] * factor(1, 1, last)
    poro = stress_last[3] * factor(0, 2, last)
    for row, stresses in ((last - 1, end_inner), (last, end_last)):
        poro = poro + stresses[3] * factor(1, 2, row)
    return vel_last + end_inner + end_last, perm, poro


def left_changes_soon(vel, stress, sent, own_late, got, factor):
    gain_first = from_before(vel, *got[:3])
    beyond = beyond_gain(stress, *plus(sent[:3], gain_first[:3]))
    flow = got[3] + vel[1] * beyond[0] + vel[2] * beyond[3]
    shear = got[4] + beyond[2]
    stress_first = strains(stress, gain_first, NOTHING)
    vel_first = plus(gain_first, velocity_gain(vel, *forces(vel, stress_first, gain_first[2:])))
    vel_first = plus(vel_first, (0.0, -vel[0] * shear, flow, vel[1] * shear))
    vel_second = from_before(vel, stress_first[0], stress_first[2], stress_first[3])
    end_first = plus(stress_first, strains(stress, vel_first, vel_second))
    end_second = strains(stress, vel_second, NOTHING)
    perm = gain_first[2] * factor(0, 0, 0) + gain_first[3] * factor(0, 1, 0)
    for row, vels in ((0, vel_first), (1, vel_second)):
        perm = perm + vels[2] * factor(1, 0, row) + vels[3] * factor(1, 1, row)
    poro = stress_first[3] * factor(0, 2, 0)
    for row, stresses in ((0, end_first), (1, end_second)):
        poro = poro + stresses[3] * factor(1, 2, row)
    rest = (vel[0] * beyond[0] + vel[1] * beyond[3],)
    return vel_first + vel_second + end_first + end_second + rest, perm, poro


def right_changes_soon(vel, stress, sent, own_late, got, factor, last):
    gain_after = from_before(vel, *sent[:3])
    stress_last = beyond_gain(stress, *plus(got[:3], gain_after[:3]))
    true_last = (own_late[0] + stress_last[0], sent[4] + stress_last[2], own_late[1] + stress_last[3])
    vel_last = velocity_gain(
        vel,
        stress_last[0] + depth_lower(stress_last[2]),
        stress_last[2] + depth_lower(stress_last[1]),
        stress_last[3],
        depth_lower(stress_last[3]),
    )
    stress_after = strains(stress, gain_after, NOTHING)
    again = plus(
        plus(gain_after, velocity_gain(vel, *forces(vel, stress_after, gain_after[2:]))),
        from_before(vel, *true_last),
    )
    drain = got[3] + stress[2] * again[0] + stress[3] * again[2]
    end_inner = beyond_gain(stress, *vel_last[:3])
    end_last = plus(stress_last, strains(stress, vel_last, NOTHING))
    perm = vel_last[2] * factor(1, 0, last) + vel_last[3] * factor(1, 1, last)
    poro = stress_last[3] * factor(0, 2, last)
    poro = poro + end_inner[3] * factor(1, 2, last - 1) + (end_last[3] - drain) * factor(1, 2, last)
    poro = poro - stress[2] * (vel[0] * true_last[0] + vel[1] * true_last[2]) * got[4]
    return vel_last + end_inner + end_last + again[:3], perm, poro


def side_sums(sizes, over_chips, weights, sent, own_late, got, vel_ref, stress_ref, changes):
    events, rows, depth, _, _ = sizes
    vel = load_coeffs(vel_ref)
    stress = load_coeffs(stress_ref)
    last = rows - 1
    left, right = sides(over_chips)
    count = SOON if over_chips else HALO

    def fill(changed, partial):
        for chunk in range(0, events, 8):

            def row_of(refs, i):
                each = count // len(refs)
                return refs[i // each][pl.ds(i % each * events + chunk, 8), :]

            def factor(step, kind, row):
                return weights[step * 3 + kind, pl.ds(chunk * rows + row, 8, stride=rows), :]

            own = tuple(row_of(sent, i) for i in range(count))
            new = tuple(row_of(got, i) for i in range(count))
            if over_chips:
                late = tuple(own_late[pl.ds(i * events + chunk, 8), :] for i in range(LATE))
                values, perm, poro = changed(vel, stress, own, late, new, factor)
            else:
                values, perm, poro = changed(vel, stress, own, new, factor)
            for i, value in enumerate(values):
                changes[i, pl.ds(chunk, 8), :] = value
            partial = (partial[0] + perm, partial[1] + poro)
        return partial

    zero = (jnp.zeros((8, depth), jnp.float32),) * 2
    from_left = left_changes_soon if over_chips else left_changes
    from_right = functools.partial(right_changes_soon if over_chips else right_changes, last=last)
    return lax.cond(
        left,
        lambda: fill(from_left, zero),
        lambda: lax.cond(right, lambda: fill(from_right, zero), lambda: zero),
    )


def sides(over_chips):
    place = lax.axis_index("gx")
    odd = lax.rem(place, 2) == 1
    if over_chips:
        return jnp.logical_and(jnp.logical_not(odd), place > 0), jnp.logical_and(
            odd, place < lax.axis_size("gx") - 1
        )
    return odd, jnp.logical_not(odd)


def core_kernel(
    sizes, sums_in, weights, sent_a, sent_b, got_a, got_b, vel_ref, stress_ref, changes, sums
):
    rows = sizes[1]
    sent, got = (sent_a, sent_b), (got_a, got_b)
    perm, poro = side_sums(sizes, False, weights, sent, None, got, vel_ref, stress_ref, changes)
    sums[pl.ds(0, rows), :] = sums_in[pl.ds(0, rows), :] + perm
    sums[pl.ds(rows, rows), :] = sums_in[pl.ds(rows, rows), :] + poro


def chip_kernel(
    sizes, normalizer, sums, weights, sent, late, got, vel_ref, stress_ref, changes, totals
):
    rows = sizes[1]
    vel = load_coeffs(vel_ref)
    stress = load_coeffs(stress_ref)
    perm, poro = side_sums(sizes, True, weights, (sent,), late, (got,), vel_ref, stress_ref, changes)
    perm = jnp.sum(sums[pl.ds(0, rows), :] + perm, axis=0, keepdims=True)
    poro = jnp.sum(sums[pl.ds(rows, rows), :] + poro, axis=0, keepdims=True)
    totals[pl.ds(0, 1), :] = perm * (vel[2] * vel[3] * normalizer)
    totals[pl.ds(1, 1), :] = poro * (stress[3] * normalizer)


def finish_kernel(
    sizes, state_in, changes_core, changes_chip, late, vel_ref, stress_ref, state, out_hbm, done, sems
):
    events, rows, _, _, _ = sizes
    vel = load_coeffs(vel_ref)
    stress = load_coeffs(stress_ref)
    last = rows - 1
    left_places = [(s + f, row) for s in (0, 4) for row in (0, 1) for f in range(4)]
    right_places = [(f, last) for f in range(4)] + [(4 + f, row) for row in (last - 1, last) for f in range(4)]
    got = [late[pl.ds(i * events, events), :] for i in range(LATE)]

    def left_late():
        push = vel[0] * got[0] + vel[1] * got[1] + changes_chip[len(left_places)]
        stresses = stress_gain(stress, push, 0.0, 0.0, depth_upper(-push))
        return {(VX, 0): -push} | {(SXX + f, 0): stresses[f] for f in range(4)}

    def right_late():
        again = [got[i] + changes_chip[len(right_places) + i] for i in range(LATE)]
        stresses = beyond_gain(stress, *again)
        return {(SXX + f, last): stresses[f] for f in range(4)}

    def patch(changes, places, fields, more):
        added = more() if more else {}
        for i, (field, row) in enumerate(places):
            if field in fields:
                at = pl.ds(row, events, stride=rows)
                value = changes[i]
                if (field, row) in added:
                    value = value + added[field, row]
                state[field, at, :] = state_in[field, at, :] + value

    half = FIELDS // 2
    copies = []
    for i in range(2):
        fields = range(i * half, (i + 1) * half)
        for over_chips, changes in ((False, changes_core), (True, changes_chip)):
            left, right = sides(over_chips)
            pl.when(left)(
                functools.partial(patch, changes, left_places, fields, left_late if over_chips else None)
            )
            pl.when(right)(
                functools.partial(patch, changes, right_places, fields, right_late if over_chips else None)
            )
        own = pl.ds(i * half, half)
        copies.append(pltpu.make_async_copy(state.at[own], out_hbm.at[own], sems.at[i]))
        copies[i].start()
    done[...] = jnp.zeros_like(done)
    for copy in copies:
        copy.wait()


def swap_with(value, size, mask):
    return lax.ppermute(value, "gx", [(i, i ^ mask) for i in range(size)])


def swap_over_chips(value, groups, size):
    route = []
    for group in range(groups):
        base = group * size
        other = (group ^ 1) * size
        for i in range(1, size - 1, 2):
            route += [(base + i, base + i + 1), (base + i + 1, base + i)]
        route += [(base, other), (base + size - 1, other + size - 1)]
    return lax.ppermute(value, ("groups", "gx"), route)


def shards(
    adjoint_state, forward_fields, vel_coeffs, stress_coeffs, drm_cells, drm_force, source_id
):
    fields, events, rows, depth = adjoint_state.shape
    steps = forward_fields.shape[0]
    sources = drm_force.shape[0]
    entries = drm_cells.shape[0]
    size = lax.axis_size("gx")
    groups = lax.axis_size("groups")
    sizes = (events, rows, depth, steps, sources)
    blocks = entries // 128
    tiles = events * rows
    f32 = jnp.float32
    any_space = pl.BlockSpec(memory_space=pl.ANY)
    vmem = pl.BlockSpec(memory_space=pltpu.VMEM)
    state = adjoint_state.reshape(fields, tiles, depth)
    forward = forward_fields.reshape(steps * 3, tiles, depth)
    cells = drm_cells.reshape(blocks, 128)
    force = drm_force.reshape(sources * steps, 2, blocks, 128).transpose(0, 2, 1, 3)
    force = force.reshape(sources * steps * 2 * blocks, 128)
    soon = pltpu.VMEM((SOON * events, depth), f32)
    late = pltpu.VMEM((LATE * events, depth), f32)
    half = pltpu.VMEM((HALO // 2 * events, depth), f32)
    limits = pltpu.CompilerParams(vmem_limit_bytes=ROOM)

    def kept(space, *values):
        return tuple(pltpu.with_memory_space_constraint(v, space) for v in values)

    (
        forward,
        source_row,
        table,
        message_first,
        message_second,
        message_chip,
        message_late,
        vel,
        stress,
    ) = pl.pallas_call(
        functools.partial(edge_kernel, sizes),
        out_shape=(
            pltpu.VMEM(forward.shape, forward.dtype),
            pltpu.VMEM((1, events), jnp.int32),
            pltpu.VMEM(force.shape, f32),
            half,
            half,
            soon,
            late,
            pltpu.VMEM(vel_coeffs.shape, f32),
            pltpu.VMEM(stress_coeffs.shape, f32),
        ),
        in_specs=[any_space] * 8,
        out_specs=(vmem,) * 9,
        scratch_shapes=[
            pltpu.VMEM((fields * events, rows, depth), f32),
            pltpu.VMEM((tiles, depth), f32),
            pltpu.VMEM(cells.shape, jnp.int32),
            pltpu.VMEM(force.shape, f32),
            pltpu.VMEM(force.shape, f32),
            pltpu.VMEM((tiles, depth), f32),
            pltpu.SMEM(source_id.shape, jnp.int32),
            pltpu.SemaphoreType.DMA((10,)),
        ],
        compiler_params=limits,
        name="edges",
    )(
        *kept(
            pltpu.HBM,
            state.reshape(fields * events, rows, depth),
            forward,
            vel_coeffs,
            stress_coeffs,
            cells,
            force,
            source_id,
            source_id.reshape(1, events),
        )
    )

    got_first = swap_with(message_first, size, 1)
    got_second = swap_with(message_second, size, 1)
    got_chip = swap_over_chips(message_chip, groups, size)

    state, weights, sums, message_late = pl.pallas_call(
        functools.partial(bulk_kernel, sizes),
        out_shape=(
            pltpu.VMEM(state.shape, f32),
            pltpu.VMEM(forward.shape, f32),
            pltpu.VMEM((2 * rows, depth), f32),
            late,
        ),
        in_specs=[vmem] * 7,
        out_specs=(vmem,) * 4,
        input_output_aliases={6: 3},
        scratch_shapes=[pltpu.VMEM((steps * 2 * tiles, depth), f32)],
        compiler_params=limits,
        cost_estimate=pl.CostEstimate(
            flops=steps * 80 * tiles * depth, bytes_accessed=8 * state.size, transcendentals=0
        ),
        name="bulk",
    )(state, *kept(pltpu.VMEM, forward, source_row, table, vel, stress, message_late))
    got_late = swap_over_chips(message_late, groups, size)

    normalizer = (events * rows * size) ** (-0.5)
    changed = pltpu.VMEM((17, events, depth), f32)
    changes_core, sums = pl.pallas_call(
        functools.partial(core_kernel, sizes),
        out_shape=(changed, pltpu.VMEM(sums.shape, f32)),
        in_specs=[vmem] * 8,
        out_specs=(vmem,) * 2,
        compiler_params=limits,
        name="join_core",
    )(
        *kept(
            pltpu.VMEM,
            sums,
            weights,
            message_first,
            message_second,
            got_first,
            got_second,
            vel,
            stress,
        )
    )

    changes_chip, totals = pl.pallas_call(
        functools.partial(chip_kernel, sizes, normalizer),
        out_shape=(changed, pltpu.VMEM((2, depth), f32)),
        in_specs=[vmem] * 7,
        out_specs=(vmem,) * 2,
        compiler_params=limits,
        name="join_chip",
    )(*kept(pltpu.VMEM, sums, weights, message_chip, message_late, got_chip, vel, stress))

    _, out, done = pl.pallas_call(
        functools.partial(finish_kernel, sizes),
        out_shape=(
            pltpu.VMEM(state.shape, f32),
            jax.ShapeDtypeStruct(state.shape, f32),
            pltpu.VMEM((2, depth), f32),
        ),
        in_specs=[vmem] * 6,
        out_specs=(vmem, any_space, vmem),
        input_output_aliases={0: 0},
        scratch_shapes=[pltpu.SemaphoreType.DMA((2,))],
        compiler_params=limits,
        cost_estimate=pl.CostEstimate(flops=0, bytes_accessed=2 * 4 * state.size, transcendentals=0),
        name="finish",
    )(*kept(pltpu.VMEM, state, changes_core, changes_chip, got_late, vel, stress))

    mask = 1
    while mask < size:
        totals = totals + swap_with(totals, size, mask | 1)
        if mask * 4 == size:
            totals = totals + done
        mask *= 2
    return out.reshape(adjoint_state.shape), totals


def solution(mesh):
    in_specs = (
        P(None, "groups", "gx", None),
        P(None, None, "groups", "gx", None),
        P("groups", None),
        P("groups", None),
        P("gx"),
        P("groups", None, None, "gx"),
        P("groups"),
    )
    out_specs = (P(None, "groups", "gx", None), P("groups", None))
    return jax.shard_map(shards, mesh=mesh, in_specs=in_specs, out_specs=out_specs, check_vma=False)
```

```python
import functools

import jax
import jax.numpy as jnp
from jax import lax
from jax.experimental import pallas as pl
from jax.experimental.pallas import tpu as pltpu
from jax.sharding import PartitionSpec as P

LAYER = 8
FIELDS = 8
VX, VZ, QX, QZ, SXX, SZZ, SXZ, PR = range(FIELDS)
HALO = 6
SOON = 5
LATE = 3
PUSHED = ((0, 0), (0, 1), (1, 0), (0, -1))
GROUPS = (16, 8, 4, 2)
ROOM = 16 << 20


def depth_lower(values):
    lane = lax.broadcasted_iota(jnp.int32, values.shape, 1)
    return values - jnp.where(lane == 0, 0.0, pltpu.roll(values, 1, 1))


def depth_upper(values):
    depth = values.shape[1]
    lane = lax.broadcasted_iota(jnp.int32, values.shape, 1)
    return jnp.where(lane == depth - 1, 0.0, pltpu.roll(values, depth - 1, 1)) - values


def row_lower(values):
    row = lax.broadcasted_iota(jnp.int32, values.shape, 0)
    return values - jnp.where(row == 0, 0.0, pltpu.roll(values, 1, 0))


def row_upper(values):
    rows = values.shape[0]
    row = lax.broadcasted_iota(jnp.int32, values.shape, 0)
    return jnp.where(row == rows - 1, 0.0, pltpu.roll(values, rows - 1, 0)) - values


def velocity_gain(coeffs, force_x, force_z, push_x, push_z):
    solid, couple, fluid, _ = coeffs
    return (
        solid * force_x + couple * push_x,
        solid * force_z + couple * push_z,
        -couple * force_x - fluid * push_x,
        -couple * force_z - fluid * push_z,
    )


def stress_gain(coeffs, strain_x, strain_z, inflow, shear):
    lame, modulus, coupling, fluid = coeffs
    dilation = strain_x + strain_z
    common = lame * dilation - coupling * inflow
    return (
        common + 2.0 * modulus * strain_x,
        common + 2.0 * modulus * strain_z,
        modulus * shear,
        -coupling * dilation - fluid * inflow,
    )


def beyond_gain(coeffs, vel_x, vel_z, flow_x):
    lame, modulus, coupling, fluid = coeffs
    return (
        (lame + 2.0 * modulus) * vel_x - coupling * flow_x,
        lame * vel_x - coupling * flow_x,
        modulus * vel_z,
        -coupling * vel_x - fluid * flow_x,
    )


def plus(left, right):
    return tuple(a + b for a, b in zip(left, right))


def minus(left, right):
    return tuple(a - b for a, b in zip(left, right))


def load_coeffs(ref):
    return tuple(ref[pl.ds(i, 1), :] for i in range(4))


def at_row(layers, row, depth):
    lane = lax.broadcasted_iota(jnp.int32, layers.shape, 1)
    moved = pltpu.roll(layers, (depth - LAYER - LAYER * row) % depth, 1)
    return jnp.where(lane >= depth - LAYER, moved, 0.0)


def exact_pieces(values):
    pieces = []
    for _ in range(3):
        pieces.append(values.astype(jnp.bfloat16))
        values = values - pieces[-1].astype(jnp.float32)
    return pieces


def edge_kernel(
    sizes,
    state_hbm,
    forward_hbm,
    vel_hbm,
    stress_hbm,
    cells_hbm,
    force_hbm,
    source_hbm,
    forward,
    source,
    table_ref,
    message_first,
    message_second,
    message_chip,
    message_late,
    vel_ref,
    stress_ref,
    near,
    weights,
    cells,
    force,
    near_force,
    pushes,
    sems,
):
    events, rows, depth, steps, sources = sizes
    final_kind = steps * 3 - 1
    copies = [
        pltpu.make_async_copy(src, dst, sems.at[i])
        for i, (src, dst) in enumerate(
            [
                (cells_hbm, cells),
                (force_hbm, force),
                (source_hbm, source),
                (vel_hbm, vel_ref),
                (stress_hbm, stress_ref),
                (state_hbm.at[:, pl.ds(0, 2)], near.at[:, pl.ds(0, 2)]),
                (state_hbm.at[:, pl.ds(rows - 2, 2)], near.at[:, pl.ds(rows - 2, 2)]),
                (forward_hbm.at[pl.ds(final_kind, 1)], forward.at[pl.ds(final_kind, 1)]),
                (forward_hbm.at[pl.ds(0, final_kind)], forward.at[pl.ds(0, final_kind)]),
            ]
        )
    ]
    for copy in copies:
        copy.start()
    copies[0].wait()
    copies[1].wait()
    lanes = cells.shape[1]
    local = cells[...] & (rows * depth - 1)
    slot = (local // depth) * LAYER + (local & (depth - 1)) - (depth - LAYER)
    blocks = cells.shape[0]
    spots = lax.broadcasted_iota(jnp.int32, (depth, lanes), 0)
    hits = [(spots == slot[i : i + 1, :]).astype(jnp.float32).astype(jnp.bfloat16) for i in range(blocks)]
    pieces = exact_pieces(force[...])
    terms = [
        lax.dot_general(
            jnp.concatenate(pieces, axis=0),
            hit,
            (((1,), (1,)), ((), ())),
            preferred_element_type=jnp.float32,
        )
        for hit in hits
    ]
    count = force.shape[0]
    terms = [t[:count] + t[count : 2 * count] + t[2 * count :] for t in terms]
    layers = terms[0]
    for block in range(1, blocks):
        layers = layers + pltpu.roll(terms[block], count - 2 * block, 0)
    table_ref[...] = layers
    def moved(row):
        return at_row(layers, row, depth)

    own = lax.broadcasted_iota(jnp.int32, layers.shape, 0) & (rows - 1)
    picked = jnp.where(own < 6, pltpu.roll(moved(1), 2, 0), pltpu.roll(moved(rows - 1), 6, 0))
    near_force[...] = jnp.where((own & 2) == 0, moved(0), picked)
    copies[2].wait()
    for event in range(events):
        record = pl.multiple_of(source[event] * rows, rows)
        pushes[pl.ds(event * rows, rows), :] = near_force[pl.ds(record, rows), :]
    for copy in copies[3:-1]:
        copy.wait()
    weights[...] = forward[final_kind].astype(jnp.float32)
    vel = load_coeffs(vel_ref)
    stress = load_coeffs(stress_ref)
    odd = lax.rem(lax.axis_index("gx"), 2) == 1
    message_core = (message_first, message_second)
    last = rows - 1
    state = near.reshape(near.shape[0] * rows, depth)

    def rim(chunk, field, row):
        return state[pl.ds((field * events + chunk) * rows + row, 8, stride=rows), :]

    def pushed(chunk, step, part, row):
        at = PUSHED.index((step, row if row < last else -1)) * 2 + part
        return pushes[pl.ds(chunk * rows + at, 8, stride=rows), :]

    for chunk in range(0, events, 8):
        first = [rim(chunk, f, 0) for f in range(FIELDS)]
        second = [rim(chunk, f, 1) for f in range(FIELDS)]
        final = [rim(chunk, f, last) for f in range(FIELDS)]
        inner = {f: rim(chunk, f, last - 1) for f in (SXX, SXZ, PR)}

        def kicked(fields, gains, step, row):
            vel_x, vel_z, flow_x, flow_z = plus(fields, gains)
            return (
                vel_x + pushed(chunk, step, 0, row),
                vel_z + pushed(chunk, step, 1, row),
                flow_x,
                flow_z,
            )

        def forces(fields, before):
            return (
                fields[SXX] - before[SXX] + depth_lower(fields[SXZ]),
                fields[SXZ] - before[SXZ] + depth_lower(fields[SZZ]),
                fields[PR] - before[PR] + vel[3] * fields[QX],
                depth_lower(fields[PR]) + vel[3] * fields[QZ],
            )

        nothing = {SXX: 0.0, SXZ: 0.0, PR: 0.0}
        vel_first = kicked(first[:4], velocity_gain(vel, *forces(first, nothing)), 0, 0)
        vel_second = kicked(second[:4], velocity_gain(vel, *forces(second, first)), 0, 1)
        vel_final = kicked(final[:4], velocity_gain(vel, *forces(final, inner)), 0, last)
        stress_first = plus(
            first[4:],
            stress_gain(
                stress,
                vel_second[0] - vel_first[0],
                depth_upper(vel_first[1]),
                vel_second[2] - vel_first[2] + depth_upper(vel_first[3]),
                depth_upper(vel_first[0]) + vel_second[1] - vel_first[1],
            ),
        )
        stress_final = plus(
            final[4:],
            stress_gain(
                stress,
                -vel_final[0],
                depth_upper(vel_final[1]),
                -vel_final[2] + depth_upper(vel_final[3]),
                depth_upper(vel_final[0]) - vel_final[1],
            ),
        )
        again = kicked(
            vel_first,
            velocity_gain(vel, *forces(list(vel_first) + list(stress_first), nothing)),
            1,
            0,
        )
        right = [final[SXX], final[SXZ], final[PR], stress_final[0], stress_final[2], stress_final[3]]
        left = [vel_first[0], vel_first[1], vel_first[2], again[0], again[1], again[2]]
        for i in range(HALO):
            half = message_core[i // 3]
            half[pl.ds(i % 3 * events + chunk, 8), :] = jnp.where(odd, left[i], right[i])
        flow = vel[1] * stress_final[0] + vel[2] * stress_final[3]
        drain = stress[2] * again[0] + stress[3] * again[2]
        weight = weights[pl.ds(chunk * rows, 8, stride=rows), :]
        right_soon = right[:3] + [flow, stress_final[2]]
        left_soon = left[:3] + [drain, weight]
        right_late = [stress_final[0], stress_final[3], stress_final[3]]
        for i in range(SOON):
            message_chip[pl.ds(i * events + chunk, 8), :] = jnp.where(odd, right_soon[i], left_soon[i])
        for i in range(LATE):
            message_late[pl.ds(i * events + chunk, 8), :] = jnp.where(odd, right_late[i], left[3 + i])
    copies[-1].wait()


def group_of(events):
    return next(g for g in GROUPS if events % g == 0)


def bulk_kernel(
    sizes,
    state_in,
    forward,
    source,
    table_ref,
    vel_ref,
    stress_ref,
    late_in,
    state,
    weights,
    sums,
    late,
    by_source,
):
    events, rows, depth, steps, sources = sizes
    group = group_of(events)
    each = table_ref.shape[0] // sources
    for step in range(steps):
        for part in range(2):
            layers = table_ref[pl.ds(step * (each // steps) + part, sources, stride=each), :]
            for row in range(rows):
                at = (step * 2 + part) * sources * rows + row
                by_source[pl.ds(at, sources, stride=rows), :] = at_row(layers, row, depth)
    vel = tuple(jnp.broadcast_to(c, (rows, depth)) for c in load_coeffs(vel_ref))
    stress = tuple(jnp.broadcast_to(c, (rows, depth)) for c in load_coeffs(stress_ref))

    def body(i, carry):
        perm, poro = carry

        def tile(sub, count=1):
            at = (i * group + sub) * rows
            return pl.ds(pl.multiple_of(at, count * rows), count * rows)

        def pushed(step, part, sub):
            at = ((step * 2 + part) * sources + source[i * group + sub]) * rows
            return by_source[pl.ds(pl.multiple_of(at, rows), rows), :]

        fields = [[state_in[f, tile(sub), :] for f in range(FIELDS)] for sub in range(group)]
        for step in range(steps):
            factors = [[] for _ in range(group)]
            for kind in range(3):
                for sub in range(0, group, 2):
                    both = forward[step * 3 + kind, tile(sub, 2), :].astype(jnp.float32)
                    for half in range(2):
                        value = both[half * rows : (half + 1) * rows]
                        weights[step * 3 + kind, tile(sub + half), :] = value
                        factors[sub + half].append(value)
            for sub, own in enumerate(fields):
                gains = velocity_gain(
                    vel,
                    row_lower(own[SXX]) + depth_lower(own[SXZ]),
                    row_lower(own[SXZ]) + depth_lower(own[SZZ]),
                    row_lower(own[PR]) + vel[3] * own[QX],
                    depth_lower(own[PR]) + vel[3] * own[QZ],
                )
                own[:4] = plus(own[:4], gains)
                own[VX] = own[VX] + pushed(step, 0, sub)
                own[VZ] = own[VZ] + pushed(step, 1, sub)
                perm = perm + own[QX] * factors[sub][0] + own[QZ] * factors[sub][1]
            for sub, own in enumerate(fields):
                own[4:] = plus(
                    own[4:],
                    stress_gain(
                        stress,
                        row_upper(own[VX]),
                        depth_upper(own[VZ]),
                        row_upper(own[QX]) + depth_upper(own[QZ]),
                        depth_upper(own[VX]) + row_upper(own[VZ]),
                    ),
                )
                poro = poro + own[PR] * factors[sub][2]
        for sub, own in enumerate(fields):
            for f in range(FIELDS):
                state[f, tile(sub), :] = own[f]
        return perm, poro

    zero = jnp.zeros((rows, depth), jnp.float32)
    perm, poro = lax.fori_loop(0, events // group, body, (zero, zero))
    sums[pl.ds(0, rows), :] = perm
    sums[pl.ds(rows, rows), :] = poro


def from_before(vel, stress_x, stress_xz, pressure):
    return velocity_gain(vel, -stress_x, -stress_xz, -pressure, 0.0)


def forces(vel, stresses, flows):
    return (
        stresses[0] + depth_lower(stresses[2]),
        stresses[2] + depth_lower(stresses[1]),
        stresses[3] + vel[3] * flows[0],
        depth_lower(stresses[3]) + vel[3] * flows[1],
    )


def strains(stress, vels, after):
    return stress_gain(
        stress,
        after[0] - vels[0],
        depth_upper(vels[1]),
        after[2] - vels[2] + depth_upper(vels[3]),
        depth_upper(vels[0]) + after[1] - vels[1],
    )


NOTHING = (0.0, 0.0, 0.0)


def left_changes(vel, stress, sent, got, factor):
    gain_first = from_before(vel, *got[:3])
    before = beyond_gain(stress, *plus(sent[:3], gain_first[:3]))
    before = plus(got[3:], (before[0], before[2], before[3]))
    stress_first = strains(stress, gain_first, NOTHING)
    vel_first = plus(
        plus(gain_first, velocity_gain(vel, *forces(vel, stress_first, gain_first[2:]))),
        from_before(vel, *before),
    )
    vel_second = from_before(vel, stress_first[0], stress_first[2], stress_first[3])
    end_first = plus(stress_first, strains(stress, vel_first, vel_second))
    end_second = strains(stress, vel_second, NOTHING)
    perm = gain_first[2] * factor(0, 0, 0) + gain_first[3] * factor(0, 1, 0)
    for row, vels in ((0, vel_first), (1, vel_second)):
        perm = perm + vels[2] * factor(1, 0, row) + vels[3] * factor(1, 1, row)
    poro = stress_first[3] * factor(0, 2, 0)
    for row, stresses in ((0, end_first), (1, end_second)):
        poro = poro + stresses[3] * factor(1, 2, row)
    return vel_first + vel_second + end_first + end_second, perm, poro


def right_changes(vel, stress, sent, got, factor, last):
    gain_after = from_before(vel, *sent[:3])
    stress_last = beyond_gain(stress, *plus(got[:3], gain_after[:3]))
    true_last = plus(sent[3:], (stress_last[0], stress_last[2], stress_last[3]))
    vel_last = velocity_gain(
        vel,
        stress_last[0] + depth_lower(stress_last[2]),
        stress_last[2] + depth_lower(stress_last[1]),
        stress_last[3],
        depth_lower(stress_last[3]),
    )
    stress_after = strains(stress, gain_after, NOTHING)
    again = plus(
        plus(gain_after, velocity_gain(vel, *forces(vel, stress_after, gain_after[2:]))),
        from_before(vel, *true_last),
    )
    again = plus(got[3:], again[:3])
    end_inner = beyond_gain(stress, *vel_last[:3])
    end_last = plus(stress_last, strains(stress, vel_last, again))
    perm = vel_last[2] * factor(1, 0, last) + vel_last[3] * factor(1, 1, last)
    poro = stress_last[3] * factor(0, 2, last)
    for row, stresses in ((last - 1, end_inner), (last, end_last)):
        poro = poro + stresses[3] * factor(1, 2, row)
    return vel_last + end_inner + end_last, perm, poro


def left_changes_soon(vel, stress, sent, own_late, got, factor):
    gain_first = from_before(vel, *got[:3])
    beyond = beyond_gain(stress, *plus(sent[:3], gain_first[:3]))
    flow = got[3] + vel[1] * beyond[0] + vel[2] * beyond[3]
    shear = got[4] + beyond[2]
    stress_first = strains(stress, gain_first, NOTHING)
    vel_first = plus(gain_first, velocity_gain(vel, *forces(vel, stress_first, gain_first[2:])))
    vel_first = plus(vel_first, (0.0, -vel[0] * shear, flow, vel[1] * shear))
    vel_second = from_before(vel, stress_first[0], stress_first[2], stress_first[3])
    end_first = plus(stress_first, strains(stress, vel_first, vel_second))
    end_second = strains(stress, vel_second, NOTHING)
    perm = gain_first[2] * factor(0, 0, 0) + gain_first[3] * factor(0, 1, 0)
    for row, vels in ((0, vel_first), (1, vel_second)):
        perm = perm + vels[2] * factor(1, 0, row) + vels[3] * factor(1, 1, row)
    poro = stress_first[3] * factor(0, 2, 0)
    for row, stresses in ((0, end_first), (1, end_second)):
        poro = poro + stresses[3] * factor(1, 2, row)
    rest = (vel[0] * beyond[0] + vel[1] * beyond[3],)
    return vel_first + vel_second + end_first + end_second + rest, perm, poro


def right_changes_soon(vel, stress, sent, own_late, got, factor, last):
    gain_after = from_before(vel, *sent[:3])
    stress_last = beyond_gain(stress, *plus(got[:3], gain_after[:3]))
    true_last = (own_late[0] + stress_last[0], sent[4] + stress_last[2], own_late[1] + stress_last[3])
    vel_last = velocity_gain(
        vel,
        stress_last[0] + depth_lower(stress_last[2]),
        stress_last[2] + depth_lower(stress_last[1]),
        stress_last[3],
        depth_lower(stress_last[3]),
    )
    stress_after = strains(stress, gain_after, NOTHING)
    again = plus(
        plus(gain_after, velocity_gain(vel, *forces(vel, stress_after, gain_after[2:]))),
        from_before(vel, *true_last),
    )
    drain = got[3] + stress[2] * again[0] + stress[3] * again[2]
    end_inner = beyond_gain(stress, *vel_last[:3])
    end_last = plus(stress_last, strains(stress, vel_last, NOTHING))
    perm = vel_last[2] * factor(1, 0, last) + vel_last[3] * factor(1, 1, last)
    poro = stress_last[3] * factor(0, 2, last)
    poro = poro + end_inner[3] * factor(1, 2, last - 1) + (end_last[3] - drain) * factor(1, 2, last)
    poro = poro - stress[2] * (vel[0] * true_last[0] + vel[1] * true_last[2]) * got[4]
    return vel_last + end_inner + end_last + again[:3], perm, poro


def side_sums(sizes, over_chips, weights, sent, own_late, got, vel_ref, stress_ref, changes):
    events, rows, depth, _, _ = sizes
    vel = load_coeffs(vel_ref)
    stress = load_coeffs(stress_ref)
    last = rows - 1
    left, right = sides(over_chips)
    count = SOON if over_chips else HALO

    def fill(changed, partial):
        for chunk in range(0, events, 8):

            def row_of(refs, i):
                each = count // len(refs)
                return refs[i // each][pl.ds(i % each * events + chunk, 8), :]

            def factor(step, kind, row):
                return weights[step * 3 + kind, pl.ds(chunk * rows + row, 8, stride=rows), :]

            own = tuple(row_of(sent, i) for i in range(count))
            new = tuple(row_of(got, i) for i in range(count))
            if over_chips:
                late = tuple(own_late[pl.ds(i * events + chunk, 8), :] for i in range(LATE))
                values, perm, poro = changed(vel, stress, own, late, new, factor)
            else:
                values, perm, poro = changed(vel, stress, own, new, factor)
            for i, value in enumerate(values):
                changes[i, pl.ds(chunk, 8), :] = value
            partial = (partial[0] + perm, partial[1] + poro)
        return partial

    zero = (jnp.zeros((8, depth), jnp.float32),) * 2
    from_left = left_changes_soon if over_chips else left_changes
    from_right = functools.partial(right_changes_soon if over_chips else right_changes, last=last)
    return lax.cond(
        left,
        lambda: fill(from_left, zero),
        lambda: lax.cond(right, lambda: fill(from_right, zero), lambda: zero),
    )


def sides(over_chips):
    place = lax.axis_index("gx")
    odd = lax.rem(place, 2) == 1
    if over_chips:
        return jnp.logical_and(jnp.logical_not(odd), place > 0), jnp.logical_and(
            odd, place < lax.axis_size("gx") - 1
        )
    return odd, jnp.logical_not(odd)


def core_kernel(
    sizes, sums_in, weights, sent_a, sent_b, got_a, got_b, vel_ref, stress_ref, changes, sums
):
    rows = sizes[1]
    sent, got = (sent_a, sent_b), (got_a, got_b)
    perm, poro = side_sums(sizes, False, weights, sent, None, got, vel_ref, stress_ref, changes)
    sums[pl.ds(0, rows), :] = sums_in[pl.ds(0, rows), :] + perm
    sums[pl.ds(rows, rows), :] = sums_in[pl.ds(rows, rows), :] + poro


def chip_kernel(
    sizes, normalizer, sums, weights, sent, late, got, vel_ref, stress_ref, changes, totals
):
    rows = sizes[1]
    vel = load_coeffs(vel_ref)
    stress = load_coeffs(stress_ref)
    perm, poro = side_sums(sizes, True, weights, (sent,), late, (got,), vel_ref, stress_ref, changes)
    perm = jnp.sum(sums[pl.ds(0, rows), :] + perm, axis=0, keepdims=True)
    poro = jnp.sum(sums[pl.ds(rows, rows), :] + poro, axis=0, keepdims=True)
    totals[pl.ds(0, 1), :] = perm * (vel[2] * vel[3] * normalizer)
    totals[pl.ds(1, 1), :] = poro * (stress[3] * normalizer)


def finish_kernel(
    sizes, state_in, changes_core, changes_chip, late, vel_ref, stress_ref, state, out_hbm, done, sems
):
    events, rows, _, _, _ = sizes
    vel = load_coeffs(vel_ref)
    stress = load_coeffs(stress_ref)
    last = rows - 1
    left_places = [(s + f, row) for s in (0, 4) for row in (0, 1) for f in range(4)]
    right_places = [(f, last) for f in range(4)] + [(4 + f, row) for row in (last - 1, last) for f in range(4)]
    got = [late[pl.ds(i * events, events), :] for i in range(LATE)]

    def left_late():
        push = vel[0] * got[0] + vel[1] * got[1] + changes_chip[len(left_places)]
        stresses = stress_gain(stress, push, 0.0, 0.0, depth_upper(-push))
        return {(VX, 0): -push} | {(SXX + f, 0): stresses[f] for f in range(4)}

    def right_late():
        again = [got[i] + changes_chip[len(right_places) + i] for i in range(LATE)]
        stresses = beyond_gain(stress, *again)
        return {(SXX + f, last): stresses[f] for f in range(4)}

    def patch(changes, places, fields, more):
        added = more() if more else {}
        for i, (field, row) in enumerate(places):
            if field in fields:
                at = pl.ds(row, events, stride=rows)
                value = changes[i]
                if (field, row) in added:
                    value = value + added[field, row]
                state[field, at, :] = state_in[field, at, :] + value

    half = FIELDS // 2
    copies = []
    for i in range(2):
        fields = range(i * half, (i + 1) * half)
        for over_chips, changes in ((False, changes_core), (True, changes_chip)):
            left, right = sides(over_chips)
            pl.when(left)(
                functools.partial(patch, changes, left_places, fields, left_late if over_chips else None)
            )
            pl.when(right)(
                functools.partial(patch, changes, right_places, fields, right_late if over_chips else None)
            )
        own = pl.ds(i * half, half)
        copies.append(pltpu.make_async_copy(state.at[own], out_hbm.at[own], sems.at[i]))
        copies[i].start()
    done[...] = jnp.zeros_like(done)
    for copy in copies:
        copy.wait()


def swap_with(value, size, mask):
    return lax.ppermute(value, "gx", [(i, i ^ mask) for i in range(size)])


def swap_over_chips(value, groups, size):
    route = []
    for group in range(groups):
        base = group * size
        other = (group ^ 1) * size
        for i in range(1, size - 1, 2):
            route += [(base + i, base + i + 1), (base + i + 1, base + i)]
        route += [(base, other), (base + size - 1, other + size - 1)]
    return lax.ppermute(value, ("groups", "gx"), route)


def shards(
    adjoint_state, forward_fields, vel_coeffs, stress_coeffs, drm_cells, drm_force, source_id
):
    fields, events, rows, depth = adjoint_state.shape
    steps = forward_fields.shape[0]
    sources = drm_force.shape[0]
    entries = drm_cells.shape[0]
    size = lax.axis_size("gx")
    groups = lax.axis_size("groups")
    sizes = (events, rows, depth, steps, sources)
    blocks = entries // 128
    tiles = events * rows
    f32 = jnp.float32
    any_space = pl.BlockSpec(memory_space=pl.ANY)
    vmem = pl.BlockSpec(memory_space=pltpu.VMEM)
    smem = pl.BlockSpec(memory_space=pltpu.SMEM)
    state = adjoint_state.reshape(fields, tiles, depth)
    forward = forward_fields.reshape(steps * 3, tiles, depth)
    cells = drm_cells.reshape(blocks, 128)
    force = drm_force.reshape(sources * steps, 2, blocks, 128).transpose(0, 2, 1, 3)
    force = force.reshape(sources * steps * 2 * blocks, 128)
    soon = pltpu.VMEM((SOON * events, depth), f32)
    late = pltpu.VMEM((LATE * events, depth), f32)
    half = pltpu.VMEM((HALO // 2 * events, depth), f32)
    limits = pltpu.CompilerParams(vmem_limit_bytes=ROOM)

    def kept(space, *values):
        return tuple(pltpu.with_memory_space_constraint(v, space) for v in values)

    (
        forward,
        source,
        table,
        message_first,
        message_second,
        message_chip,
        message_late,
        vel,
        stress,
    ) = pl.pallas_call(
        functools.partial(edge_kernel, sizes),
        out_shape=(
            pltpu.VMEM(forward.shape, forward.dtype),
            pltpu.SMEM((events,), jnp.int32),
            pltpu.VMEM(force.shape, f32),
            half,
            half,
            soon,
            late,
            pltpu.VMEM(vel_coeffs.shape, f32),
            pltpu.VMEM(stress_coeffs.shape, f32),
        ),
        in_specs=[any_space] * 7,
        out_specs=(vmem, smem) + (vmem,) * 7,
        scratch_shapes=[
            pltpu.VMEM((fields * events, rows, depth), f32),
            pltpu.VMEM((tiles, depth), f32),
            pltpu.VMEM(cells.shape, jnp.int32),
            pltpu.VMEM(force.shape, f32),
            pltpu.VMEM(force.shape, f32),
            pltpu.VMEM((tiles, depth), f32),
            pltpu.SemaphoreType.DMA((9,)),
        ],
        compiler_params=limits,
        name="edges",
    )(
        *kept(
            pltpu.HBM,
            state.reshape(fields * events, rows, depth),
            forward,
            vel_coeffs,
            stress_coeffs,
            cells,
            force,
            source_id,
        )
    )

    got_first = swap_with(message_first, size, 1)
    got_second = swap_with(message_second, size, 1)
    got_chip = swap_over_chips(message_chip, groups, size)

    state, weights, sums, message_late = pl.pallas_call(
        functools.partial(bulk_kernel, sizes),
        out_shape=(
            pltpu.VMEM(state.shape, f32),
            pltpu.VMEM(forward.shape, f32),
            pltpu.VMEM((2 * rows, depth), f32),
            late,
        ),
        in_specs=[vmem] * 2 + [smem] + [vmem] * 4,
        out_specs=(vmem,) * 4,
        input_output_aliases={6: 3},
        scratch_shapes=[pltpu.VMEM((steps * 2 * sources * rows, depth), f32)],
        compiler_params=limits,
        cost_estimate=pl.CostEstimate(
            flops=steps * 80 * tiles * depth, bytes_accessed=8 * state.size, transcendentals=0
        ),
        name="bulk",
    )(
        state,
        *kept(pltpu.VMEM, forward),
        *kept(pltpu.SMEM, source),
        *kept(pltpu.VMEM, table, vel, stress, message_late),
    )
    got_late = swap_over_chips(message_late, groups, size)

    normalizer = (events * rows * size) ** (-0.5)
    changed = pltpu.VMEM((17, events, depth), f32)
    changes_core, sums = pl.pallas_call(
        functools.partial(core_kernel, sizes),
        out_shape=(changed, pltpu.VMEM(sums.shape, f32)),
        in_specs=[vmem] * 8,
        out_specs=(vmem,) * 2,
        compiler_params=limits,
        name="join_core",
    )(
        *kept(
            pltpu.VMEM,
            sums,
            weights,
            message_first,
            message_second,
            got_first,
            got_second,
            vel,
            stress,
        )
    )

    changes_chip, totals = pl.pallas_call(
        functools.partial(chip_kernel, sizes, normalizer),
        out_shape=(changed, pltpu.VMEM((2, depth), f32)),
        in_specs=[vmem] * 7,
        out_specs=(vmem,) * 2,
        compiler_params=limits,
        name="join_chip",
    )(*kept(pltpu.VMEM, sums, weights, message_chip, message_late, got_chip, vel, stress))

    _, out, done = pl.pallas_call(
        functools.partial(finish_kernel, sizes),
        out_shape=(
            pltpu.VMEM(state.shape, f32),
            jax.ShapeDtypeStruct(state.shape, f32),
            pltpu.VMEM((2, depth), f32),
        ),
        in_specs=[vmem] * 6,
        out_specs=(vmem, any_space, vmem),
        input_output_aliases={0: 0},
        scratch_shapes=[pltpu.SemaphoreType.DMA((2,))],
        compiler_params=limits,
        cost_estimate=pl.CostEstimate(flops=0, bytes_accessed=2 * 4 * state.size, transcendentals=0),
        name="finish",
    )(*kept(pltpu.VMEM, state, changes_core, changes_chip, got_late, vel, stress))

    mask = 1
    while mask < size:
        totals = totals + swap_with(totals, size, mask | 1)
        if mask * 4 == size:
            totals = totals + done
        mask *= 2
    return out.reshape(adjoint_state.shape), totals


def solution(mesh):
    in_specs = (
        P(None, "groups", "gx", None),
        P(None, None, "groups", "gx", None),
        P("groups", None),
        P("groups", None),
        P("gx"),
        P("groups", None, None, "gx"),
        P("groups"),
    )
    out_specs = (P(None, "groups", "gx", None), P("groups", None))
    return jax.shard_map(shards, mesh=mesh, in_specs=in_specs, out_specs=out_specs, check_vma=False)
```

```python
import functools

import jax
import jax.numpy as jnp
from jax import lax
from jax.experimental import pallas as pl
from jax.experimental.pallas import tpu as pltpu
from jax.sharding import PartitionSpec as P

LAYER = 8
FIELDS = 8
VX, VZ, QX, QZ, SXX, SZZ, SXZ, PR = range(FIELDS)
HALO = 6
SOON = 5
LATE = 3
PUSHED = ((0, 0), (0, 1), (1, 0), (0, -1))
GROUPS = (16, 8, 4, 2)
ROOM = 16 << 20


def depth_lower(values):
    lane = lax.broadcasted_iota(jnp.int32, values.shape, 1)
    return values - jnp.where(lane == 0, 0.0, pltpu.roll(values, 1, 1))


def depth_upper(values):
    depth = values.shape[1]
    lane = lax.broadcasted_iota(jnp.int32, values.shape, 1)
    return jnp.where(lane == depth - 1, 0.0, pltpu.roll(values, depth - 1, 1)) - values


def row_lower(values):
    row = lax.broadcasted_iota(jnp.int32, values.shape, 0)
    return values - jnp.where(row == 0, 0.0, pltpu.roll(values, 1, 0))


def row_upper(values):
    rows = values.shape[0]
    row = lax.broadcasted_iota(jnp.int32, values.shape, 0)
    return jnp.where(row == rows - 1, 0.0, pltpu.roll(values, rows - 1, 0)) - values


def velocity_gain(coeffs, force_x, force_z, push_x, push_z):
    solid, couple, fluid, _ = coeffs
    return (
        solid * force_x + couple * push_x,
        solid * force_z + couple * push_z,
        -couple * force_x - fluid * push_x,
        -couple * force_z - fluid * push_z,
    )


def stress_gain(coeffs, strain_x, strain_z, inflow, shear):
    lame, modulus, coupling, fluid = coeffs
    dilation = strain_x + strain_z
    common = lame * dilation - coupling * inflow
    return (
        common + 2.0 * modulus * strain_x,
        common + 2.0 * modulus * strain_z,
        modulus * shear,
        -coupling * dilation - fluid * inflow,
    )


def beyond_gain(coeffs, vel_x, vel_z, flow_x):
    lame, modulus, coupling, fluid = coeffs
    return (
        (lame + 2.0 * modulus) * vel_x - coupling * flow_x,
        lame * vel_x - coupling * flow_x,
        modulus * vel_z,
        -coupling * vel_x - fluid * flow_x,
    )


def plus(left, right):
    return tuple(a + b for a, b in zip(left, right))


def minus(left, right):
    return tuple(a - b for a, b in zip(left, right))


def load_coeffs(ref):
    return tuple(ref[pl.ds(i, 1), :] for i in range(4))


def at_row(layers, row, depth):
    lane = lax.broadcasted_iota(jnp.int32, layers.shape, 1)
    moved = pltpu.roll(layers, (depth - LAYER - LAYER * row) % depth, 1)
    return jnp.where(lane >= depth - LAYER, moved, 0.0)


def exact_pieces(values):
    pieces = []
    for _ in range(3):
        pieces.append(values.astype(jnp.bfloat16))
        values = values - pieces[-1].astype(jnp.float32)
    return pieces


def edge_kernel(
    sizes,
    state_hbm,
    forward_hbm,
    vel_hbm,
    stress_hbm,
    cells_hbm,
    force_hbm,
    source_hbm,
    near,
    forward,
    source,
    table_ref,
    message_first,
    message_second,
    message_chip,
    message_late,
    vel_ref,
    stress_ref,
    weights,
    cells,
    force,
    near_force,
    pushes,
    sems,
):
    events, rows, depth, steps, sources = sizes
    final_kind = steps * 3 - 1
    copies = [
        pltpu.make_async_copy(src, dst, sems.at[i])
        for i, (src, dst) in enumerate(
            [
                (cells_hbm, cells),
                (force_hbm, force),
                (source_hbm, source),
                (vel_hbm, vel_ref),
                (stress_hbm, stress_ref),
                (state_hbm.at[:, pl.ds(0, 2)], near.at[:, pl.ds(0, 2)]),
                (state_hbm.at[:, pl.ds(rows - 2, 2)], near.at[:, pl.ds(rows - 2, 2)]),
                (forward_hbm.at[pl.ds(final_kind, 1)], forward.at[pl.ds(final_kind, 1)]),
                (state_hbm.at[:, pl.ds(2, rows - 4)], near.at[:, pl.ds(2, rows - 4)]),
                (forward_hbm.at[pl.ds(0, final_kind)], forward.at[pl.ds(0, final_kind)]),
            ]
        )
    ]
    for copy in copies:
        copy.start()
    copies[0].wait()
    copies[1].wait()
    lanes = cells.shape[1]
    local = cells[...] & (rows * depth - 1)
    slot = (local // depth) * LAYER + (local & (depth - 1)) - (depth - LAYER)
    blocks = cells.shape[0]
    spots = lax.broadcasted_iota(jnp.int32, (depth, lanes), 0)
    hits = [(spots == slot[i : i + 1, :]).astype(jnp.float32).astype(jnp.bfloat16) for i in range(blocks)]
    pieces = exact_pieces(force[...])
    terms = [
        lax.dot_general(
            jnp.concatenate(pieces, axis=0),
            hit,
            (((1,), (1,)), ((), ())),
            preferred_element_type=jnp.float32,
        )
        for hit in hits
    ]
    count = force.shape[0]
    terms = [t[:count] + t[count : 2 * count] + t[2 * count :] for t in terms]
    layers = terms[0]
    for block in range(1, blocks):
        layers = layers + pltpu.roll(terms[block], count - 2 * block, 0)
    table_ref[...] = layers
    def moved(row):
        return at_row(layers, row, depth)

    own = lax.broadcasted_iota(jnp.int32, layers.shape, 0) & (rows - 1)
    picked = jnp.where(own < 6, pltpu.roll(moved(1), 2, 0), pltpu.roll(moved(rows - 1), 6, 0))
    near_force[...] = jnp.where((own & 2) == 0, moved(0), picked)
    copies[2].wait()
    for event in range(events):
        record = pl.multiple_of(source[event] * rows, rows)
        pushes[pl.ds(event * rows, rows), :] = near_force[pl.ds(record, rows), :]
    for copy in copies[3:-2]:
        copy.wait()
    weights[...] = forward[final_kind].astype(jnp.float32)
    vel = load_coeffs(vel_ref)
    stress = load_coeffs(stress_ref)
    odd = lax.rem(lax.axis_index("gx"), 2) == 1
    message_core = (message_first, message_second)
    last = rows - 1
    state = near.reshape(near.shape[0] * rows, depth)

    def rim(chunk, field, row):
        return state[pl.ds((field * events + chunk) * rows + row, 8, stride=rows), :]

    def pushed(chunk, step, part, row):
        at = PUSHED.index((step, row if row < last else -1)) * 2 + part
        return pushes[pl.ds(chunk * rows + at, 8, stride=rows), :]

    for chunk in range(0, events, 8):
        first = [rim(chunk, f, 0) for f in range(FIELDS)]
        second = [rim(chunk, f, 1) for f in range(FIELDS)]
        final = [rim(chunk, f, last) for f in range(FIELDS)]
        inner = {f: rim(chunk, f, last - 1) for f in (SXX, SXZ, PR)}

        def kicked(fields, gains, step, row):
            vel_x, vel_z, flow_x, flow_z = plus(fields, gains)
            return (
                vel_x + pushed(chunk, step, 0, row),
                vel_z + pushed(chunk, step, 1, row),
                flow_x,
                flow_z,
            )

        def forces(fields, before):
            return (
                fields[SXX] - before[SXX] + depth_lower(fields[SXZ]),
                fields[SXZ] - before[SXZ] + depth_lower(fields[SZZ]),
                fields[PR] - before[PR] + vel[3] * fields[QX],
                depth_lower(fields[PR]) + vel[3] * fields[QZ],
            )

        nothing = {SXX: 0.0, SXZ: 0.0, PR: 0.0}
        vel_first = kicked(first[:4], velocity_gain(vel, *forces(first, nothing)), 0, 0)
        vel_second = kicked(second[:4], velocity_gain(vel, *forces(second, first)), 0, 1)
        vel_final = kicked(final[:4], velocity_gain(vel, *forces(final, inner)), 0, last)
        stress_first = plus(
            first[4:],
            stress_gain(
                stress,
                vel_second[0] - vel_first[0],
                depth_upper(vel_first[1]),
                vel_second[2] - vel_first[2] + depth_upper(vel_first[3]),
                depth_upper(vel_first[0]) + vel_second[1] - vel_first[1],
            ),
        )
        stress_final = plus(
            final[4:],
            stress_gain(
                stress,
                -vel_final[0],
                depth_upper(vel_final[1]),
                -vel_final[2] + depth_upper(vel_final[3]),
                depth_upper(vel_final[0]) - vel_final[1],
            ),
        )
        again = kicked(
            vel_first,
            velocity_gain(vel, *forces(list(vel_first) + list(stress_first), nothing)),
            1,
            0,
        )
        right = [final[SXX], final[SXZ], final[PR], stress_final[0], stress_final[2], stress_final[3]]
        left = [vel_first[0], vel_first[1], vel_first[2], again[0], again[1], again[2]]
        for i in range(HALO):
            half = message_core[i // 3]
            half[pl.ds(i % 3 * events + chunk, 8), :] = jnp.where(odd, left[i], right[i])
        flow = vel[1] * stress_final[0] + vel[2] * stress_final[3]
        drain = stress[2] * again[0] + stress[3] * again[2]
        weight = weights[pl.ds(chunk * rows, 8, stride=rows), :]
        right_soon = right[:3] + [flow, stress_final[2]]
        left_soon = left[:3] + [drain, weight]
        right_late = [stress_final[0], stress_final[3], stress_final[3]]
        for i in range(SOON):
            message_chip[pl.ds(i * events + chunk, 8), :] = jnp.where(odd, right_soon[i], left_soon[i])
        for i in range(LATE):
            message_late[pl.ds(i * events + chunk, 8), :] = jnp.where(odd, right_late[i], left[3 + i])
    for copy in copies[-2:]:
        copy.wait()


def group_of(events):
    return next(g for g in GROUPS if events % g == 0)


def bulk_kernel(
    sizes,
    given,
    forward,
    source,
    table_ref,
    vel_ref,
    stress_ref,
    late_in,
    changed,
    weights,
    sums,
    late,
    by_source,
):
    events, rows, depth, steps, sources = sizes
    group = group_of(events)
    state_in = given.reshape(FIELDS, events * rows, depth)
    state = changed.reshape(FIELDS, events * rows, depth)
    each = table_ref.shape[0] // sources
    for step in range(steps):
        for part in range(2):
            layers = table_ref[pl.ds(step * (each // steps) + part, sources, stride=each), :]
            for row in range(rows):
                at = (step * 2 + part) * sources * rows + row
                by_source[pl.ds(at, sources, stride=rows), :] = at_row(layers, row, depth)
    vel = tuple(jnp.broadcast_to(c, (rows, depth)) for c in load_coeffs(vel_ref))
    stress = tuple(jnp.broadcast_to(c, (rows, depth)) for c in load_coeffs(stress_ref))

    def body(i, carry):
        perm, poro = carry

        def tile(sub, count=1):
            at = (i * group + sub) * rows
            return pl.ds(pl.multiple_of(at, count * rows), count * rows)

        def pushed(step, part, sub):
            at = ((step * 2 + part) * sources + source[i * group + sub]) * rows
            return by_source[pl.ds(pl.multiple_of(at, rows), rows), :]

        fields = [[state_in[f, tile(sub), :] for f in range(FIELDS)] for sub in range(group)]
        for step in range(steps):
            factors = [[] for _ in range(group)]
            for kind in range(3):
                for sub in range(0, group, 2):
                    both = forward[step * 3 + kind, tile(sub, 2), :].astype(jnp.float32)
                    for half in range(2):
                        value = both[half * rows : (half + 1) * rows]
                        weights[step * 3 + kind, tile(sub + half), :] = value
                        factors[sub + half].append(value)
            for sub, own in enumerate(fields):
                gains = velocity_gain(
                    vel,
                    row_lower(own[SXX]) + depth_lower(own[SXZ]),
                    row_lower(own[SXZ]) + depth_lower(own[SZZ]),
                    row_lower(own[PR]) + vel[3] * own[QX],
                    depth_lower(own[PR]) + vel[3] * own[QZ],
                )
                own[:4] = plus(own[:4], gains)
                own[VX] = own[VX] + pushed(step, 0, sub)
                own[VZ] = own[VZ] + pushed(step, 1, sub)
                perm = perm + own[QX] * factors[sub][0] + own[QZ] * factors[sub][1]
            for sub, own in enumerate(fields):
                own[4:] = plus(
                    own[4:],
                    stress_gain(
                        stress,
                        row_upper(own[VX]),
                        depth_upper(own[VZ]),
                        row_upper(own[QX]) + depth_upper(own[QZ]),
                        depth_upper(own[VX]) + row_upper(own[VZ]),
                    ),
                )
                poro = poro + own[PR] * factors[sub][2]
        for sub, own in enumerate(fields):
            for f in range(FIELDS):
                state[f, tile(sub), :] = own[f]
        return perm, poro

    zero = jnp.zeros((rows, depth), jnp.float32)
    perm, poro = lax.fori_loop(0, events // group, body, (zero, zero))
    sums[pl.ds(0, rows), :] = perm
    sums[pl.ds(rows, rows), :] = poro


def from_before(vel, stress_x, stress_xz, pressure):
    return velocity_gain(vel, -stress_x, -stress_xz, -pressure, 0.0)


def forces(vel, stresses, flows):
    return (
        stresses[0] + depth_lower(stresses[2]),
        stresses[2] + depth_lower(stresses[1]),
        stresses[3] + vel[3] * flows[0],
        depth_lower(stresses[3]) + vel[3] * flows[1],
    )


def strains(stress, vels, after):
    return stress_gain(
        stress,
        after[0] - vels[0],
        depth_upper(vels[1]),
        after[2] - vels[2] + depth_upper(vels[3]),
        depth_upper(vels[0]) + after[1] - vels[1],
    )


NOTHING = (0.0, 0.0, 0.0)


def left_changes(vel, stress, sent, got, factor):
    gain_first = from_before(vel, *got[:3])
    before = beyond_gain(stress, *plus(sent[:3], gain_first[:3]))
    before = plus(got[3:], (before[0], before[2], before[3]))
    stress_first = strains(stress, gain_first, NOTHING)
    vel_first = plus(
        plus(gain_first, velocity_gain(vel, *forces(vel, stress_first, gain_first[2:]))),
        from_before(vel, *before),
    )
    vel_second = from_before(vel, stress_first[0], stress_first[2], stress_first[3])
    end_first = plus(stress_first, strains(stress, vel_first, vel_second))
    end_second = strains(stress, vel_second, NOTHING)
    perm = gain_first[2] * factor(0, 0, 0) + gain_first[3] * factor(0, 1, 0)
    for row, vels in ((0, vel_first), (1, vel_second)):
        perm = perm + vels[2] * factor(1, 0, row) + vels[3] * factor(1, 1, row)
    poro = stress_first[3] * factor(0, 2, 0)
    for row, stresses in ((0, end_first), (1, end_second)):
        poro = poro + stresses[3] * factor(1, 2, row)
    return vel_first + vel_second + end_first + end_second, perm, poro


def right_changes(vel, stress, sent, got, factor, last):
    gain_after = from_before(vel, *sent[:3])
    stress_last = beyond_gain(stress, *plus(got[:3], gain_after[:3]))
    true_last = plus(sent[3:], (stress_last[0], stress_last[2], stress_last[3]))
    vel_last = velocity_gain(
        vel,
        stress_last[0] + depth_lower(stress_last[2]),
        stress_last[2] + depth_lower(stress_last[1]),
        stress_last[3],
        depth_lower(stress_last[3]),
    )
    stress_after = strains(stress, gain_after, NOTHING)
    again = plus(
        plus(gain_after, velocity_gain(vel, *forces(vel, stress_after, gain_after[2:]))),
        from_before(vel, *true_last),
    )
    again = plus(got[3:], again[:3])
    end_inner = beyond_gain(stress, *vel_last[:3])
    end_last = plus(stress_last, strains(stress, vel_last, again))
    perm = vel_last[2] * factor(1, 0, last) + vel_last[3] * factor(1, 1, last)
    poro = stress_last[3] * factor(0, 2, last)
    for row, stresses in ((last - 1, end_inner), (last, end_last)):
        poro = poro + stresses[3] * factor(1, 2, row)
    return vel_last + end_inner + end_last, perm, poro


def left_changes_soon(vel, stress, sent, own_late, got, factor):
    gain_first = from_before(vel, *got[:3])
    beyond = beyond_gain(stress, *plus(sent[:3], gain_first[:3]))
    flow = got[3] + vel[1] * beyond[0] + vel[2] * beyond[3]
    shear = got[4] + beyond[2]
    stress_first = strains(stress, gain_first, NOTHING)
    vel_first = plus(gain_first, velocity_gain(vel, *forces(vel, stress_first, gain_first[2:])))
    vel_first = plus(vel_first, (0.0, -vel[0] * shear, flow, vel[1] * shear))
    vel_second = from_before(vel, stress_first[0], stress_first[2], stress_first[3])
    end_first = plus(stress_first, strains(stress, vel_first, vel_second))
    end_second = strains(stress, vel_second, NOTHING)
    perm = gain_first[2] * factor(0, 0, 0) + gain_first[3] * factor(0, 1, 0)
    for row, vels in ((0, vel_first), (1, vel_second)):
        perm = perm + vels[2] * factor(1, 0, row) + vels[3] * factor(1, 1, row)
    poro = stress_first[3] * factor(0, 2, 0)
    for row, stresses in ((0, end_first), (1, end_second)):
        poro = poro + stresses[3] * factor(1, 2, row)
    rest = (vel[0] * beyond[0] + vel[1] * beyond[3],)
    return vel_first + vel_second + end_first + end_second + rest, perm, poro


def right_changes_soon(vel, stress, sent, own_late, got, factor, last):
    gain_after = from_before(vel, *sent[:3])
    stress_last = beyond_gain(stress, *plus(got[:3], gain_after[:3]))
    true_last = (own_late[0] + stress_last[0], sent[4] + stress_last[2], own_late[1] + stress_last[3])
    vel_last = velocity_gain(
        vel,
        stress_last[0] + depth_lower(stress_last[2]),
        stress_last[2] + depth_lower(stress_last[1]),
        stress_last[3],
        depth_lower(stress_last[3]),
    )
    stress_after = strains(stress, gain_after, NOTHING)
    again = plus(
        plus(gain_after, velocity_gain(vel, *forces(vel, stress_after, gain_after[2:]))),
        from_before(vel, *true_last),
    )
    drain = got[3] + stress[2] * again[0] + stress[3] * again[2]
    end_inner = beyond_gain(stress, *vel_last[:3])
    end_last = plus(stress_last, strains(stress, vel_last, NOTHING))
    perm = vel_last[2] * factor(1, 0, last) + vel_last[3] * factor(1, 1, last)
    poro = stress_last[3] * factor(0, 2, last)
    poro = poro + end_inner[3] * factor(1, 2, last - 1) + (end_last[3] - drain) * factor(1, 2, last)
    poro = poro - stress[2] * (vel[0] * true_last[0] + vel[1] * true_last[2]) * got[4]
    return vel_last + end_inner + end_last + again[:3], perm, poro


def side_sums(sizes, over_chips, weights, sent, own_late, got, vel_ref, stress_ref, changes):
    events, rows, depth, _, _ = sizes
    vel = load_coeffs(vel_ref)
    stress = load_coeffs(stress_ref)
    last = rows - 1
    left, right = sides(over_chips)
    count = SOON if over_chips else HALO

    def fill(changed, partial):
        for chunk in range(0, events, 8):

            def row_of(refs, i):
                each = count // len(refs)
                return refs[i // each][pl.ds(i % each * events + chunk, 8), :]

            def factor(step, kind, row):
                return weights[step * 3 + kind, pl.ds(chunk * rows + row, 8, stride=rows), :]

            own = tuple(row_of(sent, i) for i in range(count))
            new = tuple(row_of(got, i) for i in range(count))
            if over_chips:
                late = tuple(own_late[pl.ds(i * events + chunk, 8), :] for i in range(LATE))
                values, perm, poro = changed(vel, stress, own, late, new, factor)
            else:
                values, perm, poro = changed(vel, stress, own, new, factor)
            for i, value in enumerate(values):
                changes[i, pl.ds(chunk, 8), :] = value
            partial = (partial[0] + perm, partial[1] + poro)
        return partial

    zero = (jnp.zeros((8, depth), jnp.float32),) * 2
    from_left = left_changes_soon if over_chips else left_changes
    from_right = functools.partial(right_changes_soon if over_chips else right_changes, last=last)
    return lax.cond(
        left,
        lambda: fill(from_left, zero),
        lambda: lax.cond(right, lambda: fill(from_right, zero), lambda: zero),
    )


def sides(over_chips):
    place = lax.axis_index("gx")
    odd = lax.rem(place, 2) == 1
    if over_chips:
        return jnp.logical_and(jnp.logical_not(odd), place > 0), jnp.logical_and(
            odd, place < lax.axis_size("gx") - 1
        )
    return odd, jnp.logical_not(odd)


def core_kernel(
    sizes, sums_in, weights, sent_a, sent_b, got_a, got_b, vel_ref, stress_ref, changes, sums
):
    rows = sizes[1]
    sent, got = (sent_a, sent_b), (got_a, got_b)
    perm, poro = side_sums(sizes, False, weights, sent, None, got, vel_ref, stress_ref, changes)
    sums[pl.ds(0, rows), :] = sums_in[pl.ds(0, rows), :] + perm
    sums[pl.ds(rows, rows), :] = sums_in[pl.ds(rows, rows), :] + poro


def chip_kernel(
    sizes, normalizer, sums, weights, sent, late, got, vel_ref, stress_ref, changes, totals
):
    rows = sizes[1]
    vel = load_coeffs(vel_ref)
    stress = load_coeffs(stress_ref)
    perm, poro = side_sums(sizes, True, weights, (sent,), late, (got,), vel_ref, stress_ref, changes)
    perm = jnp.sum(sums[pl.ds(0, rows), :] + perm, axis=0, keepdims=True)
    poro = jnp.sum(sums[pl.ds(rows, rows), :] + poro, axis=0, keepdims=True)
    totals[pl.ds(0, 1), :] = perm * (vel[2] * vel[3] * normalizer)
    totals[pl.ds(1, 1), :] = poro * (stress[3] * normalizer)


def finish_kernel(
    sizes, given, changes_core, changes_chip, late, vel_ref, stress_ref, changed, out_hbm, done, sems
):
    events, rows, depth, _, _ = sizes
    state_in = given.reshape(FIELDS, events * rows, depth)
    state = changed.reshape(FIELDS, events * rows, depth)
    vel = load_coeffs(vel_ref)
    stress = load_coeffs(stress_ref)
    last = rows - 1
    left_places = [(s + f, row) for s in (0, 4) for row in (0, 1) for f in range(4)]
    right_places = [(f, last) for f in range(4)] + [(4 + f, row) for row in (last - 1, last) for f in range(4)]
    got = [late[pl.ds(i * events, events), :] for i in range(LATE)]

    def left_late():
        push = vel[0] * got[0] + vel[1] * got[1] + changes_chip[len(left_places)]
        stresses = stress_gain(stress, push, 0.0, 0.0, depth_upper(-push))
        return {(VX, 0): -push} | {(SXX + f, 0): stresses[f] for f in range(4)}

    def right_late():
        again = [got[i] + changes_chip[len(right_places) + i] for i in range(LATE)]
        stresses = beyond_gain(stress, *again)
        return {(SXX + f, last): stresses[f] for f in range(4)}

    def patch(changes, places, fields, more):
        added = more() if more else {}
        for i, (field, row) in enumerate(places):
            if field in fields:
                at = pl.ds(row, events, stride=rows)
                value = changes[i]
                if (field, row) in added:
                    value = value + added[field, row]
                state[field, at, :] = state_in[field, at, :] + value

    half = FIELDS // 2
    copies = []
    for i in range(2):
        fields = range(i * half, (i + 1) * half)
        for over_chips, changes in ((False, changes_core), (True, changes_chip)):
            left, right = sides(over_chips)
            pl.when(left)(
                functools.partial(patch, changes, left_places, fields, left_late if over_chips else None)
            )
            pl.when(right)(
                functools.partial(patch, changes, right_places, fields, right_late if over_chips else None)
            )
        own = pl.ds(i * half * events, half * events)
        copies.append(pltpu.make_async_copy(changed.at[own], out_hbm.at[own], sems.at[i]))
        copies[i].start()
    done[...] = jnp.zeros_like(done)
    for copy in copies:
        copy.wait()


def swap_with(value, size, mask):
    return lax.ppermute(value, "gx", [(i, i ^ mask) for i in range(size)])


def swap_over_chips(value, groups, size):
    route = []
    for group in range(groups):
        base = group * size
        other = (group ^ 1) * size
        for i in range(1, size - 1, 2):
            route += [(base + i, base + i + 1), (base + i + 1, base + i)]
        route += [(base, other), (base + size - 1, other + size - 1)]
    return lax.ppermute(value, ("groups", "gx"), route)


def shards(
    adjoint_state, forward_fields, vel_coeffs, stress_coeffs, drm_cells, drm_force, source_id
):
    fields, events, rows, depth = adjoint_state.shape
    steps = forward_fields.shape[0]
    sources = drm_force.shape[0]
    entries = drm_cells.shape[0]
    size = lax.axis_size("gx")
    groups = lax.axis_size("groups")
    sizes = (events, rows, depth, steps, sources)
    blocks = entries // 128
    tiles = events * rows
    f32 = jnp.float32
    any_space = pl.BlockSpec(memory_space=pl.ANY)
    vmem = pl.BlockSpec(memory_space=pltpu.VMEM)
    smem = pl.BlockSpec(memory_space=pltpu.SMEM)
    state = adjoint_state.reshape(fields * events, rows, depth)
    forward = forward_fields.reshape(steps * 3, tiles, depth)
    cells = drm_cells.reshape(blocks, 128)
    force = drm_force.reshape(sources * steps, 2, blocks, 128).transpose(0, 2, 1, 3)
    force = force.reshape(sources * steps * 2 * blocks, 128)
    soon = pltpu.VMEM((SOON * events, depth), f32)
    late = pltpu.VMEM((LATE * events, depth), f32)
    half = pltpu.VMEM((HALO // 2 * events, depth), f32)
    limits = pltpu.CompilerParams(vmem_limit_bytes=ROOM)

    def kept(space, *values):
        return tuple(pltpu.with_memory_space_constraint(v, space) for v in values)

    (
        state,
        forward,
        source,
        table,
        message_first,
        message_second,
        message_chip,
        message_late,
        vel,
        stress,
    ) = pl.pallas_call(
        functools.partial(edge_kernel, sizes),
        out_shape=(
            pltpu.VMEM(state.shape, f32),
            pltpu.VMEM(forward.shape, forward.dtype),
            pltpu.SMEM((events,), jnp.int32),
            pltpu.VMEM(force.shape, f32),
            half,
            half,
            soon,
            late,
            pltpu.VMEM(vel_coeffs.shape, f32),
            pltpu.VMEM(stress_coeffs.shape, f32),
        ),
        in_specs=[any_space] * 7,
        out_specs=(vmem, vmem, smem) + (vmem,) * 7,
        scratch_shapes=[
            pltpu.VMEM((tiles, depth), f32),
            pltpu.VMEM(cells.shape, jnp.int32),
            pltpu.VMEM(force.shape, f32),
            pltpu.VMEM(force.shape, f32),
            pltpu.VMEM((tiles, depth), f32),
            pltpu.SemaphoreType.DMA((10,)),
        ],
        compiler_params=limits,
        name="edges",
    )(
        *kept(
            pltpu.HBM,
            state,
            forward,
            vel_coeffs,
            stress_coeffs,
            cells,
            force,
            source_id,
        )
    )

    got_first = swap_with(message_first, size, 1)
    got_second = swap_with(message_second, size, 1)
    got_chip = swap_over_chips(message_chip, groups, size)

    state, weights, sums, message_late = pl.pallas_call(
        functools.partial(bulk_kernel, sizes),
        out_shape=(
            pltpu.VMEM(state.shape, f32),
            pltpu.VMEM(forward.shape, f32),
            pltpu.VMEM((2 * rows, depth), f32),
            late,
        ),
        in_specs=[vmem] * 2 + [smem] + [vmem] * 4,
        out_specs=(vmem,) * 4,
        input_output_aliases={0: 0, 6: 3},
        scratch_shapes=[pltpu.VMEM((steps * 2 * sources * rows, depth), f32)],
        compiler_params=limits,
        cost_estimate=pl.CostEstimate(
            flops=steps * 80 * tiles * depth, bytes_accessed=8 * state.size, transcendentals=0
        ),
        name="bulk",
    )(
        *kept(pltpu.VMEM, state, forward),
        *kept(pltpu.SMEM, source),
        *kept(pltpu.VMEM, table, vel, stress, message_late),
    )
    got_late = swap_over_chips(message_late, groups, size)

    normalizer = (events * rows * size) ** (-0.5)
    changed = pltpu.VMEM((17, events, depth), f32)
    changes_core, sums = pl.pallas_call(
        functools.partial(core_kernel, sizes),
        out_shape=(changed, pltpu.VMEM(sums.shape, f32)),
        in_specs=[vmem] * 8,
        out_specs=(vmem,) * 2,
        compiler_params=limits,
        name="join_core",
    )(
        *kept(
            pltpu.VMEM,
            sums,
            weights,
            message_first,
            message_second,
            got_first,
            got_second,
            vel,
            stress,
        )
    )

    changes_chip, totals = pl.pallas_call(
        functools.partial(chip_kernel, sizes, normalizer),
        out_shape=(changed, pltpu.VMEM((2, depth), f32)),
        in_specs=[vmem] * 7,
        out_specs=(vmem,) * 2,
        compiler_params=limits,
        name="join_chip",
    )(*kept(pltpu.VMEM, sums, weights, message_chip, message_late, got_chip, vel, stress))

    _, out, done = pl.pallas_call(
        functools.partial(finish_kernel, sizes),
        out_shape=(
            pltpu.VMEM(state.shape, f32),
            jax.ShapeDtypeStruct(state.shape, f32),
            pltpu.VMEM((2, depth), f32),
        ),
        in_specs=[vmem] * 6,
        out_specs=(vmem, any_space, vmem),
        input_output_aliases={0: 0},
        scratch_shapes=[pltpu.SemaphoreType.DMA((2,))],
        compiler_params=limits,
        cost_estimate=pl.CostEstimate(flops=0, bytes_accessed=2 * 4 * state.size, transcendentals=0),
        name="finish",
    )(*kept(pltpu.VMEM, state, changes_core, changes_chip, got_late, vel, stress))

    mask = 1
    while mask < size:
        totals = totals + swap_with(totals, size, mask | 1)
        if mask * 4 == size:
            totals = totals + done
        mask *= 2
    return out.reshape(adjoint_state.shape), totals


def solution(mesh):
    in_specs = (
        P(None, "groups", "gx", None),
        P(None, None, "groups", "gx", None),
        P("groups", None),
        P("groups", None),
        P("gx"),
        P("groups", None, None, "gx"),
        P("groups"),
    )
    out_specs = (P(None, "groups", "gx", None), P("groups", None))
    return jax.shard_map(shards, mesh=mesh, in_specs=in_specs, out_specs=out_specs, check_vma=False)
```

```python
import functools

import jax
import jax.numpy as jnp
from jax import lax
from jax.experimental import pallas as pl
from jax.experimental.pallas import tpu as pltpu
from jax.sharding import PartitionSpec as P

LAYER = 8
FIELDS = 8
VX, VZ, QX, QZ, SXX, SZZ, SXZ, PR = range(FIELDS)
HALO = 6
SOON = 5
LATE = 3
PUSHED = ((0, 0), (0, 1), (1, 0), (0, -1))
GROUPS = (16, 8, 4, 2)
ROOM = 16 << 20


def depth_lower(values):
    lane = lax.broadcasted_iota(jnp.int32, values.shape, 1)
    return values - jnp.where(lane == 0, 0.0, pltpu.roll(values, 1, 1))


def depth_upper(values):
    depth = values.shape[1]
    lane = lax.broadcasted_iota(jnp.int32, values.shape, 1)
    return jnp.where(lane == depth - 1, 0.0, pltpu.roll(values, depth - 1, 1)) - values


def row_lower(values):
    row = lax.broadcasted_iota(jnp.int32, values.shape, 0)
    return values - jnp.where(row == 0, 0.0, pltpu.roll(values, 1, 0))


def row_upper(values):
    rows = values.shape[0]
    row = lax.broadcasted_iota(jnp.int32, values.shape, 0)
    return jnp.where(row == rows - 1, 0.0, pltpu.roll(values, rows - 1, 0)) - values


def velocity_gain(coeffs, force_x, force_z, push_x, push_z):
    solid, couple, fluid, _ = coeffs
    return (
        solid * force_x + couple * push_x,
        solid * force_z + couple * push_z,
        -couple * force_x - fluid * push_x,
        -couple * force_z - fluid * push_z,
    )


def stress_gain(coeffs, strain_x, strain_z, inflow, shear):
    lame, modulus, coupling, fluid = coeffs
    dilation = strain_x + strain_z
    common = lame * dilation - coupling * inflow
    return (
        common + 2.0 * modulus * strain_x,
        common + 2.0 * modulus * strain_z,
        modulus * shear,
        -coupling * dilation - fluid * inflow,
    )


def beyond_gain(coeffs, vel_x, vel_z, flow_x):
    lame, modulus, coupling, fluid = coeffs
    return (
        (lame + 2.0 * modulus) * vel_x - coupling * flow_x,
        lame * vel_x - coupling * flow_x,
        modulus * vel_z,
        -coupling * vel_x - fluid * flow_x,
    )


def plus(left, right):
    return tuple(a + b for a, b in zip(left, right))


def minus(left, right):
    return tuple(a - b for a, b in zip(left, right))


def load_coeffs(ref):
    return tuple(ref[pl.ds(i, 1), :] for i in range(4))


def at_row(layers, row, depth):
    lane = lax.broadcasted_iota(jnp.int32, layers.shape, 1)
    moved = pltpu.roll(layers, (depth - LAYER - LAYER * row) % depth, 1)
    return jnp.where(lane >= depth - LAYER, moved, 0.0)


def exact_pieces(values):
    pieces = []
    for _ in range(3):
        pieces.append(values.astype(jnp.bfloat16))
        values = values - pieces[-1].astype(jnp.float32)
    return pieces


def edge_kernel(
    sizes,
    state_hbm,
    forward_hbm,
    vel_hbm,
    stress_hbm,
    cells_hbm,
    force_hbm,
    source_hbm,
    near,
    forward,
    source,
    table_ref,
    message_first,
    message_second,
    message_chip,
    message_late,
    vel_ref,
    stress_ref,
    weights,
    cells,
    force,
    near_force,
    pushes,
    sems,
):
    events, rows, depth, steps, sources = sizes
    final_kind = steps * 3 - 1
    copies = [
        pltpu.make_async_copy(src, dst, sems.at[min(i, 3) if i < 8 else 4])
        for i, (src, dst) in enumerate(
            [
                (cells_hbm, cells),
                (force_hbm, force),
                (source_hbm, source),
                (vel_hbm, vel_ref),
                (stress_hbm, stress_ref),
                (state_hbm.at[:, pl.ds(0, 2)], near.at[:, pl.ds(0, 2)]),
                (state_hbm.at[:, pl.ds(rows - 2, 2)], near.at[:, pl.ds(rows - 2, 2)]),
                (forward_hbm.at[pl.ds(final_kind, 1)], forward.at[pl.ds(final_kind, 1)]),
                (state_hbm.at[:, pl.ds(2, rows - 4)], near.at[:, pl.ds(2, rows - 4)]),
                (forward_hbm.at[pl.ds(0, final_kind)], forward.at[pl.ds(0, final_kind)]),
            ]
        )
    ]
    for copy in copies:
        copy.start()
    copies[0].wait()
    copies[1].wait()
    lanes = cells.shape[1]
    local = cells[...] & (rows * depth - 1)
    slot = (local // depth) * LAYER + (local & (depth - 1)) - (depth - LAYER)
    blocks = cells.shape[0]
    spots = lax.broadcasted_iota(jnp.int32, (depth, lanes), 0)
    hits = [(spots == slot[i : i + 1, :]).astype(jnp.float32).astype(jnp.bfloat16) for i in range(blocks)]
    pieces = exact_pieces(force[...])
    terms = [
        lax.dot_general(
            jnp.concatenate(pieces, axis=0),
            hit,
            (((1,), (1,)), ((), ())),
            preferred_element_type=jnp.float32,
        )
        for hit in hits
    ]
    count = force.shape[0]
    terms = [t[:count] + t[count : 2 * count] + t[2 * count :] for t in terms]
    layers = terms[0]
    for block in range(1, blocks):
        layers = layers + pltpu.roll(terms[block], count - 2 * block, 0)
    table_ref[...] = layers
    def moved(row):
        return at_row(layers, row, depth)

    own = lax.broadcasted_iota(jnp.int32, layers.shape, 0) & (rows - 1)
    picked = jnp.where(own < 6, pltpu.roll(moved(1), 2, 0), pltpu.roll(moved(rows - 1), 6, 0))
    near_force[...] = jnp.where((own & 2) == 0, moved(0), picked)
    copies[2].wait()
    for event in range(events):
        record = pl.multiple_of(source[event] * rows, rows)
        pushes[pl.ds(event * rows, rows), :] = near_force[pl.ds(record, rows), :]
    def wait_tiles(index, count):
        own = near.at[pl.ds(0, count)]
        pltpu.make_async_copy(own, own, sems.at[index]).wait()

    kind_tiles = events // 2
    coeff_tiles = 2 * vel_ref.shape[0] // rows
    wait_tiles(3, FIELDS * events * 4 // rows + kind_tiles + coeff_tiles)
    weights[...] = forward[final_kind].astype(jnp.float32)
    vel = load_coeffs(vel_ref)
    stress = load_coeffs(stress_ref)
    odd = lax.rem(lax.axis_index("gx"), 2) == 1
    message_core = (message_first, message_second)
    last = rows - 1
    state = near.reshape(near.shape[0] * rows, depth)

    def rim(chunk, field, row):
        return state[pl.ds((field * events + chunk) * rows + row, 8, stride=rows), :]

    def pushed(chunk, step, part, row):
        at = PUSHED.index((step, row if row < last else -1)) * 2 + part
        return pushes[pl.ds(chunk * rows + at, 8, stride=rows), :]

    for chunk in range(0, events, 8):
        first = [rim(chunk, f, 0) for f in range(FIELDS)]
        second = [rim(chunk, f, 1) for f in range(FIELDS)]
        final = [rim(chunk, f, last) for f in range(FIELDS)]
        inner = {f: rim(chunk, f, last - 1) for f in (SXX, SXZ, PR)}

        def kicked(fields, gains, step, row):
            vel_x, vel_z, flow_x, flow_z = plus(fields, gains)
            return (
                vel_x + pushed(chunk, step, 0, row),
                vel_z + pushed(chunk, step, 1, row),
                flow_x,
                flow_z,
            )

        def forces(fields, before):
            return (
                fields[SXX] - before[SXX] + depth_lower(fields[SXZ]),
                fields[SXZ] - before[SXZ] + depth_lower(fields[SZZ]),
                fields[PR] - before[PR] + vel[3] * fields[QX],
                depth_lower(fields[PR]) + vel[3] * fields[QZ],
            )

        nothing = {SXX: 0.0, SXZ: 0.0, PR: 0.0}
        vel_first = kicked(first[:4], velocity_gain(vel, *forces(first, nothing)), 0, 0)
        vel_second = kicked(second[:4], velocity_gain(vel, *forces(second, first)), 0, 1)
        vel_final = kicked(final[:4], velocity_gain(vel, *forces(final, inner)), 0, last)
        stress_first = plus(
            first[4:],
            stress_gain(
                stress,
                vel_second[0] - vel_first[0],
                depth_upper(vel_first[1]),
                vel_second[2] - vel_first[2] + depth_upper(vel_first[3]),
                depth_upper(vel_first[0]) + vel_second[1] - vel_first[1],
            ),
        )
        stress_final = plus(
            final[4:],
            stress_gain(
                stress,
                -vel_final[0],
                depth_upper(vel_final[1]),
                -vel_final[2] + depth_upper(vel_final[3]),
                depth_upper(vel_final[0]) - vel_final[1],
            ),
        )
        again = kicked(
            vel_first,
            velocity_gain(vel, *forces(list(vel_first) + list(stress_first), nothing)),
            1,
            0,
        )
        right = [final[SXX], final[SXZ], final[PR], stress_final[0], stress_final[2], stress_final[3]]
        left = [vel_first[0], vel_first[1], vel_first[2], again[0], again[1], again[2]]
        for i in range(HALO):
            half = message_core[i // 3]
            half[pl.ds(i % 3 * events + chunk, 8), :] = jnp.where(odd, left[i], right[i])
        flow = vel[1] * stress_final[0] + vel[2] * stress_final[3]
        drain = stress[2] * again[0] + stress[3] * again[2]
        weight = weights[pl.ds(chunk * rows, 8, stride=rows), :]
        right_soon = right[:3] + [flow, stress_final[2]]
        left_soon = left[:3] + [drain, weight]
        right_late = [stress_final[0], stress_final[3], stress_final[3]]
        for i in range(SOON):
            message_chip[pl.ds(i * events + chunk, 8), :] = jnp.where(odd, right_soon[i], left_soon[i])
        for i in range(LATE):
            message_late[pl.ds(i * events + chunk, 8), :] = jnp.where(odd, right_late[i], left[3 + i])
    wait_tiles(4, FIELDS * events * (rows - 4) // rows + final_kind * kind_tiles)


def group_of(events):
    return next(g for g in GROUPS if events % g == 0)


def bulk_kernel(
    sizes,
    given,
    forward,
    source,
    table_ref,
    vel_ref,
    stress_ref,
    late_in,
    changed,
    weights,
    sums,
    late,
    by_source,
):
    events, rows, depth, steps, sources = sizes
    group = group_of(events)
    state_in = given.reshape(FIELDS, events * rows, depth)
    state = changed.reshape(FIELDS, events * rows, depth)
    each = table_ref.shape[0] // sources
    for step in range(steps):
        for part in range(2):
            layers = table_ref[pl.ds(step * (each // steps) + part, sources, stride=each), :]
            for row in range(rows):
                at = (step * 2 + part) * sources * rows + row
                by_source[pl.ds(at, sources, stride=rows), :] = at_row(layers, row, depth)
    vel = tuple(jnp.broadcast_to(c, (rows, depth)) for c in load_coeffs(vel_ref))
    stress = tuple(jnp.broadcast_to(c, (rows, depth)) for c in load_coeffs(stress_ref))

    def body(i, carry):
        perm, poro = carry

        def tile(sub, count=1):
            at = (i * group + sub) * rows
            return pl.ds(pl.multiple_of(at, count * rows), count * rows)

        def pushed(step, part, sub):
            at = ((step * 2 + part) * sources + source[i * group + sub]) * rows
            return by_source[pl.ds(pl.multiple_of(at, rows), rows), :]

        fields = [[state_in[f, tile(sub), :] for f in range(FIELDS)] for sub in range(group)]
        for step in range(steps):
            factors = [[] for _ in range(group)]
            for kind in range(3):
                for sub in range(0, group, 2):
                    both = forward[step * 3 + kind, tile(sub, 2), :].astype(jnp.float32)
                    for half in range(2):
                        value = both[half * rows : (half + 1) * rows]
                        weights[step * 3 + kind, tile(sub + half), :] = value
                        factors[sub + half].append(value)
            for sub, own in enumerate(fields):
                gains = velocity_gain(
                    vel,
                    row_lower(own[SXX]) + depth_lower(own[SXZ]),
                    row_lower(own[SXZ]) + depth_lower(own[SZZ]),
                    row_lower(own[PR]) + vel[3] * own[QX],
                    depth_lower(own[PR]) + vel[3] * own[QZ],
                )
                own[:4] = plus(own[:4], gains)
                own[VX] = own[VX] + pushed(step, 0, sub)
                own[VZ] = own[VZ] + pushed(step, 1, sub)
                perm = perm + own[QX] * factors[sub][0] + own[QZ] * factors[sub][1]
            for sub, own in enumerate(fields):
                own[4:] = plus(
                    own[4:],
                    stress_gain(
                        stress,
                        row_upper(own[VX]),
                        depth_upper(own[VZ]),
                        row_upper(own[QX]) + depth_upper(own[QZ]),
                        depth_upper(own[VX]) + row_upper(own[VZ]),
                    ),
                )
                poro = poro + own[PR] * factors[sub][2]
        for sub, own in enumerate(fields):
            for f in range(FIELDS):
                state[f, tile(sub), :] = own[f]
        return perm, poro

    zero = jnp.zeros((rows, depth), jnp.float32)
    perm, poro = lax.fori_loop(0, events // group, body, (zero, zero))
    sums[pl.ds(0, rows), :] = perm
    sums[pl.ds(rows, rows), :] = poro


def from_before(vel, stress_x, stress_xz, pressure):
    return velocity_gain(vel, -stress_x, -stress_xz, -pressure, 0.0)


def forces(vel, stresses, flows):
    return (
        stresses[0] + depth_lower(stresses[2]),
        stresses[2] + depth_lower(stresses[1]),
        stresses[3] + vel[3] * flows[0],
        depth_lower(stresses[3]) + vel[3] * flows[1],
    )


def strains(stress, vels, after):
    return stress_gain(
        stress,
        after[0] - vels[0],
        depth_upper(vels[1]),
        after[2] - vels[2] + depth_upper(vels[3]),
        depth_upper(vels[0]) + after[1] - vels[1],
    )


NOTHING = (0.0, 0.0, 0.0)


def left_changes(vel, stress, sent, got, factor):
    gain_first = from_before(vel, *got[:3])
    before = beyond_gain(stress, *plus(sent[:3], gain_first[:3]))
    before = plus(got[3:], (before[0], before[2], before[3]))
    stress_first = strains(stress, gain_first, NOTHING)
    vel_first = plus(
        plus(gain_first, velocity_gain(vel, *forces(vel, stress_first, gain_first[2:]))),
        from_before(vel, *before),
    )
    vel_second = from_before(vel, stress_first[0], stress_first[2], stress_first[3])
    end_first = plus(stress_first, strains(stress, vel_first, vel_second))
    end_second = strains(stress, vel_second, NOTHING)
    perm = gain_first[2] * factor(0, 0, 0) + gain_first[3] * factor(0, 1, 0)
    for row, vels in ((0, vel_first), (1, vel_second)):
        perm = perm + vels[2] * factor(1, 0, row) + vels[3] * factor(1, 1, row)
    poro = stress_first[3] * factor(0, 2, 0)
    for row, stresses in ((0, end_first), (1, end_second)):
        poro = poro + stresses[3] * factor(1, 2, row)
    return vel_first + vel_second + end_first + end_second, perm, poro


def right_changes(vel, stress, sent, got, factor, last):
    gain_after = from_before(vel, *sent[:3])
    stress_last = beyond_gain(stress, *plus(got[:3], gain_after[:3]))
    true_last = plus(sent[3:], (stress_last[0], stress_last[2], stress_last[3]))
    vel_last = velocity_gain(
        vel,
        stress_last[0] + depth_lower(stress_last[2]),
        stress_last[2] + depth_lower(stress_last[1]),
        stress_last[3],
        depth_lower(stress_last[3]),
    )
    stress_after = strains(stress, gain_after, NOTHING)
    again = plus(
        plus(gain_after, velocity_gain(vel, *forces(vel, stress_after, gain_after[2:]))),
        from_before(vel, *true_last),
    )
    again = plus(got[3:], again[:3])
    end_inner = beyond_gain(stress, *vel_last[:3])
    end_last = plus(stress_last, strains(stress, vel_last, again))
    perm = vel_last[2] * factor(1, 0, last) + vel_last[3] * factor(1, 1, last)
    poro = stress_last[3] * factor(0, 2, last)
    for row, stresses in ((last - 1, end_inner), (last, end_last)):
        poro = poro + stresses[3] * factor(1, 2, row)
    return vel_last + end_inner + end_last, perm, poro


def left_changes_soon(vel, stress, sent, own_late, got, factor):
    gain_first = from_before(vel, *got[:3])
    beyond = beyond_gain(stress, *plus(sent[:3], gain_first[:3]))
    flow = got[3] + vel[1] * beyond[0] + vel[2] * beyond[3]
    shear = got[4] + beyond[2]
    stress_first = strains(stress, gain_first, NOTHING)
    vel_first = plus(gain_first, velocity_gain(vel, *forces(vel, stress_first, gain_first[2:])))
    vel_first = plus(vel_first, (0.0, -vel[0] * shear, flow, vel[1] * shear))
    vel_second = from_before(vel, stress_first[0], stress_first[2], stress_first[3])
    end_first = plus(stress_first, strains(stress, vel_first, vel_second))
    end_second = strains(stress, vel_second, NOTHING)
    perm = gain_first[2] * factor(0, 0, 0) + gain_first[3] * factor(0, 1, 0)
    for row, vels in ((0, vel_first), (1, vel_second)):
        perm = perm + vels[2] * factor(1, 0, row) + vels[3] * factor(1, 1, row)
    poro = stress_first[3] * factor(0, 2, 0)
    for row, stresses in ((0, end_first), (1, end_second)):
        poro = poro + stresses[3] * factor(1, 2, row)
    rest = (vel[0] * beyond[0] + vel[1] * beyond[3],)
    return vel_first + vel_second + end_first + end_second + rest, perm, poro


def right_changes_soon(vel, stress, sent, own_late, got, factor, last):
    gain_after = from_before(vel, *sent[:3])
    stress_last = beyond_gain(stress, *plus(got[:3], gain_after[:3]))
    true_last = (own_late[0] + stress_last[0], sent[4] + stress_last[2], own_late[1] + stress_last[3])
    vel_last = velocity_gain(
        vel,
        stress_last[0] + depth_lower(stress_last[2]),
        stress_last[2] + depth_lower(stress_last[1]),
        stress_last[3],
        depth_lower(stress_last[3]),
    )
    stress_after = strains(stress, gain_after, NOTHING)
    again = plus(
        plus(gain_after, velocity_gain(vel, *forces(vel, stress_after, gain_after[2:]))),
        from_before(vel, *true_last),
    )
    drain = got[3] + stress[2] * again[0] + stress[3] * again[2]
    end_inner = beyond_gain(stress, *vel_last[:3])
    end_last = plus(stress_last, strains(stress, vel_last, NOTHING))
    perm = vel_last[2] * factor(1, 0, last) + vel_last[3] * factor(1, 1, last)
    poro = stress_last[3] * factor(0, 2, last)
    poro = poro + end_inner[3] * factor(1, 2, last - 1) + (end_last[3] - drain) * factor(1, 2, last)
    poro = poro - stress[2] * (vel[0] * true_last[0] + vel[1] * true_last[2]) * got[4]
    return vel_last + end_inner + end_last + again[:3], perm, poro


def side_sums(sizes, over_chips, weights, sent, own_late, got, vel_ref, stress_ref, changes):
    events, rows, depth, _, _ = sizes
    vel = load_coeffs(vel_ref)
    stress = load_coeffs(stress_ref)
    last = rows - 1
    left, right = sides(over_chips)
    count = SOON if over_chips else HALO

    def fill(changed, partial):
        for chunk in range(0, events, 8):

            def row_of(refs, i):
                each = count // len(refs)
                return refs[i // each][pl.ds(i % each * events + chunk, 8), :]

            def factor(step, kind, row):
                return weights[step * 3 + kind, pl.ds(chunk * rows + row, 8, stride=rows), :]

            own = tuple(row_of(sent, i) for i in range(count))
            new = tuple(row_of(got, i) for i in range(count))
            if over_chips:
                late = tuple(own_late[pl.ds(i * events + chunk, 8), :] for i in range(LATE))
                values, perm, poro = changed(vel, stress, own, late, new, factor)
            else:
                values, perm, poro = changed(vel, stress, own, new, factor)
            for i, value in enumerate(values):
                changes[i, pl.ds(chunk, 8), :] = value
            partial = (partial[0] + perm, partial[1] + poro)
        return partial

    zero = (jnp.zeros((8, depth), jnp.float32),) * 2
    from_left = left_changes_soon if over_chips else left_changes
    from_right = functools.partial(right_changes_soon if over_chips else right_changes, last=last)
    return lax.cond(
        left,
        lambda: fill(from_left, zero),
        lambda: lax.cond(right, lambda: fill(from_right, zero), lambda: zero),
    )


def sides(over_chips):
    place = lax.axis_index("gx")
    odd = lax.rem(place, 2) == 1
    if over_chips:
        return jnp.logical_and(jnp.logical_not(odd), place > 0), jnp.logical_and(
            odd, place < lax.axis_size("gx") - 1
        )
    return odd, jnp.logical_not(odd)


def core_kernel(
    sizes, sums_in, weights, sent_a, sent_b, got_a, got_b, vel_ref, stress_ref, changes, sums
):
    rows = sizes[1]
    sent, got = (sent_a, sent_b), (got_a, got_b)
    perm, poro = side_sums(sizes, False, weights, sent, None, got, vel_ref, stress_ref, changes)
    sums[pl.ds(0, rows), :] = sums_in[pl.ds(0, rows), :] + perm
    sums[pl.ds(rows, rows), :] = sums_in[pl.ds(rows, rows), :] + poro


def chip_kernel(
    sizes, normalizer, sums, weights, sent, late, got, vel_ref, stress_ref, changes, totals
):
    rows = sizes[1]
    vel = load_coeffs(vel_ref)
    stress = load_coeffs(stress_ref)
    perm, poro = side_sums(sizes, True, weights, (sent,), late, (got,), vel_ref, stress_ref, changes)
    perm = jnp.sum(sums[pl.ds(0, rows), :] + perm, axis=0, keepdims=True)
    poro = jnp.sum(sums[pl.ds(rows, rows), :] + poro, axis=0, keepdims=True)
    totals[pl.ds(0, 1), :] = perm * (vel[2] * vel[3] * normalizer)
    totals[pl.ds(1, 1), :] = poro * (stress[3] * normalizer)


def finish_kernel(
    sizes, given, changes_core, changes_chip, late, vel_ref, stress_ref, changed, out_hbm, done, sems
):
    events, rows, depth, _, _ = sizes
    state_in = given.reshape(FIELDS, events * rows, depth)
    state = changed.reshape(FIELDS, events * rows, depth)
    vel = load_coeffs(vel_ref)
    stress = load_coeffs(stress_ref)
    last = rows - 1
    left_places = [(s + f, row) for s in (0, 4) for row in (0, 1) for f in range(4)]
    right_places = [(f, last) for f in range(4)] + [(4 + f, row) for row in (last - 1, last) for f in range(4)]
    got = [late[pl.ds(i * events, events), :] for i in range(LATE)]

    def left_late():
        push = vel[0] * got[0] + vel[1] * got[1] + changes_chip[len(left_places)]
        stresses = stress_gain(stress, push, 0.0, 0.0, depth_upper(-push))
        return {(VX, 0): -push} | {(SXX + f, 0): stresses[f] for f in range(4)}

    def right_late():
        again = [got[i] + changes_chip[len(right_places) + i] for i in range(LATE)]
        stresses = beyond_gain(stress, *again)
        return {(SXX + f, last): stresses[f] for f in range(4)}

    def patch(changes, places, fields, more):
        added = more() if more else {}
        for i, (field, row) in enumerate(places):
            if field in fields:
                at = pl.ds(row, events, stride=rows)
                value = changes[i]
                if (field, row) in added:
                    value = value + added[field, row]
                state[field, at, :] = state_in[field, at, :] + value

    half = FIELDS // 2
    copies = []
    for i in range(2):
        fields = range(i * half, (i + 1) * half)
        for over_chips, changes in ((False, changes_core), (True, changes_chip)):
            left, right = sides(over_chips)
            pl.when(left)(
                functools.partial(patch, changes, left_places, fields, left_late if over_chips else None)
            )
            pl.when(right)(
                functools.partial(patch, changes, right_places, fields, right_late if over_chips else None)
            )
        own = pl.ds(i * half * events, half * events)
        copies.append(pltpu.make_async_copy(changed.at[own], out_hbm.at[own], sems.at[i]))
        copies[i].start()
    done[...] = jnp.zeros_like(done)
    for copy in copies:
        copy.wait()


def swap_with(value, size, mask):
    return lax.ppermute(value, "gx", [(i, i ^ mask) for i in range(size)])


def swap_over_chips(value, groups, size):
    route = []
    for group in range(groups):
        base = group * size
        other = (group ^ 1) * size
        for i in range(1, size - 1, 2):
            route += [(base + i, base + i + 1), (base + i + 1, base + i)]
        route += [(base, other), (base + size - 1, other + size - 1)]
    return lax.ppermute(value, ("groups", "gx"), route)


def shards(
    adjoint_state, forward_fields, vel_coeffs, stress_coeffs, drm_cells, drm_force, source_id
):
    fields, events, rows, depth = adjoint_state.shape
    steps = forward_fields.shape[0]
    sources = drm_force.shape[0]
    entries = drm_cells.shape[0]
    size = lax.axis_size("gx")
    groups = lax.axis_size("groups")
    sizes = (events, rows, depth, steps, sources)
    blocks = entries // 128
    tiles = events * rows
    f32 = jnp.float32
    any_space = pl.BlockSpec(memory_space=pl.ANY)
    vmem = pl.BlockSpec(memory_space=pltpu.VMEM)
    smem = pl.BlockSpec(memory_space=pltpu.SMEM)
    state = adjoint_state.reshape(fields * events, rows, depth)
    forward = forward_fields.reshape(steps * 3, tiles, depth)
    cells = drm_cells.reshape(blocks, 128)
    force = drm_force.reshape(sources * steps, 2, blocks, 128).transpose(0, 2, 1, 3)
    force = force.reshape(sources * steps * 2 * blocks, 128)
    soon = pltpu.VMEM((SOON * events, depth), f32)
    late = pltpu.VMEM((LATE * events, depth), f32)
    half = pltpu.VMEM((HALO // 2 * events, depth), f32)
    limits = pltpu.CompilerParams(vmem_limit_bytes=ROOM)

    def kept(space, *values):
        return tuple(pltpu.with_memory_space_constraint(v, space) for v in values)

    (
        state,
        forward,
        source,
        table,
        message_first,
        message_second,
        message_chip,
        message_late,
        vel,
        stress,
    ) = pl.pallas_call(
        functools.partial(edge_kernel, sizes),
        out_shape=(
            pltpu.VMEM(state.shape, f32),
            pltpu.VMEM(forward.shape, forward.dtype),
            pltpu.SMEM((events,), jnp.int32),
            pltpu.VMEM(force.shape, f32),
            half,
            half,
            soon,
            late,
            pltpu.VMEM(vel_coeffs.shape, f32),
            pltpu.VMEM(stress_coeffs.shape, f32),
        ),
        in_specs=[any_space] * 7,
        out_specs=(vmem, vmem, smem) + (vmem,) * 7,
        scratch_shapes=[
            pltpu.VMEM((tiles, depth), f32),
            pltpu.VMEM(cells.shape, jnp.int32),
            pltpu.VMEM(force.shape, f32),
            pltpu.VMEM(force.shape, f32),
            pltpu.VMEM((tiles, depth), f32),
            pltpu.SemaphoreType.DMA((5,)),
        ],
        compiler_params=limits,
        name="edges",
    )(
        *kept(
            pltpu.HBM,
            state,
            forward,
            vel_coeffs,
            stress_coeffs,
            cells,
            force,
            source_id,
        )
    )

    got_first = swap_with(message_first, size, 1)
    got_second = swap_with(message_second, size, 1)
    got_chip = swap_over_chips(message_chip, groups, size)

    state, weights, sums, message_late = pl.pallas_call(
        functools.partial(bulk_kernel, sizes),
        out_shape=(
            pltpu.VMEM(state.shape, f32),
            pltpu.VMEM(forward.shape, f32),
            pltpu.VMEM((2 * rows, depth), f32),
            late,
        ),
        in_specs=[vmem] * 2 + [smem] + [vmem] * 4,
        out_specs=(vmem,) * 4,
        input_output_aliases={0: 0, 6: 3},
        scratch_shapes=[pltpu.VMEM((steps * 2 * sources * rows, depth), f32)],
        compiler_params=limits,
        cost_estimate=pl.CostEstimate(
            flops=steps * 80 * tiles * depth, bytes_accessed=8 * state.size, transcendentals=0
        ),
        name="bulk",
    )(
        *kept(pltpu.VMEM, state, forward),
        *kept(pltpu.SMEM, source),
        *kept(pltpu.VMEM, table, vel, stress, message_late),
    )
    got_late = swap_over_chips(message_late, groups, size)

    normalizer = (events * rows * size) ** (-0.5)
    changed = pltpu.VMEM((17, events, depth), f32)
    changes_core, sums = pl.pallas_call(
        functools.partial(core_kernel, sizes),
        out_shape=(changed, pltpu.VMEM(sums.shape, f32)),
        in_specs=[vmem] * 8,
        out_specs=(vmem,) * 2,
        compiler_params=limits,
        name="join_core",
    )(
        *kept(
            pltpu.VMEM,
            sums,
            weights,
            message_first,
            message_second,
            got_first,
            got_second,
            vel,
            stress,
        )
    )

    changes_chip, totals = pl.pallas_call(
        functools.partial(chip_kernel, sizes, normalizer),
        out_shape=(changed, pltpu.VMEM((2, depth), f32)),
        in_specs=[vmem] * 7,
        out_specs=(vmem,) * 2,
        compiler_params=limits,
        name="join_chip",
    )(*kept(pltpu.VMEM, sums, weights, message_chip, message_late, got_chip, vel, stress))

    _, out, done = pl.pallas_call(
        functools.partial(finish_kernel, sizes),
        out_shape=(
            pltpu.VMEM(state.shape, f32),
            jax.ShapeDtypeStruct(state.shape, f32),
            pltpu.VMEM((2, depth), f32),
        ),
        in_specs=[vmem] * 6,
        out_specs=(vmem, any_space, vmem),
        input_output_aliases={0: 0},
        scratch_shapes=[pltpu.SemaphoreType.DMA((2,))],
        compiler_params=limits,
        cost_estimate=pl.CostEstimate(flops=0, bytes_accessed=2 * 4 * state.size, transcendentals=0),
        name="finish",
    )(*kept(pltpu.VMEM, state, changes_core, changes_chip, got_late, vel, stress))

    mask = 1
    while mask < size:
        totals = totals + swap_with(totals, size, mask | 1)
        if mask * 4 == size:
            totals = totals + done
        mask *= 2
    return out.reshape(adjoint_state.shape), totals


def solution(mesh):
    in_specs = (
        P(None, "groups", "gx", None),
        P(None, None, "groups", "gx", None),
        P("groups", None),
        P("groups", None),
        P("gx"),
        P("groups", None, None, "gx"),
        P("groups"),
    )
    out_specs = (P(None, "groups", "gx", None), P("groups", None))
    return jax.shard_map(shards, mesh=mesh, in_specs=in_specs, out_specs=out_specs, check_vma=False)
```

```python
import functools

import jax
import jax.numpy as jnp
from jax import lax
from jax.experimental import pallas as pl
from jax.experimental.pallas import tpu as pltpu
from jax.sharding import PartitionSpec as P

LAYER = 8
FIELDS = 8
VX, VZ, QX, QZ, SXX, SZZ, SXZ, PR = range(FIELDS)
HALO = 6
SOON = 5
LATE = 2
PUSHED = ((0, 0), (0, 1), (1, 0), (0, -1))
GROUPS = (16, 8, 4, 2)
ROOM = 16 << 20


def depth_lower(values):
    lane = lax.broadcasted_iota(jnp.int32, values.shape, 1)
    return values - jnp.where(lane == 0, 0.0, pltpu.roll(values, 1, 1))


def depth_upper(values):
    depth = values.shape[1]
    lane = lax.broadcasted_iota(jnp.int32, values.shape, 1)
    return jnp.where(lane == depth - 1, 0.0, pltpu.roll(values, depth - 1, 1)) - values


def row_lower(values):
    row = lax.broadcasted_iota(jnp.int32, values.shape, 0)
    return values - jnp.where(row == 0, 0.0, pltpu.roll(values, 1, 0))


def row_upper(values):
    rows = values.shape[0]
    row = lax.broadcasted_iota(jnp.int32, values.shape, 0)
    return jnp.where(row == rows - 1, 0.0, pltpu.roll(values, rows - 1, 0)) - values


def velocity_gain(coeffs, force_x, force_z, push_x, push_z):
    solid, couple, fluid, _ = coeffs
    return (
        solid * force_x + couple * push_x,
        solid * force_z + couple * push_z,
        -couple * force_x - fluid * push_x,
        -couple * force_z - fluid * push_z,
    )


def stress_gain(coeffs, strain_x, strain_z, inflow, shear):
    lame, modulus, coupling, fluid = coeffs
    dilation = strain_x + strain_z
    common = lame * dilation - coupling * inflow
    return (
        common + 2.0 * modulus * strain_x,
        common + 2.0 * modulus * strain_z,
        modulus * shear,
        -coupling * dilation - fluid * inflow,
    )


def beyond_gain(coeffs, vel_x, vel_z, flow_x):
    lame, modulus, coupling, fluid = coeffs
    return (
        (lame + 2.0 * modulus) * vel_x - coupling * flow_x,
        lame * vel_x - coupling * flow_x,
        modulus * vel_z,
        -coupling * vel_x - fluid * flow_x,
    )


def plus(left, right):
    return tuple(a + b for a, b in zip(left, right))


def minus(left, right):
    return tuple(a - b for a, b in zip(left, right))


def load_coeffs(ref):
    return tuple(ref[pl.ds(i, 1), :] for i in range(4))


def at_row(layers, row, depth):
    lane = lax.broadcasted_iota(jnp.int32, layers.shape, 1)
    moved = pltpu.roll(layers, (depth - LAYER - LAYER * row) % depth, 1)
    return jnp.where(lane >= depth - LAYER, moved, 0.0)


def exact_pieces(values):
    pieces = []
    for _ in range(3):
        pieces.append(values.astype(jnp.bfloat16))
        values = values - pieces[-1].astype(jnp.float32)
    return pieces


def edge_kernel(
    sizes,
    state_hbm,
    forward_hbm,
    vel_hbm,
    stress_hbm,
    cells_hbm,
    force_hbm,
    source_hbm,
    near,
    forward,
    source,
    table_ref,
    message_first,
    message_second,
    message_chip,
    message_late,
    vel_ref,
    stress_ref,
    weights,
    cells,
    force,
    near_force,
    pushes,
    sems,
):
    events, rows, depth, steps, sources = sizes
    final_kind = steps * 3 - 1
    copies = [
        pltpu.make_async_copy(src, dst, sems.at[min(i, 3) if i < 8 else 4])
        for i, (src, dst) in enumerate(
            [
                (cells_hbm, cells),
                (force_hbm, force),
                (source_hbm, source),
                (vel_hbm, vel_ref),
                (stress_hbm, stress_ref),
                (state_hbm.at[:, pl.ds(0, 2)], near.at[:, pl.ds(0, 2)]),
                (state_hbm.at[:, pl.ds(rows - 2, 2)], near.at[:, pl.ds(rows - 2, 2)]),
                (forward_hbm.at[pl.ds(final_kind, 1)], forward.at[pl.ds(final_kind, 1)]),
                (state_hbm.at[:, pl.ds(2, rows - 4)], near.at[:, pl.ds(2, rows - 4)]),
                (forward_hbm.at[pl.ds(0, final_kind)], forward.at[pl.ds(0, final_kind)]),
            ]
        )
    ]
    for copy in copies:
        copy.start()
    copies[0].wait()
    copies[1].wait()
    lanes = cells.shape[1]
    local = cells[...] & (rows * depth - 1)
    slot = (local // depth) * LAYER + (local & (depth - 1)) - (depth - LAYER)
    blocks = cells.shape[0]
    spots = lax.broadcasted_iota(jnp.int32, (depth, lanes), 0)
    hits = [(spots == slot[i : i + 1, :]).astype(jnp.float32).astype(jnp.bfloat16) for i in range(blocks)]
    pieces = exact_pieces(force[...])
    terms = [
        lax.dot_general(
            jnp.concatenate(pieces, axis=0),
            hit,
            (((1,), (1,)), ((), ())),
            preferred_element_type=jnp.float32,
        )
        for hit in hits
    ]
    count = force.shape[0]
    terms = [t[:count] + t[count : 2 * count] + t[2 * count :] for t in terms]
    layers = terms[0]
    for block in range(1, blocks):
        layers = layers + pltpu.roll(terms[block], count - 2 * block, 0)
    table_ref[...] = layers
    def moved(row):
        return at_row(layers, row, depth)

    own = lax.broadcasted_iota(jnp.int32, layers.shape, 0) & (rows - 1)
    picked = jnp.where(own < 6, pltpu.roll(moved(1), 2, 0), pltpu.roll(moved(rows - 1), 6, 0))
    near_force[...] = jnp.where((own & 2) == 0, moved(0), picked)
    copies[2].wait()
    for event in range(events):
        record = pl.multiple_of(source[event] * rows, rows)
        pushes[pl.ds(event * rows, rows), :] = near_force[pl.ds(record, rows), :]
    def wait_tiles(index, count):
        own = near.at[pl.ds(0, count)]
        pltpu.make_async_copy(own, own, sems.at[index]).wait()

    kind_tiles = events // 2
    coeff_tiles = 2 * vel_ref.shape[0] // rows
    wait_tiles(3, FIELDS * events * 4 // rows + kind_tiles + coeff_tiles)
    weights[...] = forward[final_kind].astype(jnp.float32)
    vel = load_coeffs(vel_ref)
    stress = load_coeffs(stress_ref)
    odd = lax.rem(lax.axis_index("gx"), 2) == 1
    message_core = (message_first, message_second)
    last = rows - 1
    state = near.reshape(near.shape[0] * rows, depth)

    def rim(chunk, field, row):
        return state[pl.ds((field * events + chunk) * rows + row, 8, stride=rows), :]

    def pushed(chunk, step, part, row):
        at = PUSHED.index((step, row if row < last else -1)) * 2 + part
        return pushes[pl.ds(chunk * rows + at, 8, stride=rows), :]

    for chunk in range(0, events, 8):
        first = [rim(chunk, f, 0) for f in range(FIELDS)]
        second = [rim(chunk, f, 1) for f in range(FIELDS)]
        final = [rim(chunk, f, last) for f in range(FIELDS)]
        inner = {f: rim(chunk, f, last - 1) for f in (SXX, SXZ, PR)}

        def kicked(fields, gains, step, row):
            vel_x, vel_z, flow_x, flow_z = plus(fields, gains)
            return (
                vel_x + pushed(chunk, step, 0, row),
                vel_z + pushed(chunk, step, 1, row),
                flow_x,
                flow_z,
            )

        def forces(fields, before):
            return (
                fields[SXX] - before[SXX] + depth_lower(fields[SXZ]),
                fields[SXZ] - before[SXZ] + depth_lower(fields[SZZ]),
                fields[PR] - before[PR] + vel[3] * fields[QX],
                depth_lower(fields[PR]) + vel[3] * fields[QZ],
            )

        nothing = {SXX: 0.0, SXZ: 0.0, PR: 0.0}
        vel_first = kicked(first[:4], velocity_gain(vel, *forces(first, nothing)), 0, 0)
        vel_second = kicked(second[:4], velocity_gain(vel, *forces(second, first)), 0, 1)
        vel_final = kicked(final[:4], velocity_gain(vel, *forces(final, inner)), 0, last)
        stress_first = plus(
            first[4:],
            stress_gain(
                stress,
                vel_second[0] - vel_first[0],
                depth_upper(vel_first[1]),
                vel_second[2] - vel_first[2] + depth_upper(vel_first[3]),
                depth_upper(vel_first[0]) + vel_second[1] - vel_first[1],
            ),
        )
        stress_final = plus(
            final[4:],
            stress_gain(
                stress,
                -vel_final[0],
                depth_upper(vel_final[1]),
                -vel_final[2] + depth_upper(vel_final[3]),
                depth_upper(vel_final[0]) - vel_final[1],
            ),
        )
        again = kicked(
            vel_first,
            velocity_gain(vel, *forces(list(vel_first) + list(stress_first), nothing)),
            1,
            0,
        )
        right = [final[SXX], final[SXZ], final[PR], stress_final[0], stress_final[2], stress_final[3]]
        left = [vel_first[0], vel_first[1], vel_first[2], again[0], again[1], again[2]]
        for i in range(HALO):
            half = message_core[i // 3]
            half[pl.ds(i % 3 * events + chunk, 8), :] = jnp.where(odd, left[i], right[i])
        flow = vel[1] * stress_final[0] + vel[2] * stress_final[3]
        drain = stress[2] * again[0] + stress[3] * again[2]
        weight = weights[pl.ds(chunk * rows, 8, stride=rows), :]
        right_soon = right[:3] + [flow, stress_final[2]]
        left_soon = left[:3] + [drain, weight]
        right_late = [stress_final[0], stress_final[3]]
        for i in range(SOON):
            message_chip[pl.ds(i * events + chunk, 8), :] = jnp.where(odd, right_soon[i], left_soon[i])
        for i in range(LATE):
            message_late[pl.ds(i * events + chunk, 8), :] = jnp.where(odd, right_late[i], left[3 + i])
    wait_tiles(4, FIELDS * events * (rows - 4) // rows + final_kind * kind_tiles)


def group_of(events):
    return next(g for g in GROUPS if events % g == 0)


def bulk_kernel(
    sizes,
    given,
    forward,
    source,
    table_ref,
    vel_ref,
    stress_ref,
    late_in,
    changed,
    weights,
    sums,
    late,
    by_source,
):
    events, rows, depth, steps, sources = sizes
    group = group_of(events)
    state_in = given.reshape(FIELDS, events * rows, depth)
    state = changed.reshape(FIELDS, events * rows, depth)
    each = table_ref.shape[0] // sources
    for step in range(steps):
        for part in range(2):
            layers = table_ref[pl.ds(step * (each // steps) + part, sources, stride=each), :]
            for row in range(rows):
                at = (step * 2 + part) * sources * rows + row
                by_source[pl.ds(at, sources, stride=rows), :] = at_row(layers, row, depth)
    vel = tuple(jnp.broadcast_to(c, (rows, depth)) for c in load_coeffs(vel_ref))
    stress = tuple(jnp.broadcast_to(c, (rows, depth)) for c in load_coeffs(stress_ref))

    def body(i, carry):
        perm, poro = carry

        def tile(sub, count=1):
            at = (i * group + sub) * rows
            return pl.ds(pl.multiple_of(at, count * rows), count * rows)

        def pushed(step, part, sub):
            at = ((step * 2 + part) * sources + source[i * group + sub]) * rows
            return by_source[pl.ds(pl.multiple_of(at, rows), rows), :]

        fields = [[state_in[f, tile(sub), :] for f in range(FIELDS)] for sub in range(group)]
        for step in range(steps):
            factors = [[] for _ in range(group)]
            for kind in range(3):
                for sub in range(0, group, 2):
                    both = forward[step * 3 + kind, tile(sub, 2), :].astype(jnp.float32)
                    for half in range(2):
                        value = both[half * rows : (half + 1) * rows]
                        weights[step * 3 + kind, tile(sub + half), :] = value
                        factors[sub + half].append(value)
            for sub, own in enumerate(fields):
                gains = velocity_gain(
                    vel,
                    row_lower(own[SXX]) + depth_lower(own[SXZ]),
                    row_lower(own[SXZ]) + depth_lower(own[SZZ]),
                    row_lower(own[PR]) + vel[3] * own[QX],
                    depth_lower(own[PR]) + vel[3] * own[QZ],
                )
                own[:4] = plus(own[:4], gains)
                own[VX] = own[VX] + pushed(step, 0, sub)
                own[VZ] = own[VZ] + pushed(step, 1, sub)
                perm = perm + own[QX] * factors[sub][0] + own[QZ] * factors[sub][1]
            for sub, own in enumerate(fields):
                own[4:] = plus(
                    own[4:],
                    stress_gain(
                        stress,
                        row_upper(own[VX]),
                        depth_upper(own[VZ]),
                        row_upper(own[QX]) + depth_upper(own[QZ]),
                        depth_upper(own[VX]) + row_upper(own[VZ]),
                    ),
                )
                poro = poro + own[PR] * factors[sub][2]
        for sub, own in enumerate(fields):
            for f in range(FIELDS):
                state[f, tile(sub), :] = own[f]
        return perm, poro

    zero = jnp.zeros((rows, depth), jnp.float32)
    perm, poro = lax.fori_loop(0, events // group, body, (zero, zero))
    sums[pl.ds(0, rows), :] = perm
    sums[pl.ds(rows, rows), :] = poro


def from_before(vel, stress_x, stress_xz, pressure):
    return velocity_gain(vel, -stress_x, -stress_xz, -pressure, 0.0)


def forces(vel, stresses, flows):
    return (
        stresses[0] + depth_lower(stresses[2]),
        stresses[2] + depth_lower(stresses[1]),
        stresses[3] + vel[3] * flows[0],
        depth_lower(stresses[3]) + vel[3] * flows[1],
    )


def strains(stress, vels, after):
    return stress_gain(
        stress,
        after[0] - vels[0],
        depth_upper(vels[1]),
        after[2] - vels[2] + depth_upper(vels[3]),
        depth_upper(vels[0]) + after[1] - vels[1],
    )


NOTHING = (0.0, 0.0, 0.0)


def left_changes(vel, stress, sent, got, factor):
    gain_first = from_before(vel, *got[:3])
    before = beyond_gain(stress, *plus(sent[:3], gain_first[:3]))
    before = plus(got[3:], (before[0], before[2], before[3]))
    stress_first = strains(stress, gain_first, NOTHING)
    vel_first = plus(
        plus(gain_first, velocity_gain(vel, *forces(vel, stress_first, gain_first[2:]))),
        from_before(vel, *before),
    )
    vel_second = from_before(vel, stress_first[0], stress_first[2], stress_first[3])
    end_first = plus(stress_first, strains(stress, vel_first, vel_second))
    end_second = strains(stress, vel_second, NOTHING)
    perm = gain_first[2] * factor(0, 0, 0) + gain_first[3] * factor(0, 1, 0)
    for row, vels in ((0, vel_first), (1, vel_second)):
        perm = perm + vels[2] * factor(1, 0, row) + vels[3] * factor(1, 1, row)
    poro = stress_first[3] * factor(0, 2, 0)
    for row, stresses in ((0, end_first), (1, end_second)):
        poro = poro + stresses[3] * factor(1, 2, row)
    return vel_first + vel_second + end_first + end_second, perm, poro


def right_changes(vel, stress, sent, got, factor, last):
    gain_after = from_before(vel, *sent[:3])
    stress_last = beyond_gain(stress, *plus(got[:3], gain_after[:3]))
    true_last = plus(sent[3:], (stress_last[0], stress_last[2], stress_last[3]))
    vel_last = velocity_gain(
        vel,
        stress_last[0] + depth_lower(stress_last[2]),
        stress_last[2] + depth_lower(stress_last[1]),
        stress_last[3],
        depth_lower(stress_last[3]),
    )
    stress_after = strains(stress, gain_after, NOTHING)
    again = plus(
        plus(gain_after, velocity_gain(vel, *forces(vel, stress_after, gain_after[2:]))),
        from_before(vel, *true_last),
    )
    again = plus(got[3:], again[:3])
    end_inner = beyond_gain(stress, *vel_last[:3])
    end_last = plus(stress_last, strains(stress, vel_last, again))
    perm = vel_last[2] * factor(1, 0, last) + vel_last[3] * factor(1, 1, last)
    poro = stress_last[3] * factor(0, 2, last)
    for row, stresses in ((last - 1, end_inner), (last, end_last)):
        poro = poro + stresses[3] * factor(1, 2, row)
    return vel_last + end_inner + end_last, perm, poro


def left_changes_soon(vel, stress, sent, own_late, got, factor):
    gain_first = from_before(vel, *got[:3])
    beyond = beyond_gain(stress, *plus(sent[:3], gain_first[:3]))
    flow = got[3] + vel[1] * beyond[0] + vel[2] * beyond[3]
    shear = got[4] + beyond[2]
    stress_first = strains(stress, gain_first, NOTHING)
    vel_first = plus(gain_first, velocity_gain(vel, *forces(vel, stress_first, gain_first[2:])))
    vel_first = plus(vel_first, (0.0, -vel[0] * shear, flow, vel[1] * shear))
    vel_second = from_before(vel, stress_first[0], stress_first[2], stress_first[3])
    end_first = plus(stress_first, strains(stress, vel_first, vel_second))
    end_second = strains(stress, vel_second, NOTHING)
    perm = gain_first[2] * factor(0, 0, 0) + gain_first[3] * factor(0, 1, 0)
    for row, vels in ((0, vel_first), (1, vel_second)):
        perm = perm + vels[2] * factor(1, 0, row) + vels[3] * factor(1, 1, row)
    poro = stress_first[3] * factor(0, 2, 0)
    for row, stresses in ((0, end_first), (1, end_second)):
        poro = poro + stresses[3] * factor(1, 2, row)
    rest = (vel[0] * beyond[0] + vel[1] * beyond[3],)
    return vel_first + vel_second + end_first + end_second + rest, perm, poro


def right_changes_soon(vel, stress, sent, own_late, got, factor, last):
    gain_after = from_before(vel, *sent[:3])
    stress_last = beyond_gain(stress, *plus(got[:3], gain_after[:3]))
    true_last = (own_late[0] + stress_last[0], sent[4] + stress_last[2], own_late[1] + stress_last[3])
    vel_last = velocity_gain(
        vel,
        stress_last[0] + depth_lower(stress_last[2]),
        stress_last[2] + depth_lower(stress_last[1]),
        stress_last[3],
        depth_lower(stress_last[3]),
    )
    stress_after = strains(stress, gain_after, NOTHING)
    again = plus(
        plus(gain_after, velocity_gain(vel, *forces(vel, stress_after, gain_after[2:]))),
        from_before(vel, *true_last),
    )
    drain = got[3] + stress[2] * again[0] + stress[3] * again[2]
    end_inner = beyond_gain(stress, *vel_last[:3])
    end_last = plus(stress_last, strains(stress, vel_last, NOTHING))
    perm = vel_last[2] * factor(1, 0, last) + vel_last[3] * factor(1, 1, last)
    poro = stress_last[3] * factor(0, 2, last)
    poro = poro + end_inner[3] * factor(1, 2, last - 1) + (end_last[3] - drain) * factor(1, 2, last)
    poro = poro - stress[2] * (vel[0] * true_last[0] + vel[1] * true_last[2]) * got[4]
    return vel_last + end_inner + end_last + again[:3], perm, poro


def side_sums(sizes, over_chips, weights, sent, own_late, got, vel_ref, stress_ref, changes):
    events, rows, depth, _, _ = sizes
    vel = load_coeffs(vel_ref)
    stress = load_coeffs(stress_ref)
    last = rows - 1
    left, right = sides(over_chips)
    count = SOON if over_chips else HALO

    def fill(changed, partial):
        for chunk in range(0, events, 8):

            def row_of(refs, i):
                each = count // len(refs)
                return refs[i // each][pl.ds(i % each * events + chunk, 8), :]

            def factor(step, kind, row):
                return weights[step * 3 + kind, pl.ds(chunk * rows + row, 8, stride=rows), :]

            own = tuple(row_of(sent, i) for i in range(count))
            new = tuple(row_of(got, i) for i in range(count))
            if over_chips:
                late = tuple(own_late[pl.ds(i * events + chunk, 8), :] for i in range(LATE))
                values, perm, poro = changed(vel, stress, own, late, new, factor)
            else:
                values, perm, poro = changed(vel, stress, own, new, factor)
            for i, value in enumerate(values):
                changes[i, pl.ds(chunk, 8), :] = value
            partial = (partial[0] + perm, partial[1] + poro)
        return partial

    zero = (jnp.zeros((8, depth), jnp.float32),) * 2
    from_left = left_changes_soon if over_chips else left_changes
    from_right = functools.partial(right_changes_soon if over_chips else right_changes, last=last)
    return lax.cond(
        left,
        lambda: fill(from_left, zero),
        lambda: lax.cond(right, lambda: fill(from_right, zero), lambda: zero),
    )


def sides(over_chips):
    place = lax.axis_index("gx")
    odd = lax.rem(place, 2) == 1
    if over_chips:
        return jnp.logical_and(jnp.logical_not(odd), place > 0), jnp.logical_and(
            odd, place < lax.axis_size("gx") - 1
        )
    return odd, jnp.logical_not(odd)


def core_kernel(
    sizes, sums_in, weights, sent_a, sent_b, got_a, got_b, vel_ref, stress_ref, changes, sums
):
    rows = sizes[1]
    sent, got = (sent_a, sent_b), (got_a, got_b)
    perm, poro = side_sums(sizes, False, weights, sent, None, got, vel_ref, stress_ref, changes)
    sums[pl.ds(0, rows), :] = sums_in[pl.ds(0, rows), :] + perm
    sums[pl.ds(rows, rows), :] = sums_in[pl.ds(rows, rows), :] + poro


def chip_kernel(
    sizes, normalizer, sums, weights, sent, late, got, vel_ref, stress_ref, changes, totals
):
    rows = sizes[1]
    vel = load_coeffs(vel_ref)
    stress = load_coeffs(stress_ref)
    perm, poro = side_sums(sizes, True, weights, (sent,), late, (got,), vel_ref, stress_ref, changes)
    perm = jnp.sum(sums[pl.ds(0, rows), :] + perm, axis=0, keepdims=True)
    poro = jnp.sum(sums[pl.ds(rows, rows), :] + poro, axis=0, keepdims=True)
    totals[pl.ds(0, 1), :] = perm * (vel[2] * vel[3] * normalizer)
    totals[pl.ds(1, 1), :] = poro * (stress[3] * normalizer)


def finish_kernel(
    sizes, given, changes_core, changes_chip, soon, late, vel_ref, stress_ref, changed, out_hbm, done, sems
):
    events, rows, depth, _, _ = sizes
    state_in = given.reshape(FIELDS, events * rows, depth)
    state = changed.reshape(FIELDS, events * rows, depth)
    vel = load_coeffs(vel_ref)
    stress = load_coeffs(stress_ref)
    last = rows - 1
    left_places = [(s + f, row) for s in (0, 4) for row in (0, 1) for f in range(4)]
    right_places = [(f, last) for f in range(4)] + [(4 + f, row) for row in (last - 1, last) for f in range(4)]
    got = [late[pl.ds(i * events, events), :] for i in range(LATE)]

    def left_late():
        push = vel[0] * got[0] + vel[1] * got[1] + changes_chip[len(left_places)]
        stresses = stress_gain(stress, push, 0.0, 0.0, depth_upper(-push))
        return {(VX, 0): -push} | {(SXX + f, 0): stresses[f] for f in range(4)}

    def right_late():
        drain = soon[pl.ds(3 * events, events), :]
        flow = (drain - stress[2] * got[0]) / stress[3]
        again = [value + changes_chip[len(right_places) + i] for i, value in enumerate((*got, flow))]
        stresses = beyond_gain(stress, *again)
        return {(SXX + f, last): stresses[f] for f in range(4)}

    def patch(changes, places, fields, more):
        added = more() if more else {}
        for i, (field, row) in enumerate(places):
            if field in fields:
                at = pl.ds(row, events, stride=rows)
                value = changes[i]
                if (field, row) in added:
                    value = value + added[field, row]
                state[field, at, :] = state_in[field, at, :] + value

    half = FIELDS // 2
    copies = []
    for i in range(2):
        fields = range(i * half, (i + 1) * half)
        for over_chips, changes in ((False, changes_core), (True, changes_chip)):
            left, right = sides(over_chips)
            pl.when(left)(
                functools.partial(patch, changes, left_places, fields, left_late if over_chips else None)
            )
            pl.when(right)(
                functools.partial(patch, changes, right_places, fields, right_late if over_chips else None)
            )
        own = pl.ds(i * half * events, half * events)
        copies.append(pltpu.make_async_copy(changed.at[own], out_hbm.at[own], sems.at[i]))
        copies[i].start()
    done[...] = jnp.zeros_like(done)
    for copy in copies:
        copy.wait()


def swap_with(value, size, mask):
    return lax.ppermute(value, "gx", [(i, i ^ mask) for i in range(size)])


def swap_over_chips(value, groups, size):
    route = []
    for group in range(groups):
        base = group * size
        other = (group ^ 1) * size
        for i in range(1, size - 1, 2):
            route += [(base + i, base + i + 1), (base + i + 1, base + i)]
        route += [(base, other), (base + size - 1, other + size - 1)]
    return lax.ppermute(value, ("groups", "gx"), route)


def shards(
    adjoint_state, forward_fields, vel_coeffs, stress_coeffs, drm_cells, drm_force, source_id
):
    fields, events, rows, depth = adjoint_state.shape
    steps = forward_fields.shape[0]
    sources = drm_force.shape[0]
    entries = drm_cells.shape[0]
    size = lax.axis_size("gx")
    groups = lax.axis_size("groups")
    sizes = (events, rows, depth, steps, sources)
    blocks = entries // 128
    tiles = events * rows
    f32 = jnp.float32
    any_space = pl.BlockSpec(memory_space=pl.ANY)
    vmem = pl.BlockSpec(memory_space=pltpu.VMEM)
    smem = pl.BlockSpec(memory_space=pltpu.SMEM)
    state = adjoint_state.reshape(fields * events, rows, depth)
    forward = forward_fields.reshape(steps * 3, tiles, depth)
    cells = drm_cells.reshape(blocks, 128)
    force = drm_force.reshape(sources * steps, 2, blocks, 128).transpose(0, 2, 1, 3)
    force = force.reshape(sources * steps * 2 * blocks, 128)
    soon = pltpu.VMEM((SOON * events, depth), f32)
    late = pltpu.VMEM((LATE * events, depth), f32)
    half = pltpu.VMEM((HALO // 2 * events, depth), f32)
    limits = pltpu.CompilerParams(vmem_limit_bytes=ROOM)

    def kept(space, *values):
        return tuple(pltpu.with_memory_space_constraint(v, space) for v in values)

    (
        state,
        forward,
        source,
        table,
        message_first,
        message_second,
        message_chip,
        message_late,
        vel,
        stress,
    ) = pl.pallas_call(
        functools.partial(edge_kernel, sizes),
        out_shape=(
            pltpu.VMEM(state.shape, f32),
            pltpu.VMEM(forward.shape, forward.dtype),
            pltpu.SMEM((events,), jnp.int32),
            pltpu.VMEM(force.shape, f32),
            half,
            half,
            soon,
            late,
            pltpu.VMEM(vel_coeffs.shape, f32),
            pltpu.VMEM(stress_coeffs.shape, f32),
        ),
        in_specs=[any_space] * 7,
        out_specs=(vmem, vmem, smem) + (vmem,) * 7,
        scratch_shapes=[
            pltpu.VMEM((tiles, depth), f32),
            pltpu.VMEM(cells.shape, jnp.int32),
            pltpu.VMEM(force.shape, f32),
            pltpu.VMEM(force.shape, f32),
            pltpu.VMEM((tiles, depth), f32),
            pltpu.SemaphoreType.DMA((5,)),
        ],
        compiler_params=limits,
        name="edges",
    )(
        *kept(
            pltpu.HBM,
            state,
            forward,
            vel_coeffs,
            stress_coeffs,
            cells,
            force,
            source_id,
        )
    )

    got_first = swap_with(message_first, size, 1)
    got_second = swap_with(message_second, size, 1)
    got_chip = swap_over_chips(message_chip, groups, size)

    state, weights, sums, message_late = pl.pallas_call(
        functools.partial(bulk_kernel, sizes),
        out_shape=(
            pltpu.VMEM(state.shape, f32),
            pltpu.VMEM(forward.shape, f32),
            pltpu.VMEM((2 * rows, depth), f32),
            late,
        ),
        in_specs=[vmem] * 2 + [smem] + [vmem] * 4,
        out_specs=(vmem,) * 4,
        input_output_aliases={0: 0, 6: 3},
        scratch_shapes=[pltpu.VMEM((steps * 2 * sources * rows, depth), f32)],
        compiler_params=limits,
        cost_estimate=pl.CostEstimate(
            flops=steps * 80 * tiles * depth, bytes_accessed=8 * state.size, transcendentals=0
        ),
        name="bulk",
    )(
        *kept(pltpu.VMEM, state, forward),
        *kept(pltpu.SMEM, source),
        *kept(pltpu.VMEM, table, vel, stress, message_late),
    )
    got_late = swap_over_chips(message_late, groups, size)

    normalizer = (events * rows * size) ** (-0.5)
    changed = pltpu.VMEM((17, events, depth), f32)
    changes_core, sums = pl.pallas_call(
        functools.partial(core_kernel, sizes),
        out_shape=(changed, pltpu.VMEM(sums.shape, f32)),
        in_specs=[vmem] * 8,
        out_specs=(vmem,) * 2,
        compiler_params=limits,
        name="join_core",
    )(
        *kept(
            pltpu.VMEM,
            sums,
            weights,
            message_first,
            message_second,
            got_first,
            got_second,
            vel,
            stress,
        )
    )

    changes_chip, totals = pl.pallas_call(
        functools.partial(chip_kernel, sizes, normalizer),
        out_shape=(changed, pltpu.VMEM((2, depth), f32)),
        in_specs=[vmem] * 7,
        out_specs=(vmem,) * 2,
        compiler_params=limits,
        name="join_chip",
    )(*kept(pltpu.VMEM, sums, weights, message_chip, message_late, got_chip, vel, stress))

    _, out, done = pl.pallas_call(
        functools.partial(finish_kernel, sizes),
        out_shape=(
            pltpu.VMEM(state.shape, f32),
            jax.ShapeDtypeStruct(state.shape, f32),
            pltpu.VMEM((2, depth), f32),
        ),
        in_specs=[vmem] * 7,
        out_specs=(vmem, any_space, vmem),
        input_output_aliases={0: 0},
        scratch_shapes=[pltpu.SemaphoreType.DMA((2,))],
        compiler_params=limits,
        cost_estimate=pl.CostEstimate(flops=0, bytes_accessed=2 * 4 * state.size, transcendentals=0),
        name="finish",
    )(*kept(pltpu.VMEM, state, changes_core, changes_chip, got_chip, got_late, vel, stress))

    mask = 1
    while mask < size:
        totals = totals + swap_with(totals, size, mask | 1)
        if mask * 4 == size:
            totals = totals + done
        mask *= 2
    return out.reshape(adjoint_state.shape), totals


def solution(mesh):
    in_specs = (
        P(None, "groups", "gx", None),
        P(None, None, "groups", "gx", None),
        P("groups", None),
        P("groups", None),
        P("gx"),
        P("groups", None, None, "gx"),
        P("groups"),
    )
    out_specs = (P(None, "groups", "gx", None), P("groups", None))
    return jax.shard_map(shards, mesh=mesh, in_specs=in_specs, out_specs=out_specs, check_vma=False)
```

```python
import functools

import jax
import jax.numpy as jnp
from jax import lax
from jax.experimental import pallas as pl
from jax.experimental.pallas import tpu as pltpu
from jax.sharding import PartitionSpec as P

LAYER = 8
FIELDS = 8
VX, VZ, QX, QZ, SXX, SZZ, SXZ, PR = range(FIELDS)
HALO = 6
SOON = 5
LATE = 3
PUSHED = ((0, 0), (0, 1), (1, 0), (0, -1))
GROUPS = (24, 16, 8, 4, 2)
ROOM = 16 << 20


def depth_lower(values):
    lane = lax.broadcasted_iota(jnp.int32, values.shape, 1)
    return values - jnp.where(lane == 0, 0.0, pltpu.roll(values, 1, 1))


def depth_upper(values):
    depth = values.shape[1]
    lane = lax.broadcasted_iota(jnp.int32, values.shape, 1)
    return jnp.where(lane == depth - 1, 0.0, pltpu.roll(values, depth - 1, 1)) - values


def row_lower(values):
    row = lax.broadcasted_iota(jnp.int32, values.shape, 0)
    return values - jnp.where(row == 0, 0.0, pltpu.roll(values, 1, 0))


def row_upper(values):
    rows = values.shape[0]
    row = lax.broadcasted_iota(jnp.int32, values.shape, 0)
    return jnp.where(row == rows - 1, 0.0, pltpu.roll(values, rows - 1, 0)) - values


def velocity_gain(coeffs, force_x, force_z, push_x, push_z):
    solid, couple, fluid, _ = coeffs
    return (
        solid * force_x + couple * push_x,
        solid * force_z + couple * push_z,
        -couple * force_x - fluid * push_x,
        -couple * force_z - fluid * push_z,
    )


def stress_gain(coeffs, strain_x, strain_z, inflow, shear):
    lame, modulus, coupling, fluid = coeffs
    dilation = strain_x + strain_z
    common = lame * dilation - coupling * inflow
    return (
        common + 2.0 * modulus * strain_x,
        common + 2.0 * modulus * strain_z,
        modulus * shear,
        -coupling * dilation - fluid * inflow,
    )


def beyond_gain(coeffs, vel_x, vel_z, flow_x):
    lame, modulus, coupling, fluid = coeffs
    return (
        (lame + 2.0 * modulus) * vel_x - coupling * flow_x,
        lame * vel_x - coupling * flow_x,
        modulus * vel_z,
        -coupling * vel_x - fluid * flow_x,
    )


def plus(left, right):
    return tuple(a + b for a, b in zip(left, right))


def minus(left, right):
    return tuple(a - b for a, b in zip(left, right))


def load_coeffs(ref):
    return tuple(ref[pl.ds(i, 1), :] for i in range(4))


def at_row(layers, row, depth):
    lane = lax.broadcasted_iota(jnp.int32, layers.shape, 1)
    moved = pltpu.roll(layers, (depth - LAYER - LAYER * row) % depth, 1)
    return jnp.where(lane >= depth - LAYER, moved, 0.0)


def exact_pieces(values):
    pieces = []
    for _ in range(3):
        pieces.append(values.astype(jnp.bfloat16))
        values = values - pieces[-1].astype(jnp.float32)
    return pieces


def edge_kernel(
    sizes,
    state_hbm,
    forward_hbm,
    vel_hbm,
    stress_hbm,
    cells_hbm,
    force_hbm,
    source_hbm,
    near,
    forward,
    source,
    table_ref,
    message_first,
    message_second,
    message_chip,
    message_late,
    vel_ref,
    stress_ref,
    weights,
    cells,
    force,
    near_force,
    pushes,
    sems,
):
    events, rows, depth, steps, sources = sizes
    final_kind = steps * 3 - 1
    copies = [
        pltpu.make_async_copy(src, dst, sems.at[min(i, 3) if i < 8 else 4])
        for i, (src, dst) in enumerate(
            [
                (cells_hbm, cells),
                (force_hbm, force),
                (source_hbm, source),
                (vel_hbm, vel_ref),
                (stress_hbm, stress_ref),
                (state_hbm.at[:, pl.ds(0, 2)], near.at[:, pl.ds(0, 2)]),
                (state_hbm.at[:, pl.ds(rows - 2, 2)], near.at[:, pl.ds(rows - 2, 2)]),
                (forward_hbm.at[pl.ds(final_kind, 1)], forward.at[pl.ds(final_kind, 1)]),
                (state_hbm.at[:, pl.ds(2, rows - 4)], near.at[:, pl.ds(2, rows - 4)]),
                (forward_hbm.at[pl.ds(0, final_kind)], forward.at[pl.ds(0, final_kind)]),
            ]
        )
    ]
    for copy in copies:
        copy.start()
    copies[0].wait()
    copies[1].wait()
    lanes = cells.shape[1]
    local = cells[...] & (rows * depth - 1)
    slot = (local // depth) * LAYER + (local & (depth - 1)) - (depth - LAYER)
    blocks = cells.shape[0]
    spots = lax.broadcasted_iota(jnp.int32, (depth, lanes), 0)
    hits = [(spots == slot[i : i + 1, :]).astype(jnp.float32).astype(jnp.bfloat16) for i in range(blocks)]
    pieces = exact_pieces(force[...])
    terms = [
        lax.dot_general(
            jnp.concatenate(pieces, axis=0),
            hit,
            (((1,), (1,)), ((), ())),
            preferred_element_type=jnp.float32,
        )
        for hit in hits
    ]
    count = force.shape[0]
    terms = [t[:count] + t[count : 2 * count] + t[2 * count :] for t in terms]
    layers = terms[0]
    for block in range(1, blocks):
        layers = layers + pltpu.roll(terms[block], count - 2 * block, 0)
    table_ref[...] = layers
    def moved(row):
        return at_row(layers, row, depth)

    own = lax.broadcasted_iota(jnp.int32, layers.shape, 0) & (rows - 1)
    picked = jnp.where(own < 6, pltpu.roll(moved(1), 2, 0), pltpu.roll(moved(rows - 1), 6, 0))
    near_force[...] = jnp.where((own & 2) == 0, moved(0), picked)
    copies[2].wait()
    for event in range(events):
        record = pl.multiple_of(source[event] * rows, rows)
        pushes[pl.ds(event * rows, rows), :] = near_force[pl.ds(record, rows), :]
    def wait_tiles(index, count):
        own = near.at[pl.ds(0, count)]
        pltpu.make_async_copy(own, own, sems.at[index]).wait()

    kind_tiles = events // 2
    coeff_tiles = 2 * vel_ref.shape[0] // rows
    wait_tiles(3, FIELDS * events * 4 // rows + kind_tiles + coeff_tiles)
    weights[...] = forward[final_kind].astype(jnp.float32)
    vel = load_coeffs(vel_ref)
    stress = load_coeffs(stress_ref)
    odd = lax.rem(lax.axis_index("gx"), 2) == 1
    message_core = (message_first, message_second)
    last = rows - 1
    state = near.reshape(near.shape[0] * rows, depth)

    def rim(chunk, field, row):
        return state[pl.ds((field * events + chunk) * rows + row, 8, stride=rows), :]

    def pushed(chunk, step, part, row):
        at = PUSHED.index((step, row if row < last else -1)) * 2 + part
        return pushes[pl.ds(chunk * rows + at, 8, stride=rows), :]

    for chunk in range(0, events, 8):
        first = [rim(chunk, f, 0) for f in range(FIELDS)]
        second = [rim(chunk, f, 1) for f in range(FIELDS)]
        final = [rim(chunk, f, last) for f in range(FIELDS)]
        inner = {f: rim(chunk, f, last - 1) for f in (SXX, SXZ, PR)}

        def kicked(fields, gains, step, row):
            vel_x, vel_z, flow_x, flow_z = plus(fields, gains)
            return (
                vel_x + pushed(chunk, step, 0, row),
                vel_z + pushed(chunk, step, 1, row),
                flow_x,
                flow_z,
            )

        def forces(fields, before):
            return (
                fields[SXX] - before[SXX] + depth_lower(fields[SXZ]),
                fields[SXZ] - before[SXZ] + depth_lower(fields[SZZ]),
                fields[PR] - before[PR] + vel[3] * fields[QX],
                depth_lower(fields[PR]) + vel[3] * fields[QZ],
            )

        nothing = {SXX: 0.0, SXZ: 0.0, PR: 0.0}
        vel_first = kicked(first[:4], velocity_gain(vel, *forces(first, nothing)), 0, 0)
        vel_second = kicked(second[:4], velocity_gain(vel, *forces(second, first)), 0, 1)
        vel_final = kicked(final[:4], velocity_gain(vel, *forces(final, inner)), 0, last)
        stress_first = plus(
            first[4:],
            stress_gain(
                stress,
                vel_second[0] - vel_first[0],
                depth_upper(vel_first[1]),
                vel_second[2] - vel_first[2] + depth_upper(vel_first[3]),
                depth_upper(vel_first[0]) + vel_second[1] - vel_first[1],
            ),
        )
        stress_final = plus(
            final[4:],
            stress_gain(
                stress,
                -vel_final[0],
                depth_upper(vel_final[1]),
                -vel_final[2] + depth_upper(vel_final[3]),
                depth_upper(vel_final[0]) - vel_final[1],
            ),
        )
        again = kicked(
            vel_first,
            velocity_gain(vel, *forces(list(vel_first) + list(stress_first), nothing)),
            1,
            0,
        )
        right = [final[SXX], final[SXZ], final[PR], stress_final[0], stress_final[2], stress_final[3]]
        left = [vel_first[0], vel_first[1], vel_first[2], again[0], again[1], again[2]]
        for i in range(HALO):
            half = message_core[i // 3]
            half[pl.ds(i % 3 * events + chunk, 8), :] = jnp.where(odd, left[i], right[i])
        flow = vel[1] * stress_final[0] + vel[2] * stress_final[3]
        drain = stress[2] * again[0] + stress[3] * again[2]
        weight = weights[pl.ds(chunk * rows, 8, stride=rows), :]
        right_soon = right[:3] + [flow, stress_final[2]]
        left_soon = left[:3] + [drain, weight]
        right_late = [stress_final[0], stress_final[3], stress_final[3]]
        for i in range(SOON):
            message_chip[pl.ds(i * events + chunk, 8), :] = jnp.where(odd, right_soon[i], left_soon[i])
        for i in range(LATE):
            message_late[pl.ds(i * events + chunk, 8), :] = jnp.where(odd, right_late[i], left[3 + i])
    wait_tiles(4, FIELDS * events * (rows - 4) // rows + final_kind * kind_tiles)


def group_of(events):
    return next(g for g in GROUPS if events % g == 0)


def bulk_kernel(
    sizes,
    given,
    forward,
    source,
    table_ref,
    vel_ref,
    stress_ref,
    late_in,
    changed,
    weights,
    sums,
    late,
    by_source,
):
    events, rows, depth, steps, sources = sizes
    group = group_of(events)
    state_in = given.reshape(FIELDS, events * rows, depth)
    state = changed.reshape(FIELDS, events * rows, depth)
    each = table_ref.shape[0] // sources
    for step in range(steps):
        for part in range(2):
            layers = table_ref[pl.ds(step * (each // steps) + part, sources, stride=each), :]
            for row in range(rows):
                at = (step * 2 + part) * sources * rows + row
                by_source[pl.ds(at, sources, stride=rows), :] = at_row(layers, row, depth)
    vel = tuple(jnp.broadcast_to(c, (rows, depth)) for c in load_coeffs(vel_ref))
    stress = tuple(jnp.broadcast_to(c, (rows, depth)) for c in load_coeffs(stress_ref))

    def body(i, carry):
        perm, poro = carry

        def tile(sub, count=1):
            at = (i * group + sub) * rows
            return pl.ds(pl.multiple_of(at, count * rows), count * rows)

        def pushed(step, part, sub):
            at = ((step * 2 + part) * sources + source[i * group + sub]) * rows
            return by_source[pl.ds(pl.multiple_of(at, rows), rows), :]

        fields = [[state_in[f, tile(sub), :] for f in range(FIELDS)] for sub in range(group)]
        for step in range(steps):
            factors = [[] for _ in range(group)]
            for kind in range(3):
                for sub in range(0, group, 2):
                    both = forward[step * 3 + kind, tile(sub, 2), :].astype(jnp.float32)
                    for half in range(2):
                        value = both[half * rows : (half + 1) * rows]
                        weights[step * 3 + kind, tile(sub + half), :] = value
                        factors[sub + half].append(value)
            for sub, own in enumerate(fields):
                gains = velocity_gain(
                    vel,
                    row_lower(own[SXX]) + depth_lower(own[SXZ]),
                    row_lower(own[SXZ]) + depth_lower(own[SZZ]),
                    row_lower(own[PR]) + vel[3] * own[QX],
                    depth_lower(own[PR]) + vel[3] * own[QZ],
                )
                own[:4] = plus(own[:4], gains)
                own[VX] = own[VX] + pushed(step, 0, sub)
                own[VZ] = own[VZ] + pushed(step, 1, sub)
                perm = perm + own[QX] * factors[sub][0] + own[QZ] * factors[sub][1]
            for sub, own in enumerate(fields):
                own[4:] = plus(
                    own[4:],
                    stress_gain(
                        stress,
                        row_upper(own[VX]),
                        depth_upper(own[VZ]),
                        row_upper(own[QX]) + depth_upper(own[QZ]),
                        depth_upper(own[VX]) + row_upper(own[VZ]),
                    ),
                )
                poro = poro + own[PR] * factors[sub][2]
        for sub, own in enumerate(fields):
            for f in range(FIELDS):
                state[f, tile(sub), :] = own[f]
        return perm, poro

    zero = jnp.zeros((rows, depth), jnp.float32)
    perm, poro = lax.fori_loop(0, events // group, body, (zero, zero))
    sums[pl.ds(0, rows), :] = perm
    sums[pl.ds(rows, rows), :] = poro


def from_before(vel, stress_x, stress_xz, pressure):
    return velocity_gain(vel, -stress_x, -stress_xz, -pressure, 0.0)


def forces(vel, stresses, flows):
    return (
        stresses[0] + depth_lower(stresses[2]),
        stresses[2] + depth_lower(stresses[1]),
        stresses[3] + vel[3] * flows[0],
        depth_lower(stresses[3]) + vel[3] * flows[1],
    )


def strains(stress, vels, after):
    return stress_gain(
        stress,
        after[0] - vels[0],
        depth_upper(vels[1]),
        after[2] - vels[2] + depth_upper(vels[3]),
        depth_upper(vels[0]) + after[1] - vels[1],
    )


NOTHING = (0.0, 0.0, 0.0)


def left_changes(vel, stress, sent, got, factor):
    gain_first = from_before(vel, *got[:3])
    before = beyond_gain(stress, *plus(sent[:3], gain_first[:3]))
    before = plus(got[3:], (before[0], before[2], before[3]))
    stress_first = strains(stress, gain_first, NOTHING)
    vel_first = plus(
        plus(gain_first, velocity_gain(vel, *forces(vel, stress_first, gain_first[2:]))),
        from_before(vel, *before),
    )
    vel_second = from_before(vel, stress_first[0], stress_first[2], stress_first[3])
    end_first = plus(stress_first, strains(stress, vel_first, vel_second))
    end_second = strains(stress, vel_second, NOTHING)
    perm = gain_first[2] * factor(0, 0, 0) + gain_first[3] * factor(0, 1, 0)
    for row, vels in ((0, vel_first), (1, vel_second)):
        perm = perm + vels[2] * factor(1, 0, row) + vels[3] * factor(1, 1, row)
    poro = stress_first[3] * factor(0, 2, 0)
    for row, stresses in ((0, end_first), (1, end_second)):
        poro = poro + stresses[3] * factor(1, 2, row)
    return vel_first + vel_second + end_first + end_second, perm, poro


def right_changes(vel, stress, sent, got, factor, last):
    gain_after = from_before(vel, *sent[:3])
    stress_last = beyond_gain(stress, *plus(got[:3], gain_after[:3]))
    true_last = plus(sent[3:], (stress_last[0], stress_last[2], stress_last[3]))
    vel_last = velocity_gain(
        vel,
        stress_last[0] + depth_lower(stress_last[2]),
        stress_last[2] + depth_lower(stress_last[1]),
        stress_last[3],
        depth_lower(stress_last[3]),
    )
    stress_after = strains(stress, gain_after, NOTHING)
    again = plus(
        plus(gain_after, velocity_gain(vel, *forces(vel, stress_after, gain_after[2:]))),
        from_before(vel, *true_last),
    )
    again = plus(got[3:], again[:3])
    end_inner = beyond_gain(stress, *vel_last[:3])
    end_last = plus(stress_last, strains(stress, vel_last, again))
    perm = vel_last[2] * factor(1, 0, last) + vel_last[3] * factor(1, 1, last)
    poro = stress_last[3] * factor(0, 2, last)
    for row, stresses in ((last - 1, end_inner), (last, end_last)):
        poro = poro + stresses[3] * factor(1, 2, row)
    return vel_last + end_inner + end_last, perm, poro


def left_changes_soon(vel, stress, sent, own_late, got, factor):
    gain_first = from_before(vel, *got[:3])
    beyond = beyond_gain(stress, *plus(sent[:3], gain_first[:3]))
    flow = got[3] + vel[1] * beyond[0] + vel[2] * beyond[3]
    shear = got[4] + beyond[2]
    stress_first = strains(stress, gain_first, NOTHING)
    vel_first = plus(gain_first, velocity_gain(vel, *forces(vel, stress_first, gain_first[2:])))
    vel_first = plus(vel_first, (0.0, -vel[0] * shear, flow, vel[1] * shear))
    vel_second = from_before(vel, stress_first[0], stress_first[2], stress_first[3])
    end_first = plus(stress_first, strains(stress, vel_first, vel_second))
    end_second = strains(stress, vel_second, NOTHING)
    perm = gain_first[2] * factor(0, 0, 0) + gain_first[3] * factor(0, 1, 0)
    for row, vels in ((0, vel_first), (1, vel_second)):
        perm = perm + vels[2] * factor(1, 0, row) + vels[3] * factor(1, 1, row)
    poro = stress_first[3] * factor(0, 2, 0)
    for row, stresses in ((0, end_first), (1, end_second)):
        poro = poro + stresses[3] * factor(1, 2, row)
    rest = (vel[0] * beyond[0] + vel[1] * beyond[3],)
    return vel_first + vel_second + end_first + end_second + rest, perm, poro


def right_changes_soon(vel, stress, sent, own_late, got, factor, last):
    gain_after = from_before(vel, *sent[:3])
    stress_last = beyond_gain(stress, *plus(got[:3], gain_after[:3]))
    true_last = (own_late[0] + stress_last[0], sent[4] + stress_last[2], own_late[1] + stress_last[3])
    vel_last = velocity_gain(
        vel,
        stress_last[0] + depth_lower(stress_last[2]),
        stress_last[2] + depth_lower(stress_last[1]),
        stress_last[3],
        depth_lower(stress_last[3]),
    )
    stress_after = strains(stress, gain_after, NOTHING)
    again = plus(
        plus(gain_after, velocity_gain(vel, *forces(vel, stress_after, gain_after[2:]))),
        from_before(vel, *true_last),
    )
    drain = got[3] + stress[2] * again[0] + stress[3] * again[2]
    end_inner = beyond_gain(stress, *vel_last[:3])
    end_last = plus(stress_last, strains(stress, vel_last, NOTHING))
    perm = vel_last[2] * factor(1, 0, last) + vel_last[3] * factor(1, 1, last)
    poro = stress_last[3] * factor(0, 2, last)
    poro = poro + end_inner[3] * factor(1, 2, last - 1) + (end_last[3] - drain) * factor(1, 2, last)
    poro = poro - stress[2] * (vel[0] * true_last[0] + vel[1] * true_last[2]) * got[4]
    return vel_last + end_inner + end_last + again[:3], perm, poro


def side_sums(sizes, over_chips, weights, sent, own_late, got, vel_ref, stress_ref, changes):
    events, rows, depth, _, _ = sizes
    vel = load_coeffs(vel_ref)
    stress = load_coeffs(stress_ref)
    last = rows - 1
    left, right = sides(over_chips)
    count = SOON if over_chips else HALO

    def fill(changed, partial):
        for chunk in range(0, events, 8):

            def row_of(refs, i):
                each = count // len(refs)
                return refs[i // each][pl.ds(i % each * events + chunk, 8), :]

            def factor(step, kind, row):
                return weights[step * 3 + kind, pl.ds(chunk * rows + row, 8, stride=rows), :]

            own = tuple(row_of(sent, i) for i in range(count))
            new = tuple(row_of(got, i) for i in range(count))
            if over_chips:
                late = tuple(own_late[pl.ds(i * events + chunk, 8), :] for i in range(LATE))
                values, perm, poro = changed(vel, stress, own, late, new, factor)
            else:
                values, perm, poro = changed(vel, stress, own, new, factor)
            for i, value in enumerate(values):
                changes[i, pl.ds(chunk, 8), :] = value
            partial = (partial[0] + perm, partial[1] + poro)
        return partial

    zero = (jnp.zeros((8, depth), jnp.float32),) * 2
    from_left = left_changes_soon if over_chips else left_changes
    from_right = functools.partial(right_changes_soon if over_chips else right_changes, last=last)
    return lax.cond(
        left,
        lambda: fill(from_left, zero),
        lambda: lax.cond(right, lambda: fill(from_right, zero), lambda: zero),
    )


def sides(over_chips):
    place = lax.axis_index("gx")
    odd = lax.rem(place, 2) == 1
    if over_chips:
        return jnp.logical_and(jnp.logical_not(odd), place > 0), jnp.logical_and(
            odd, place < lax.axis_size("gx") - 1
        )
    return odd, jnp.logical_not(odd)


def core_kernel(
    sizes, sums_in, weights, sent_a, sent_b, got_a, got_b, vel_ref, stress_ref, changes, sums
):
    rows = sizes[1]
    sent, got = (sent_a, sent_b), (got_a, got_b)
    perm, poro = side_sums(sizes, False, weights, sent, None, got, vel_ref, stress_ref, changes)
    sums[pl.ds(0, rows), :] = sums_in[pl.ds(0, rows), :] + perm
    sums[pl.ds(rows, rows), :] = sums_in[pl.ds(rows, rows), :] + poro


def chip_kernel(
    sizes, normalizer, sums, weights, sent, late, got, vel_ref, stress_ref, changes, totals
):
    rows = sizes[1]
    vel = load_coeffs(vel_ref)
    stress = load_coeffs(stress_ref)
    perm, poro = side_sums(sizes, True, weights, (sent,), late, (got,), vel_ref, stress_ref, changes)
    perm = jnp.sum(sums[pl.ds(0, rows), :] + perm, axis=0, keepdims=True)
    poro = jnp.sum(sums[pl.ds(rows, rows), :] + poro, axis=0, keepdims=True)
    totals[pl.ds(0, 1), :] = perm * (vel[2] * vel[3] * normalizer)
    totals[pl.ds(1, 1), :] = poro * (stress[3] * normalizer)


def finish_kernel(
    sizes, given, changes_core, changes_chip, late, vel_ref, stress_ref, changed, out_hbm, done, sems
):
    events, rows, depth, _, _ = sizes
    state_in = given.reshape(FIELDS, events * rows, depth)
    state = changed.reshape(FIELDS, events * rows, depth)
    vel = load_coeffs(vel_ref)
    stress = load_coeffs(stress_ref)
    last = rows - 1
    left_places = [(s + f, row) for s in (0, 4) for row in (0, 1) for f in range(4)]
    right_places = [(f, last) for f in range(4)] + [(4 + f, row) for row in (last - 1, last) for f in range(4)]
    got = [late[pl.ds(i * events, events), :] for i in range(LATE)]

    def left_late():
        push = vel[0] * got[0] + vel[1] * got[1] + changes_chip[len(left_places)]
        stresses = stress_gain(stress, push, 0.0, 0.0, depth_upper(-push))
        return {(VX, 0): -push} | {(SXX + f, 0): stresses[f] for f in range(4)}

    def right_late():
        again = [got[i] + changes_chip[len(right_places) + i] for i in range(LATE)]
        stresses = beyond_gain(stress, *again)
        return {(SXX + f, last): stresses[f] for f in range(4)}

    def patch(changes, places, fields, more):
        added = more() if more else {}
        for i, (field, row) in enumerate(places):
            if field in fields:
                at = pl.ds(row, events, stride=rows)
                value = changes[i]
                if (field, row) in added:
                    value = value + added[field, row]
                state[field, at, :] = state_in[field, at, :] + value

    half = FIELDS // 2
    copies = []
    for i in range(2):
        fields = range(i * half, (i + 1) * half)
        for over_chips, changes in ((False, changes_core), (True, changes_chip)):
            left, right = sides(over_chips)
            pl.when(left)(
                functools.partial(patch, changes, left_places, fields, left_late if over_chips else None)
            )
            pl.when(right)(
                functools.partial(patch, changes, right_places, fields, right_late if over_chips else None)
            )
        own = pl.ds(i * half * events, half * events)
        copies.append(pltpu.make_async_copy(changed.at[own], out_hbm.at[own], sems.at[i]))
        copies[i].start()
    done[...] = jnp.zeros_like(done)
    for copy in copies:
        copy.wait()


def swap_with(value, size, mask):
    return lax.ppermute(value, "gx", [(i, i ^ mask) for i in range(size)])


def swap_over_chips(value, groups, size):
    route = []
    for group in range(groups):
        base = group * size
        other = (group ^ 1) * size
        for i in range(1, size - 1, 2):
            route += [(base + i, base + i + 1), (base + i + 1, base + i)]
        route += [(base, other), (base + size - 1, other + size - 1)]
    return lax.ppermute(value, ("groups", "gx"), route)


def shards(
    adjoint_state, forward_fields, vel_coeffs, stress_coeffs, drm_cells, drm_force, source_id
):
    fields, events, rows, depth = adjoint_state.shape
    steps = forward_fields.shape[0]
    sources = drm_force.shape[0]
    entries = drm_cells.shape[0]
    size = lax.axis_size("gx")
    groups = lax.axis_size("groups")
    sizes = (events, rows, depth, steps, sources)
    blocks = entries // 128
    tiles = events * rows
    f32 = jnp.float32
    any_space = pl.BlockSpec(memory_space=pl.ANY)
    vmem = pl.BlockSpec(memory_space=pltpu.VMEM)
    smem = pl.BlockSpec(memory_space=pltpu.SMEM)
    state = adjoint_state.reshape(fields * events, rows, depth)
    forward = forward_fields.reshape(steps * 3, tiles, depth)
    cells = drm_cells.reshape(blocks, 128)
    force = drm_force.reshape(sources * steps, 2, blocks, 128).transpose(0, 2, 1, 3)
    force = force.reshape(sources * steps * 2 * blocks, 128)
    soon = pltpu.VMEM((SOON * events, depth), f32)
    late = pltpu.VMEM((LATE * events, depth), f32)
    half = pltpu.VMEM((HALO // 2 * events, depth), f32)
    limits = pltpu.CompilerParams(vmem_limit_bytes=ROOM)

    def kept(space, *values):
        return tuple(pltpu.with_memory_space_constraint(v, space) for v in values)

    (
        state,
        forward,
        source,
        table,
        message_first,
        message_second,
        message_chip,
        message_late,
        vel,
        stress,
    ) = pl.pallas_call(
        functools.partial(edge_kernel, sizes),
        out_shape=(
            pltpu.VMEM(state.shape, f32),
            pltpu.VMEM(forward.shape, forward.dtype),
            pltpu.SMEM((events,), jnp.int32),
            pltpu.VMEM(force.shape, f32),
            half,
            half,
            soon,
            late,
            pltpu.VMEM(vel_coeffs.shape, f32),
            pltpu.VMEM(stress_coeffs.shape, f32),
        ),
        in_specs=[any_space] * 7,
        out_specs=(vmem, vmem, smem) + (vmem,) * 7,
        scratch_shapes=[
            pltpu.VMEM((tiles, depth), f32),
            pltpu.VMEM(cells.shape, jnp.int32),
            pltpu.VMEM(force.shape, f32),
            pltpu.VMEM(force.shape, f32),
            pltpu.VMEM((tiles, depth), f32),
            pltpu.SemaphoreType.DMA((5,)),
        ],
        compiler_params=limits,
        name="edges",
    )(
        *kept(
            pltpu.HBM,
            state,
            forward,
            vel_coeffs,
            stress_coeffs,
            cells,
            force,
            source_id,
        )
    )

    got_first = swap_with(message_first, size, 1)
    got_second = swap_with(message_second, size, 1)
    got_chip = swap_over_chips(message_chip, groups, size)

    state, weights, sums, message_late = pl.pallas_call(
        functools.partial(bulk_kernel, sizes),
        out_shape=(
            pltpu.VMEM(state.shape, f32),
            pltpu.VMEM(forward.shape, f32),
            pltpu.VMEM((2 * rows, depth), f32),
            late,
        ),
        in_specs=[vmem] * 2 + [smem] + [vmem] * 4,
        out_specs=(vmem,) * 4,
        input_output_aliases={0: 0, 6: 3},
        scratch_shapes=[pltpu.VMEM((steps * 2 * sources * rows, depth), f32)],
        compiler_params=limits,
        cost_estimate=pl.CostEstimate(
            flops=steps * 80 * tiles * depth, bytes_accessed=8 * state.size, transcendentals=0
        ),
        name="bulk",
    )(
        *kept(pltpu.VMEM, state, forward),
        *kept(pltpu.SMEM, source),
        *kept(pltpu.VMEM, table, vel, stress, message_late),
    )
    got_late = swap_over_chips(message_late, groups, size)

    normalizer = (events * rows * size) ** (-0.5)
    changed = pltpu.VMEM((17, events, depth), f32)
    changes_core, sums = pl.pallas_call(
        functools.partial(core_kernel, sizes),
        out_shape=(changed, pltpu.VMEM(sums.shape, f32)),
        in_specs=[vmem] * 8,
        out_specs=(vmem,) * 2,
        compiler_params=limits,
        name="join_core",
    )(
        *kept(
            pltpu.VMEM,
            sums,
            weights,
            message_first,
            message_second,
            got_first,
            got_second,
            vel,
            stress,
        )
    )

    changes_chip, totals = pl.pallas_call(
        functools.partial(chip_kernel, sizes, normalizer),
        out_shape=(changed, pltpu.VMEM((2, depth), f32)),
        in_specs=[vmem] * 7,
        out_specs=(vmem,) * 2,
        compiler_params=limits,
        name="join_chip",
    )(*kept(pltpu.VMEM, sums, weights, message_chip, message_late, got_chip, vel, stress))

    _, out, done = pl.pallas_call(
        functools.partial(finish_kernel, sizes),
        out_shape=(
            pltpu.VMEM(state.shape, f32),
            jax.ShapeDtypeStruct(state.shape, f32),
            pltpu.VMEM((2, depth), f32),
        ),
        in_specs=[vmem] * 6,
        out_specs=(vmem, any_space, vmem),
        input_output_aliases={0: 0},
        scratch_shapes=[pltpu.SemaphoreType.DMA((2,))],
        compiler_params=limits,
        cost_estimate=pl.CostEstimate(flops=0, bytes_accessed=2 * 4 * state.size, transcendentals=0),
        name="finish",
    )(*kept(pltpu.VMEM, state, changes_core, changes_chip, got_late, vel, stress))

    mask = 1
    while mask < size:
        totals = totals + swap_with(totals, size, mask | 1)
        if mask * 4 == size:
            totals = totals + done
        mask *= 2
    return out.reshape(adjoint_state.shape), totals


def solution(mesh):
    in_specs = (
        P(None, "groups", "gx", None),
        P(None, None, "groups", "gx", None),
        P("groups", None),
        P("groups", None),
        P("gx"),
        P("groups", None, None, "gx"),
        P("groups"),
    )
    out_specs = (P(None, "groups", "gx", None), P("groups", None))
    return jax.shard_map(shards, mesh=mesh, in_specs=in_specs, out_specs=out_specs, check_vma=False)
```

```python
import functools

import jax
import jax.numpy as jnp
from jax import lax
from jax.experimental import pallas as pl
from jax.experimental.pallas import tpu as pltpu
from jax.sharding import PartitionSpec as P

LAYER = 8
FIELDS = 8
VX, VZ, QX, QZ, SXX, SZZ, SXZ, PR = range(FIELDS)
HALO = 6
SOON = 5
LATE = 2
PUSHED = ((0, 0), (0, 1), (1, 0), (0, -1))
GROUPS = (24, 16, 8, 4, 2)
ROOM = 16 << 20


def depth_lower(values):
    lane = lax.broadcasted_iota(jnp.int32, values.shape, 1)
    return values - jnp.where(lane == 0, 0.0, pltpu.roll(values, 1, 1))


def depth_upper(values):
    depth = values.shape[1]
    lane = lax.broadcasted_iota(jnp.int32, values.shape, 1)
    return jnp.where(lane == depth - 1, 0.0, pltpu.roll(values, depth - 1, 1)) - values


def row_lower(values):
    row = lax.broadcasted_iota(jnp.int32, values.shape, 0)
    return values - jnp.where(row == 0, 0.0, pltpu.roll(values, 1, 0))


def row_upper(values):
    rows = values.shape[0]
    row = lax.broadcasted_iota(jnp.int32, values.shape, 0)
    return jnp.where(row == rows - 1, 0.0, pltpu.roll(values, rows - 1, 0)) - values


def velocity_gain(coeffs, force_x, force_z, push_x, push_z):
    solid, couple, fluid, _ = coeffs
    return (
        solid * force_x + couple * push_x,
        solid * force_z + couple * push_z,
        -couple * force_x - fluid * push_x,
        -couple * force_z - fluid * push_z,
    )


def stress_gain(coeffs, strain_x, strain_z, inflow, shear):
    lame, modulus, coupling, fluid = coeffs
    dilation = strain_x + strain_z
    common = lame * dilation - coupling * inflow
    return (
        common + 2.0 * modulus * strain_x,
        common + 2.0 * modulus * strain_z,
        modulus * shear,
        -coupling * dilation - fluid * inflow,
    )


def beyond_gain(coeffs, vel_x, vel_z, flow_x):
    lame, modulus, coupling, fluid = coeffs
    return (
        (lame + 2.0 * modulus) * vel_x - coupling * flow_x,
        lame * vel_x - coupling * flow_x,
        modulus * vel_z,
        -coupling * vel_x - fluid * flow_x,
    )


def plus(left, right):
    return tuple(a + b for a, b in zip(left, right))


def minus(left, right):
    return tuple(a - b for a, b in zip(left, right))


def load_coeffs(ref):
    return tuple(ref[pl.ds(i, 1), :] for i in range(4))


def at_row(layers, row, depth):
    lane = lax.broadcasted_iota(jnp.int32, layers.shape, 1)
    moved = pltpu.roll(layers, (depth - LAYER - LAYER * row) % depth, 1)
    return jnp.where(lane >= depth - LAYER, moved, 0.0)


def exact_pieces(values):
    pieces = []
    for _ in range(3):
        pieces.append(values.astype(jnp.bfloat16))
        values = values - pieces[-1].astype(jnp.float32)
    return pieces


def edge_kernel(
    sizes,
    state_hbm,
    forward_hbm,
    vel_hbm,
    stress_hbm,
    cells_hbm,
    force_hbm,
    source_hbm,
    near,
    forward,
    source,
    table_ref,
    message_first,
    message_second,
    message_chip,
    message_late,
    vel_ref,
    stress_ref,
    weights,
    cells,
    force,
    near_force,
    pushes,
    sems,
):
    events, rows, depth, steps, sources = sizes
    final_kind = steps * 3 - 1
    copies = [
        pltpu.make_async_copy(src, dst, sems.at[min(i, 3) if i < 8 else 4])
        for i, (src, dst) in enumerate(
            [
                (cells_hbm, cells),
                (force_hbm, force),
                (source_hbm, source),
                (vel_hbm, vel_ref),
                (stress_hbm, stress_ref),
                (state_hbm.at[:, pl.ds(0, 2)], near.at[:, pl.ds(0, 2)]),
                (state_hbm.at[:, pl.ds(rows - 2, 2)], near.at[:, pl.ds(rows - 2, 2)]),
                (forward_hbm.at[pl.ds(final_kind, 1)], forward.at[pl.ds(final_kind, 1)]),
                (state_hbm.at[:, pl.ds(2, rows - 4)], near.at[:, pl.ds(2, rows - 4)]),
                (forward_hbm.at[pl.ds(0, final_kind)], forward.at[pl.ds(0, final_kind)]),
            ]
        )
    ]
    for copy in copies:
        copy.start()
    copies[0].wait()
    copies[1].wait()
    lanes = cells.shape[1]
    local = cells[...] & (rows * depth - 1)
    slot = (local // depth) * LAYER + (local & (depth - 1)) - (depth - LAYER)
    blocks = cells.shape[0]
    spots = lax.broadcasted_iota(jnp.int32, (depth, lanes), 0)
    hits = [(spots == slot[i : i + 1, :]).astype(jnp.float32).astype(jnp.bfloat16) for i in range(blocks)]
    pieces = exact_pieces(force[...])
    terms = [
        lax.dot_general(
            jnp.concatenate(pieces, axis=0),
            hit,
            (((1,), (1,)), ((), ())),
            preferred_element_type=jnp.float32,
        )
        for hit in hits
    ]
    count = force.shape[0]
    terms = [t[:count] + t[count : 2 * count] + t[2 * count :] for t in terms]
    layers = terms[0]
    for block in range(1, blocks):
        layers = layers + pltpu.roll(terms[block], count - 2 * block, 0)
    table_ref[...] = layers
    def moved(row):
        return at_row(layers, row, depth)

    own = lax.broadcasted_iota(jnp.int32, layers.shape, 0) & (rows - 1)
    picked = jnp.where(own < 6, pltpu.roll(moved(1), 2, 0), pltpu.roll(moved(rows - 1), 6, 0))
    near_force[...] = jnp.where((own & 2) == 0, moved(0), picked)
    copies[2].wait()
    for event in range(events):
        record = pl.multiple_of(source[event] * rows, rows)
        pushes[pl.ds(event * rows, rows), :] = near_force[pl.ds(record, rows), :]
    def wait_tiles(index, count):
        own = near.at[pl.ds(0, count)]
        pltpu.make_async_copy(own, own, sems.at[index]).wait()

    kind_tiles = events // 2
    coeff_tiles = 2 * vel_ref.shape[0] // rows
    wait_tiles(3, FIELDS * events * 4 // rows + kind_tiles + coeff_tiles)
    weights[...] = forward[final_kind].astype(jnp.float32)
    vel = load_coeffs(vel_ref)
    stress = load_coeffs(stress_ref)
    odd = lax.rem(lax.axis_index("gx"), 2) == 1
    message_core = (message_first, message_second)
    last = rows - 1
    state = near.reshape(near.shape[0] * rows, depth)

    def rim(chunk, field, row):
        return state[pl.ds((field * events + chunk) * rows + row, 8, stride=rows), :]

    def pushed(chunk, step, part, row):
        at = PUSHED.index((step, row if row < last else -1)) * 2 + part
        return pushes[pl.ds(chunk * rows + at, 8, stride=rows), :]

    for chunk in range(0, events, 8):
        first = [rim(chunk, f, 0) for f in range(FIELDS)]
        second = [rim(chunk, f, 1) for f in range(FIELDS)]
        final = [rim(chunk, f, last) for f in range(FIELDS)]
        inner = {f: rim(chunk, f, last - 1) for f in (SXX, SXZ, PR)}

        def kicked(fields, gains, step, row):
            vel_x, vel_z, flow_x, flow_z = plus(fields, gains)
            return (
                vel_x + pushed(chunk, step, 0, row),
                vel_z + pushed(chunk, step, 1, row),
                flow_x,
                flow_z,
            )

        def forces(fields, before):
            return (
                fields[SXX] - before[SXX] + depth_lower(fields[SXZ]),
                fields[SXZ] - before[SXZ] + depth_lower(fields[SZZ]),
                fields[PR] - before[PR] + vel[3] * fields[QX],
                depth_lower(fields[PR]) + vel[3] * fields[QZ],
            )

        nothing = {SXX: 0.0, SXZ: 0.0, PR: 0.0}
        vel_first = kicked(first[:4], velocity_gain(vel, *forces(first, nothing)), 0, 0)
        vel_second = kicked(second[:4], velocity_gain(vel, *forces(second, first)), 0, 1)
        vel_final = kicked(final[:4], velocity_gain(vel, *forces(final, inner)), 0, last)
        stress_first = plus(
            first[4:],
            stress_gain(
                stress,
                vel_second[0] - vel_first[0],
                depth_upper(vel_first[1]),
                vel_second[2] - vel_first[2] + depth_upper(vel_first[3]),
                depth_upper(vel_first[0]) + vel_second[1] - vel_first[1],
            ),
        )
        stress_final = plus(
            final[4:],
            stress_gain(
                stress,
                -vel_final[0],
                depth_upper(vel_final[1]),
                -vel_final[2] + depth_upper(vel_final[3]),
                depth_upper(vel_final[0]) - vel_final[1],
            ),
        )
        again = kicked(
            vel_first,
            velocity_gain(vel, *forces(list(vel_first) + list(stress_first), nothing)),
            1,
            0,
        )
        right = [final[SXX], final[SXZ], final[PR], stress_final[0], stress_final[2], stress_final[3]]
        left = [vel_first[0], vel_first[1], vel_first[2], again[0], again[1], again[2]]
        for i in range(HALO):
            half = message_core[i // 3]
            half[pl.ds(i % 3 * events + chunk, 8), :] = jnp.where(odd, left[i], right[i])
        flow = vel[1] * stress_final[0] + vel[2] * stress_final[3]
        drain = stress[2] * again[0] + stress[3] * again[2]
        weight = weights[pl.ds(chunk * rows, 8, stride=rows), :]
        right_soon = right[:3] + [flow, stress_final[2]]
        left_soon = left[:3] + [drain, weight]
        right_late = [stress_final[0], stress_final[3]]
        for i in range(SOON):
            message_chip[pl.ds(i * events + chunk, 8), :] = jnp.where(odd, right_soon[i], left_soon[i])
        for i in range(LATE):
            message_late[pl.ds(i * events + chunk, 8), :] = jnp.where(odd, right_late[i], left[3 + i])
    wait_tiles(4, FIELDS * events * (rows - 4) // rows + final_kind * kind_tiles)


def group_of(events):
    return next(g for g in GROUPS if events % g == 0)


def bulk_kernel(
    sizes,
    given,
    forward,
    source,
    table_ref,
    vel_ref,
    stress_ref,
    late_in,
    changed,
    weights,
    sums,
    late,
    by_source,
):
    events, rows, depth, steps, sources = sizes
    group = group_of(events)
    state_in = given.reshape(FIELDS, events * rows, depth)
    state = changed.reshape(FIELDS, events * rows, depth)
    each = table_ref.shape[0] // sources
    for step in range(steps):
        for part in range(2):
            layers = table_ref[pl.ds(step * (each // steps) + part, sources, stride=each), :]
            for row in range(rows):
                at = (step * 2 + part) * sources * rows + row
                by_source[pl.ds(at, sources, stride=rows), :] = at_row(layers, row, depth)
    vel = tuple(jnp.broadcast_to(c, (rows, depth)) for c in load_coeffs(vel_ref))
    stress = tuple(jnp.broadcast_to(c, (rows, depth)) for c in load_coeffs(stress_ref))

    def body(i, carry):
        perm, poro = carry

        def tile(sub, count=1):
            at = (i * group + sub) * rows
            return pl.ds(pl.multiple_of(at, count * rows), count * rows)

        def pushed(step, part, sub):
            at = ((step * 2 + part) * sources + source[i * group + sub]) * rows
            return by_source[pl.ds(pl.multiple_of(at, rows), rows), :]

        fields = [[state_in[f, tile(sub), :] for f in range(FIELDS)] for sub in range(group)]
        for step in range(steps):
            factors = [[] for _ in range(group)]
            for kind in range(3):
                for sub in range(0, group, 2):
                    both = forward[step * 3 + kind, tile(sub, 2), :].astype(jnp.float32)
                    for half in range(2):
                        value = both[half * rows : (half + 1) * rows]
                        weights[step * 3 + kind, tile(sub + half), :] = value
                        factors[sub + half].append(value)
            for sub, own in enumerate(fields):
                gains = velocity_gain(
                    vel,
                    row_lower(own[SXX]) + depth_lower(own[SXZ]),
                    row_lower(own[SXZ]) + depth_lower(own[SZZ]),
                    row_lower(own[PR]) + vel[3] * own[QX],
                    depth_lower(own[PR]) + vel[3] * own[QZ],
                )
                own[:4] = plus(own[:4], gains)
                own[VX] = own[VX] + pushed(step, 0, sub)
                own[VZ] = own[VZ] + pushed(step, 1, sub)
                perm = perm + own[QX] * factors[sub][0] + own[QZ] * factors[sub][1]
            for sub, own in enumerate(fields):
                own[4:] = plus(
                    own[4:],
                    stress_gain(
                        stress,
                        row_upper(own[VX]),
                        depth_upper(own[VZ]),
                        row_upper(own[QX]) + depth_upper(own[QZ]),
                        depth_upper(own[VX]) + row_upper(own[VZ]),
                    ),
                )
                poro = poro + own[PR] * factors[sub][2]
        for sub, own in enumerate(fields):
            for f in range(FIELDS):
                state[f, tile(sub), :] = own[f]
        return perm, poro

    zero = jnp.zeros((rows, depth), jnp.float32)
    perm, poro = lax.fori_loop(0, events // group, body, (zero, zero))
    sums[pl.ds(0, rows), :] = perm
    sums[pl.ds(rows, rows), :] = poro


def from_before(vel, stress_x, stress_xz, pressure):
    return velocity_gain(vel, -stress_x, -stress_xz, -pressure, 0.0)


def forces(vel, stresses, flows):
    return (
        stresses[0] + depth_lower(stresses[2]),
        stresses[2] + depth_lower(stresses[1]),
        stresses[3] + vel[3] * flows[0],
        depth_lower(stresses[3]) + vel[3] * flows[1],
    )


def strains(stress, vels, after):
    return stress_gain(
        stress,
        after[0] - vels[0],
        depth_upper(vels[1]),
        after[2] - vels[2] + depth_upper(vels[3]),
        depth_upper(vels[0]) + after[1] - vels[1],
    )


NOTHING = (0.0, 0.0, 0.0)


def left_changes(vel, stress, sent, got, factor):
    gain_first = from_before(vel, *got[:3])
    before = beyond_gain(stress, *plus(sent[:3], gain_first[:3]))
    before = plus(got[3:], (before[0], before[2], before[3]))
    stress_first = strains(stress, gain_first, NOTHING)
    vel_first = plus(
        plus(gain_first, velocity_gain(vel, *forces(vel, stress_first, gain_first[2:]))),
        from_before(vel, *before),
    )
    vel_second = from_before(vel, stress_first[0], stress_first[2], stress_first[3])
    end_first = plus(stress_first, strains(stress, vel_first, vel_second))
    end_second = strains(stress, vel_second, NOTHING)
    perm = gain_first[2] * factor(0, 0, 0) + gain_first[3] * factor(0, 1, 0)
    for row, vels in ((0, vel_first), (1, vel_second)):
        perm = perm + vels[2] * factor(1, 0, row) + vels[3] * factor(1, 1, row)
    poro = stress_first[3] * factor(0, 2, 0)
    for row, stresses in ((0, end_first), (1, end_second)):
        poro = poro + stresses[3] * factor(1, 2, row)
    return vel_first + vel_second + end_first + end_second, perm, poro


def right_changes(vel, stress, sent, got, factor, last):
    gain_after = from_before(vel, *sent[:3])
    stress_last = beyond_gain(stress, *plus(got[:3], gain_after[:3]))
    true_last = plus(sent[3:], (stress_last[0], stress_last[2], stress_last[3]))
    vel_last = velocity_gain(
        vel,
        stress_last[0] + depth_lower(stress_last[2]),
        stress_last[2] + depth_lower(stress_last[1]),
        stress_last[3],
        depth_lower(stress_last[3]),
    )
    stress_after = strains(stress, gain_after, NOTHING)
    again = plus(
        plus(gain_after, velocity_gain(vel, *forces(vel, stress_after, gain_after[2:]))),
        from_before(vel, *true_last),
    )
    again = plus(got[3:], again[:3])
    end_inner = beyond_gain(stress, *vel_last[:3])
    end_last = plus(stress_last, strains(stress, vel_last, again))
    perm = vel_last[2] * factor(1, 0, last) + vel_last[3] * factor(1, 1, last)
    poro = stress_last[3] * factor(0, 2, last)
    for row, stresses in ((last - 1, end_inner), (last, end_last)):
        poro = poro + stresses[3] * factor(1, 2, row)
    return vel_last + end_inner + end_last, perm, poro


def left_changes_soon(vel, stress, sent, own_late, got, factor):
    gain_first = from_before(vel, *got[:3])
    beyond = beyond_gain(stress, *plus(sent[:3], gain_first[:3]))
    flow = got[3] + vel[1] * beyond[0] + vel[2] * beyond[3]
    shear = got[4] + beyond[2]
    stress_first = strains(stress, gain_first, NOTHING)
    vel_first = plus(gain_first, velocity_gain(vel, *forces(vel, stress_first, gain_first[2:])))
    vel_first = plus(vel_first, (0.0, -vel[0] * shear, flow, vel[1] * shear))
    vel_second = from_before(vel, stress_first[0], stress_first[2], stress_first[3])
    end_first = plus(stress_first, strains(stress, vel_first, vel_second))
    end_second = strains(stress, vel_second, NOTHING)
    perm = gain_first[2] * factor(0, 0, 0) + gain_first[3] * factor(0, 1, 0)
    for row, vels in ((0, vel_first), (1, vel_second)):
        perm = perm + vels[2] * factor(1, 0, row) + vels[3] * factor(1, 1, row)
    poro = stress_first[3] * factor(0, 2, 0)
    for row, stresses in ((0, end_first), (1, end_second)):
        poro = poro + stresses[3] * factor(1, 2, row)
    rest = (vel[0] * beyond[0] + vel[1] * beyond[3],)
    return vel_first + vel_second + end_first + end_second + rest, perm, poro


def right_changes_soon(vel, stress, sent, own_late, got, factor, last):
    gain_after = from_before(vel, *sent[:3])
    stress_last = beyond_gain(stress, *plus(got[:3], gain_after[:3]))
    true_last = (own_late[0] + stress_last[0], sent[4] + stress_last[2], own_late[1] + stress_last[3])
    vel_last = velocity_gain(
        vel,
        stress_last[0] + depth_lower(stress_last[2]),
        stress_last[2] + depth_lower(stress_last[1]),
        stress_last[3],
        depth_lower(stress_last[3]),
    )
    stress_after = strains(stress, gain_after, NOTHING)
    again = plus(
        plus(gain_after, velocity_gain(vel, *forces(vel, stress_after, gain_after[2:]))),
        from_before(vel, *true_last),
    )
    drain = got[3] + stress[2] * again[0] + stress[3] * again[2]
    end_inner = beyond_gain(stress, *vel_last[:3])
    end_last = plus(stress_last, strains(stress, vel_last, NOTHING))
    perm = vel_last[2] * factor(1, 0, last) + vel_last[3] * factor(1, 1, last)
    poro = stress_last[3] * factor(0, 2, last)
    poro = poro + end_inner[3] * factor(1, 2, last - 1) + (end_last[3] - drain) * factor(1, 2, last)
    poro = poro - stress[2] * (vel[0] * true_last[0] + vel[1] * true_last[2]) * got[4]
    return vel_last + end_inner + end_last + again[:3], perm, poro


def side_sums(sizes, over_chips, weights, sent, own_late, got, vel_ref, stress_ref, changes):
    events, rows, depth, _, _ = sizes
    vel = load_coeffs(vel_ref)
    stress = load_coeffs(stress_ref)
    last = rows - 1
    left, right = sides(over_chips)
    count = SOON if over_chips else HALO

    def fill(changed, partial):
        for chunk in range(0, events, 8):

            def row_of(refs, i):
                each = count // len(refs)
                return refs[i // each][pl.ds(i % each * events + chunk, 8), :]

            def factor(step, kind, row):
                return weights[step * 3 + kind, pl.ds(chunk * rows + row, 8, stride=rows), :]

            own = tuple(row_of(sent, i) for i in range(count))
            new = tuple(row_of(got, i) for i in range(count))
            if over_chips:
                late = tuple(own_late[pl.ds(i * events + chunk, 8), :] for i in range(LATE))
                values, perm, poro = changed(vel, stress, own, late, new, factor)
            else:
                values, perm, poro = changed(vel, stress, own, new, factor)
            for i, value in enumerate(values):
                changes[i, pl.ds(chunk, 8), :] = value
            partial = (partial[0] + perm, partial[1] + poro)
        return partial

    zero = (jnp.zeros((8, depth), jnp.float32),) * 2
    from_left = left_changes_soon if over_chips else left_changes
    from_right = functools.partial(right_changes_soon if over_chips else right_changes, last=last)
    return lax.cond(
        left,
        lambda: fill(from_left, zero),
        lambda: lax.cond(right, lambda: fill(from_right, zero), lambda: zero),
    )


def sides(over_chips):
    place = lax.axis_index("gx")
    odd = lax.rem(place, 2) == 1
    if over_chips:
        return jnp.logical_and(jnp.logical_not(odd), place > 0), jnp.logical_and(
            odd, place < lax.axis_size("gx") - 1
        )
    return odd, jnp.logical_not(odd)


def core_kernel(
    sizes, sums_in, weights, sent_a, sent_b, got_a, got_b, vel_ref, stress_ref, changes, sums
):
    rows = sizes[1]
    sent, got = (sent_a, sent_b), (got_a, got_b)
    perm, poro = side_sums(sizes, False, weights, sent, None, got, vel_ref, stress_ref, changes)
    sums[pl.ds(0, rows), :] = sums_in[pl.ds(0, rows), :] + perm
    sums[pl.ds(rows, rows), :] = sums_in[pl.ds(rows, rows), :] + poro


def chip_kernel(
    sizes, normalizer, sums, weights, sent, late, got, vel_ref, stress_ref, changes, totals
):
    rows = sizes[1]
    vel = load_coeffs(vel_ref)
    stress = load_coeffs(stress_ref)
    perm, poro = side_sums(sizes, True, weights, (sent,), late, (got,), vel_ref, stress_ref, changes)
    perm = jnp.sum(sums[pl.ds(0, rows), :] + perm, axis=0, keepdims=True)
    poro = jnp.sum(sums[pl.ds(rows, rows), :] + poro, axis=0, keepdims=True)
    totals[pl.ds(0, 1), :] = perm * (vel[2] * vel[3] * normalizer)
    totals[pl.ds(1, 1), :] = poro * (stress[3] * normalizer)


def finish_kernel(
    sizes, given, changes_core, changes_chip, soon, late, vel_ref, stress_ref, changed, out_hbm, done, sems
):
    events, rows, depth, _, _ = sizes
    state_in = given.reshape(FIELDS, events * rows, depth)
    state = changed.reshape(FIELDS, events * rows, depth)
    vel = load_coeffs(vel_ref)
    stress = load_coeffs(stress_ref)
    last = rows - 1
    left_places = [(s + f, row) for s in (0, 4) for row in (0, 1) for f in range(4)]
    right_places = [(f, last) for f in range(4)] + [(4 + f, row) for row in (last - 1, last) for f in range(4)]
    got = [late[pl.ds(i * events, events), :] for i in range(LATE)]

    def left_late():
        push = vel[0] * got[0] + vel[1] * got[1] + changes_chip[len(left_places)]
        stresses = stress_gain(stress, push, 0.0, 0.0, depth_upper(-push))
        return {(VX, 0): -push} | {(SXX + f, 0): stresses[f] for f in range(4)}

    def right_late():
        drain = soon[pl.ds(3 * events, events), :]
        flow = (drain - stress[2] * got[0]) / stress[3]
        again = [value + changes_chip[len(right_places) + i] for i, value in enumerate((*got, flow))]
        stresses = beyond_gain(stress, *again)
        return {(SXX + f, last): stresses[f] for f in range(4)}

    def patch(changes, places, fields, more):
        added = more() if more else {}
        for i, (field, row) in enumerate(places):
            if field in fields:
                at = pl.ds(row, events, stride=rows)
                value = changes[i]
                if (field, row) in added:
                    value = value + added[field, row]
                state[field, at, :] = state_in[field, at, :] + value

    half = FIELDS // 2
    copies = []
    for i in range(2):
        fields = range(i * half, (i + 1) * half)
        for over_chips, changes in ((False, changes_core), (True, changes_chip)):
            left, right = sides(over_chips)
            pl.when(left)(
                functools.partial(patch, changes, left_places, fields, left_late if over_chips else None)
            )
            pl.when(right)(
                functools.partial(patch, changes, right_places, fields, right_late if over_chips else None)
            )
        own = pl.ds(i * half * events, half * events)
        copies.append(pltpu.make_async_copy(changed.at[own], out_hbm.at[own], sems.at[i]))
        copies[i].start()
    done[...] = jnp.zeros_like(done)
    for copy in copies:
        copy.wait()


def swap_with(value, size, mask):
    return lax.ppermute(value, "gx", [(i, i ^ mask) for i in range(size)])


def swap_over_chips(value, groups, size):
    route = []
    for group in range(groups):
        base = group * size
        other = (group ^ 1) * size
        for i in range(1, size - 1, 2):
            route += [(base + i, base + i + 1), (base + i + 1, base + i)]
        route += [(base, other), (base + size - 1, other + size - 1)]
    return lax.ppermute(value, ("groups", "gx"), route)


def shards(
    adjoint_state, forward_fields, vel_coeffs, stress_coeffs, drm_cells, drm_force, source_id
):
    fields, events, rows, depth = adjoint_state.shape
    steps = forward_fields.shape[0]
    sources = drm_force.shape[0]
    entries = drm_cells.shape[0]
    size = lax.axis_size("gx")
    groups = lax.axis_size("groups")
    sizes = (events, rows, depth, steps, sources)
    blocks = entries // 128
    tiles = events * rows
    f32 = jnp.float32
    any_space = pl.BlockSpec(memory_space=pl.ANY)
    vmem = pl.BlockSpec(memory_space=pltpu.VMEM)
    smem = pl.BlockSpec(memory_space=pltpu.SMEM)
    state = adjoint_state.reshape(fields * events, rows, depth)
    forward = forward_fields.reshape(steps * 3, tiles, depth)
    cells = drm_cells.reshape(blocks, 128)
    force = drm_force.reshape(sources * steps, 2, blocks, 128).transpose(0, 2, 1, 3)
    force = force.reshape(sources * steps * 2 * blocks, 128)
    soon = pltpu.VMEM((SOON * events, depth), f32)
    late = pltpu.VMEM((LATE * events, depth), f32)
    half = pltpu.VMEM((HALO // 2 * events, depth), f32)
    limits = pltpu.CompilerParams(vmem_limit_bytes=ROOM)

    def kept(space, *values):
        return tuple(pltpu.with_memory_space_constraint(v, space) for v in values)

    (
        state,
        forward,
        source,
        table,
        message_first,
        message_second,
        message_chip,
        message_late,
        vel,
        stress,
    ) = pl.pallas_call(
        functools.partial(edge_kernel, sizes),
        out_shape=(
            pltpu.VMEM(state.shape, f32),
            pltpu.VMEM(forward.shape, forward.dtype),
            pltpu.SMEM((events,), jnp.int32),
            pltpu.VMEM(force.shape, f32),
            half,
            half,
            soon,
            late,
            pltpu.VMEM(vel_coeffs.shape, f32),
            pltpu.VMEM(stress_coeffs.shape, f32),
        ),
        in_specs=[any_space] * 7,
        out_specs=(vmem, vmem, smem) + (vmem,) * 7,
        scratch_shapes=[
            pltpu.VMEM((tiles, depth), f32),
            pltpu.VMEM(cells.shape, jnp.int32),
            pltpu.VMEM(force.shape, f32),
            pltpu.VMEM(force.shape, f32),
            pltpu.VMEM((tiles, depth), f32),
            pltpu.SemaphoreType.DMA((5,)),
        ],
        compiler_params=limits,
        name="edges",
    )(
        *kept(
            pltpu.HBM,
            state,
            forward,
            vel_coeffs,
            stress_coeffs,
            cells,
            force,
            source_id,
        )
    )

    got_first = swap_with(message_first, size, 1)
    got_second = swap_with(message_second, size, 1)
    got_chip = swap_over_chips(message_chip, groups, size)

    state, weights, sums, message_late = pl.pallas_call(
        functools.partial(bulk_kernel, sizes),
        out_shape=(
            pltpu.VMEM(state.shape, f32),
            pltpu.VMEM(forward.shape, f32),
            pltpu.VMEM((2 * rows, depth), f32),
            late,
        ),
        in_specs=[vmem] * 2 + [smem] + [vmem] * 4,
        out_specs=(vmem,) * 4,
        input_output_aliases={0: 0, 6: 3},
        scratch_shapes=[pltpu.VMEM((steps * 2 * sources * rows, depth), f32)],
        compiler_params=limits,
        cost_estimate=pl.CostEstimate(
            flops=steps * 80 * tiles * depth, bytes_accessed=8 * state.size, transcendentals=0
        ),
        name="bulk",
    )(
        *kept(pltpu.VMEM, state, forward),
        *kept(pltpu.SMEM, source),
        *kept(pltpu.VMEM, table, vel, stress, message_late),
    )
    got_late = swap_over_chips(message_late, groups, size)

    normalizer = (events * rows * size) ** (-0.5)
    changed = pltpu.VMEM((17, events, depth), f32)
    changes_core, sums = pl.pallas_call(
        functools.partial(core_kernel, sizes),
        out_shape=(changed, pltpu.VMEM(sums.shape, f32)),
        in_specs=[vmem] * 8,
        out_specs=(vmem,) * 2,
        compiler_params=limits,
        name="join_core",
    )(
        *kept(
            pltpu.VMEM,
            sums,
            weights,
            message_first,
            message_second,
            got_first,
            got_second,
            vel,
            stress,
        )
    )

    changes_chip, totals = pl.pallas_call(
        functools.partial(chip_kernel, sizes, normalizer),
        out_shape=(changed, pltpu.VMEM((2, depth), f32)),
        in_specs=[vmem] * 7,
        out_specs=(vmem,) * 2,
        compiler_params=limits,
        name="join_chip",
    )(*kept(pltpu.VMEM, sums, weights, message_chip, message_late, got_chip, vel, stress))

    _, out, done = pl.pallas_call(
        functools.partial(finish_kernel, sizes),
        out_shape=(
            pltpu.VMEM(state.shape, f32),
            jax.ShapeDtypeStruct(state.shape, f32),
            pltpu.VMEM((2, depth), f32),
        ),
        in_specs=[vmem] * 7,
        out_specs=(vmem, any_space, vmem),
        input_output_aliases={0: 0},
        scratch_shapes=[pltpu.SemaphoreType.DMA((2,))],
        compiler_params=limits,
        cost_estimate=pl.CostEstimate(flops=0, bytes_accessed=2 * 4 * state.size, transcendentals=0),
        name="finish",
    )(*kept(pltpu.VMEM, state, changes_core, changes_chip, got_chip, got_late, vel, stress))

    mask = 1
    while mask < size:
        totals = totals + swap_with(totals, size, mask | 1)
        if mask * 4 == size:
            totals = totals + done
        mask *= 2
    return out.reshape(adjoint_state.shape), totals


def solution(mesh):
    in_specs = (
        P(None, "groups", "gx", None),
        P(None, None, "groups", "gx", None),
        P("groups", None),
        P("groups", None),
        P("gx"),
        P("groups", None, None, "gx"),
        P("groups"),
    )
    out_specs = (P(None, "groups", "gx", None), P("groups", None))
    return jax.shard_map(shards, mesh=mesh, in_specs=in_specs, out_specs=out_specs, check_vma=False)
```
